32 devices in a mesh: section: 2 (over y), batch: 16 (over z, x, core).
Axes of the slice: x: 2, y: 2, z: 4, core: 2. Of those that a mesh axis runs over, the one named last changes fastest.
Arguments:
- tokens: bfloat16 [2, 2048, 1024], P(None, 'batch'), may hold values from -13.5 to 13.5
- lengths: int32 [2, 16], P(None, 'batch'), may hold values from 26 to 128, as said below
- norm_gain: bfloat16 [2, 1024], P('section', 'batch'), may hold values from 0.5 to 1.5
- norm_bias: bfloat16 [2, 1024], P('section', 'batch'), may hold values from -1.1953125 to 1.1953125
- joint_weight: bfloat16 [2, 1024, 3072], P('section', 'batch'), may hold values from -0.1875 to 0.1875
- joint_bias: bfloat16 [2, 2048], P('section', 'batch'), may hold values from -1.1953125 to 1.1953125
- output_weight: bfloat16 [2, 1024, 1024], P('section', 'batch'), may hold values from -0.1875 to 0.1875
- output_bias: bfloat16 [2, 1024], P('section', 'batch'), may hold values from -1.1953125 to 1.1953125
- sandwich_gain: bfloat16 [2, 1024], P('section', 'batch'), may hold values from 0.5 to 1.5
- sandwich_bias: bfloat16 [2, 1024], P('section', 'batch'), may hold values from -1.1953125 to 1.1953125
- second_gain: bfloat16 [2, 1024], P('section', 'batch'), may hold values from 0.5 to 1.5
- second_bias: bfloat16 [2, 1024], P('section', 'batch'), may hold values from -1.1953125 to 1.1953125
- expand_weight: bfloat16 [2, 1024, 4096], P('section', 'batch'), may hold values from -0.1875 to 0.1875
- expand_bias: bfloat16 [2, 4096], P('section', 'batch'), may hold values from -1.1953125 to 1.1953125
- reduce_weight: bfloat16 [2, 4096, 1024], P('section', 'batch'), may hold values from -0.09375 to 0.09375
- reduce_bias: bfloat16 [2, 1024], P('section', 'batch'), may hold values from -1.1953125 to 1.1953125
- closing_gain: bfloat16 [2, 1024], P('section', 'batch'), may hold values from 0.5 to 1.5
- closing_bias: bfloat16 [2, 1024], P('section', 'batch'), may hold values from -1.1953125 to 1.1953125
- cotangent: bfloat16 [2, 2048, 1024], P(None, 'batch'), may hold values from -6 to 6
Outputs:
- section_out: bfloat16 [2, 2, 2048, 1024], P('section', None, 'batch')
- section_grad: float32 [2, 2, 2048, 1024], P('section', None, 'batch')
- magnitudes: float32 [2, 3], P('section')
- grad_norm_gain: float32 [2, 1024], P('section', 'batch')
- grad_norm_bias: float32 [2, 1024], P('section', 'batch')
- grad_joint_weight: float32 [2, 1024, 3072], P('section', 'batch')
- grad_joint_bias: float32 [2, 2048], P('section', 'batch')
- grad_output_weight: float32 [2, 1024, 1024], P('section', 'batch')
- grad_output_bias: float32 [2, 1024], P('section', 'batch')
- grad_sandwich_gain: float32 [2, 1024], P('section', 'batch')
- grad_sandwich_bias: float32 [2, 1024], P('section', 'batch')
- grad_second_gain: float32 [2, 1024], P('section', 'batch')
- grad_second_bias: float32 [2, 1024], P('section', 'batch')
- grad_expand_weight: float32 [2, 1024, 4096], P('section', 'batch')
- grad_expand_bias: float32 [2, 4096], P('section', 'batch')
- grad_reduce_weight: float32 [2, 4096, 1024], P('section', 'batch')
- grad_reduce_bias: float32 [2, 1024], P('section', 'batch')
- grad_closing_gain: float32 [2, 1024], P('section', 'batch')
- grad_closing_bias: float32 [2, 1024], P('section', 'batch')
The draws below stay inside these ranges and needn't reach their ends.
Inputs may be any that keep to these rules, and one draw needn't show every extreme that they name: lengths[m, s] is the number of used slots of sequence row s in micro-batch m; later slots are padding.
All inputs are finite; a program needn't handle non-finite values.
Results may differ from the reference program's by a relative error of at most 0.014.
Values may be sent and summed in bfloat16 or wider, within the bound.
A program may use at most 256 MiB of HBM per device.

```python
import math
import jax
import jax.numpy as jnp
from jax import lax

D = 1024
FF = 4096
HEADS = 16
HEAD_DIM = 64
ROWS = 128
MB = 2
SEQS = 16


def draw_lengths(key, part):
    key = jax.random.fold_in(key, 11)
    seq_index = jnp.arange(SEQS, dtype=jnp.int32)
    shortest = ROWS // 3
    base = shortest + (ROWS - shortest) * seq_index // max(SEQS - 1, 1)
    jitter = jax.random.randint(key, (MB, SEQS), 0, ROWS // 8 + 1, dtype=jnp.int32)
    jitter = jitter.at[0, 0].set(ROWS // 8).at[0, SEQS - 1].set(0)
    return (base[None, :] - jitter).astype(jnp.int32)


def draw_tokens(key, part):
    key = jax.random.fold_in(key, 23)
    values = jnp.clip(jax.random.normal(key, (MB, SEQS * ROWS, D), jnp.float32), -4.5, 4.5)
    return values.astype(jnp.bfloat16)


def level_of(key, dims, pieces, smallest, top_value):
    def one(position, blocks):
        draws = jax.random.uniform(jax.random.fold_in(jax.random.fold_in(key, 6), position), (blocks,), jnp.float32, smallest / len(pieces), top_value / len(pieces))
        return jnp.repeat(jnp.exp(draws), dims[position] // blocks).reshape((-1,) + (1,) * (len(dims) - position - 1))

    loudness = one(*pieces[0])
    for cut in pieces[1:]:
        loudness = loudness * one(*cut)
    return loudness


def noise(own_key, dims, width, most, pieces=(), kind=jnp.bfloat16):
    drawn = width * jax.random.normal(own_key, dims, jnp.float32)
    if pieces:
        drawn = drawn * level_of(own_key, dims, pieces, -0.22, 0.18)
    return jnp.clip(drawn, -most, most).astype(kind)


def setup_inputs(seed: int = 0) -> dict:
    keys = jax.random.split(jax.random.key(seed), 20)
    return {
        "tokens": draw_tokens(jax.random.fold_in(keys[19], 71), 0),
        "lengths": draw_lengths(jax.random.fold_in(keys[19], 71), 0),
        "norm_gain": jnp.clip(1.0 + 0.1 * jax.random.normal(keys[2], (2, D), jnp.float32), 0.5, 1.5).astype(jnp.bfloat16),
        "norm_bias": noise(keys[3], (2, D), 0.3, 1.1953125, ((0, 2), (1, 16))),
        "joint_weight": noise(keys[4], (2, D, 3 * D), D ** -0.5, 0.1875, ((0, 2), (1, 16))),
        "joint_bias": noise(keys[5], (2, 2 * D), 0.3, 1.1953125, ((0, 2), (1, 16))),
        "output_weight": noise(keys[6], (2, D, D), D ** -0.5, 0.1875, ((0, 2), (1, 16))),
        "output_bias": noise(keys[7], (2, D), 0.3, 1.1953125, ((0, 2), (1, 16))),
        "sandwich_gain": jnp.clip(1.0 + 0.1 * jax.random.normal(keys[8], (2, D), jnp.float32), 0.5, 1.5).astype(jnp.bfloat16),
        "sandwich_bias": noise(keys[9], (2, D), 0.3, 1.1953125, ((0, 2), (1, 16))),
        "second_gain": jnp.clip(1.0 + 0.1 * jax.random.normal(keys[10], (2, D), jnp.float32), 0.5, 1.5).astype(jnp.bfloat16),
        "second_bias": noise(keys[11], (2, D), 0.3, 1.1953125, ((0, 2), (1, 16))),
        "expand_weight": noise(keys[12], (2, D, FF), D ** -0.5, 0.1875, ((0, 2), (1, 16))),
        "expand_bias": noise(keys[13], (2, FF), 0.3, 1.1953125, ((0, 2), (1, 16))),
        "reduce_weight": noise(keys[14], (2, FF, D), FF ** -0.5, 0.09375, ((0, 2), (1, 16))),
        "reduce_bias": noise(keys[15], (2, D), 0.3, 1.1953125, ((0, 2), (1, 16))),
        "closing_gain": jnp.clip(1.0 + 0.1 * jax.random.normal(keys[16], (2, D), jnp.float32), 0.5, 1.5).astype(jnp.bfloat16),
        "closing_bias": noise(keys[17], (2, D), 0.3, 1.1953125, ((0, 2), (1, 16))),
        "cotangent": noise(keys[18], (MB, SEQS * ROWS, D), 1.0, 6.0, ((1, 16),)),
    }


epsilon = 1e-05
relax_scale = 32.0
masked_value = -1000000000.0

@jax.custom_vjp
def low(v):
    return lax.optimization_barrier(v.astype(jnp.bfloat16)).astype(jnp.float32)

@jax.custom_vjp
def low_back(v):
    return v

def low_keep(v):
    return (low(v), None)

def low_pass(kept, grad):
    return (grad,)

def back_keep(v):
    return (v, None)

def back_low(kept, grad):
    return (low(grad),)
low.defvjp(low_keep, low_pass)
low_back.defvjp(back_keep, back_low)

def norm_layer(value, gain, shift):
    center = lax.optimization_barrier(jnp.mean(value, axis=-1, keepdims=True))
    centered = value - center
    spread = lax.optimization_barrier(jnp.mean(centered * centered, axis=-1, keepdims=True))
    return centered * lax.rsqrt(spread + epsilon) * gain + shift

def product(left, right):
    return jnp.matmul(left, right, precision=lax.Precision.HIGHEST)

def layer(hidden, seq_lengths, params):
    norm_gain, norm_bias, joint_weight, joint_bias, output_weight, output_bias, sandwich_gain, sandwich_bias, second_gain, second_bias, expand_weight, expand_bias, reduce_weight, reduce_bias, closing_gain, closing_bias = params
    batch_rows = hidden.shape[0]
    slot_count = hidden.shape[1]
    query_scale = 1.0 / (relax_scale * math.sqrt(HEAD_DIM))
    normed = low(norm_layer(hidden, norm_gain, norm_bias))
    full_bias = jnp.concatenate([joint_bias[:D], jnp.zeros((D,), jnp.float32), joint_bias[D:]])
    mixed = low_back(product(normed, joint_weight) + full_bias)
    split_shape = (batch_rows, slot_count, HEADS, HEAD_DIM)
    queries = low(mixed[..., :D] * query_scale).reshape(split_shape)
    keys_all = low(mixed[..., D:2 * D]).reshape(split_shape)
    values_all = low(mixed[..., 2 * D:]).reshape(split_shape)
    scores = low_back(jnp.einsum('bqhd,bkhd->bhqk', queries, keys_all, precision=lax.Precision.HIGHEST))
    slots = jnp.arange(slot_count, dtype=jnp.int32)
    visible = (slots[None, None, :] <= slots[None, :, None]) & (slots[None, None, :] < seq_lengths[:, None, None])
    scores = jnp.where(visible[:, None], scores, masked_value)
    row_max = lax.optimization_barrier(jnp.max(scores, axis=-1, keepdims=True))
    exponent = jnp.exp(relax_scale * (scores - row_max))
    attn_probs = low(exponent / lax.optimization_barrier(jnp.sum(exponent, axis=-1, keepdims=True)))
    attended = jnp.einsum('bhqk,bkhd->bqhd', attn_probs, values_all, precision=lax.Precision.HIGHEST)
    attended = low(low_back(attended.reshape(batch_rows, slot_count, D)))
    branch = low_back(product(attended, output_weight) + output_bias)
    middle = hidden + norm_layer(branch, sandwich_gain, sandwich_bias)
    inner = low(norm_layer(middle, second_gain, second_bias))
    before = low_back(product(inner, expand_weight) + expand_bias)
    active = low(jax.nn.gelu(before))
    feed = low_back(product(active, reduce_weight) + reduce_bias)
    result = middle + norm_layer(feed, closing_gain, closing_bias)
    valid_rows = (slots[None, :] < seq_lengths[:, None]).astype(jnp.float32)[..., None]
    squares = jnp.stack([jnp.sum(branch * branch * valid_rows), jnp.sum(feed * feed * valid_rows), jnp.sum(result * result * valid_rows)])
    return (result, squares)

def reference(tokens, lengths, norm_gain, norm_bias, joint_weight, joint_bias, output_weight, output_bias, sandwich_gain, sandwich_bias, second_gain, second_bias, expand_weight, expand_bias, reduce_weight, reduce_bias, closing_gain, closing_bias, cotangent):
    row_total = MB * SEQS
    params = tuple((p.astype(jnp.float32) for p in (norm_gain, norm_bias, joint_weight, joint_bias, output_weight, output_bias, sandwich_gain, sandwich_bias, second_gain, second_bias, expand_weight, expand_bias, reduce_weight, reduce_bias, closing_gain, closing_bias)))
    flat_tokens = tokens.astype(jnp.float32).reshape(row_total, ROWS, D)
    seq_lengths = lengths.reshape(row_total).astype(jnp.int32)
    per_block = 1
    while per_block * 2 * ROWS <= 4096 and row_total % (per_block * 2) == 0:
        per_block = per_block * 2
    block_count = row_total // per_block

    def forward(inputs, probe, weights):
        first_layer = tuple((w[0] for w in weights))
        second_layer = tuple((w[1] for w in weights))

        def run_block(operand):
            hidden, extra, block_lengths = operand
            first_out, first_squares = layer(hidden, block_lengths, first_layer)
            carried = low_back(low(first_out)) + extra
            second_out, second_squares = layer(carried, block_lengths, second_layer)
            return (first_out, second_out, jnp.stack([first_squares, second_squares]))
        shaped = (inputs.reshape(block_count, per_block, ROWS, D), probe.reshape(block_count, per_block, ROWS, D), seq_lengths.reshape(block_count, per_block))
        first_all, second_all, squares = lax.map(jax.checkpoint(run_block), shaped)
        return (first_all.reshape(row_total, ROWS, D), second_all.reshape(row_total, ROWS, D), lax.optimization_barrier(jnp.sum(squares, axis=0)))
    probe = jnp.zeros_like(flat_tokens)
    (first_all, second_all, squares), pullback = jax.vjp(forward, flat_tokens, probe, params)
    slots = jnp.arange(ROWS, dtype=jnp.int32)
    valid_rows = (slots[None, :] < seq_lengths[:, None]).astype(jnp.float32)[..., None]
    grad_seed = cotangent.astype(jnp.float32).reshape(row_total, ROWS, D) * valid_rows
    grad_input, grad_probe, grad_params = pullback((jnp.zeros_like(first_all), grad_seed, jnp.zeros_like(squares)))
    token_count = jnp.sum(lengths.astype(jnp.float32))
    magnitudes = jnp.sqrt(squares / (token_count * D))
    full_shape = (2, MB, SEQS * ROWS, D)
    section_out = jnp.stack([first_all, second_all]).reshape(full_shape).astype(jnp.bfloat16)
    section_grad = jnp.stack([grad_input, grad_probe]).reshape(full_shape)
    return (section_out, section_grad, magnitudes, grad_params[0], grad_params[1], grad_params[2], grad_params[3], grad_params[4], grad_params[5], grad_params[6], grad_params[7], grad_params[8], grad_params[9], grad_params[10], grad_params[11], grad_params[12], grad_params[13], grad_params[14], grad_params[15])
```

```python
import math

import jax
import jax.numpy as jnp
from jax import lax
from jax.sharding import PartitionSpec as P

HEADS = 16
HEAD_DIM = 64
EPSILON = 1e-05
RELAX = 32.0
MASKED = -1000000000.0
QUERY_SCALE = 1.0 / (RELAX * math.sqrt(HEAD_DIM))

BF = jnp.bfloat16
F32 = jnp.float32

VECTORS = (
    "norm_gain", "norm_bias", "joint_bias", "output_bias", "sandwich_gain", "sandwich_bias",
    "second_gain", "second_bias", "expand_bias", "reduce_bias", "closing_gain", "closing_bias",
)
MATRICES = ("joint_weight", "output_weight", "expand_weight", "reduce_weight")
ORDER = (
    "norm_gain", "norm_bias", "joint_weight", "joint_bias", "output_weight", "output_bias",
    "sandwich_gain", "sandwich_bias", "second_gain", "second_bias", "expand_weight", "expand_bias",
    "reduce_weight", "reduce_bias", "closing_gain", "closing_bias",
)


def dot(left, right, contract):
    return lax.dot_general(left, right, (contract, ((), ())), preferred_element_type=F32)


def norm_parts(value):
    center = jnp.mean(value, axis=-1, keepdims=True)
    centered = value - center
    rate = lax.rsqrt(jnp.mean(centered * centered, axis=-1, keepdims=True) + EPSILON)
    return centered * rate, rate


def norm_back(grad, normal, rate, gain):
    scaled = grad * gain
    first = jnp.mean(scaled, axis=-1, keepdims=True)
    second = jnp.mean(scaled * normal, axis=-1, keepdims=True)
    gain_grad = jnp.sum(grad * normal, axis=0)
    bias_grad = jnp.sum(grad, axis=0)
    return rate * (scaled - first - normal * second), gain_grad, bias_grad


def heads_of(flat, sequences):
    return flat.reshape(sequences, flat.shape[0] // sequences, HEADS, HEAD_DIM)


def layer_fore(hidden_in, w, lengths):
    sequences = lengths.shape[0]
    model = hidden_in.shape[1]
    hidden = hidden_in.astype(F32)
    n1, r1 = norm_parts(hidden)
    a = (n1 * w["norm_gain"] + w["norm_bias"]).astype(BF)
    mixed = dot(a, w["joint_weight"], ((1,), (0,)))
    q = ((mixed[:, :model] + w["joint_bias"][:model]) * QUERY_SCALE).astype(BF)
    k = mixed[:, model : 2 * model].astype(BF)
    v = (mixed[:, 2 * model :] + w["joint_bias"][model:]).astype(BF)
    qh, kh, vh = heads_of(q, sequences), heads_of(k, sequences), heads_of(v, sequences)
    scores = jnp.einsum("bqhd,bkhd->bhqk", qh, kh, preferred_element_type=F32)
    slots = scores.shape[-1]
    query_slot = lax.broadcasted_iota(jnp.int32, (sequences, slots, slots), 1)
    key_slot = lax.broadcasted_iota(jnp.int32, (sequences, slots, slots), 2)
    seen = (key_slot <= query_slot) & (key_slot < lengths[:, None, None])
    scores = jnp.where(seen[:, None], scores, MASKED)
    exponent = jnp.exp(RELAX * (scores - jnp.max(scores, axis=-1, keepdims=True)))
    probs = exponent / jnp.sum(exponent, axis=-1, keepdims=True)
    o = jnp.einsum("bhqk,bkhd->bqhd", probs.astype(BF), vh, preferred_element_type=F32)
    o = o.reshape(hidden.shape).astype(BF)
    y = dot(o, w["output_weight"], ((1,), (0,))) + w["output_bias"]
    ny, ry = norm_parts(y)
    mid = hidden + ny * w["sandwich_gain"] + w["sandwich_bias"]
    nm, rm = norm_parts(mid)
    c = (nm * w["second_gain"] + w["second_bias"]).astype(BF)
    f = dot(c, w["expand_weight"], ((1,), (0,))) + w["expand_bias"]
    g = jax.nn.gelu(f).astype(BF)
    e = dot(g, w["reduce_weight"], ((1,), (0,))) + w["reduce_bias"]
    ne, re = norm_parts(e)
    out = mid + ne * w["closing_gain"] + w["closing_bias"]
    kept = dict(n1=n1, r1=r1, a=a, qh=qh, kh=kh, vh=vh, probs=probs, o=o, y=y, ny=ny, ry=ry,
                nm=nm, rm=rm, c=c, f=f, g=g, e=e, ne=ne, re=re, out=out)
    return out, kept


def layer_back(dout, w, s, want_weights):
    sequences = s["qh"].shape[0]
    grads = {}
    de, grads["closing_gain"], grads["closing_bias"] = norm_back(dout, s["ne"], s["re"], w["closing_gain"])
    de = de.astype(BF)
    dg = dot(de, w["reduce_weight"], ((1,), (1,)))
    df = jax.vjp(jax.nn.gelu, s["f"])[1](dg)[0].astype(BF)
    dc = dot(df, w["expand_weight"], ((1,), (1,)))
    dmid, grads["second_gain"], grads["second_bias"] = norm_back(dc, s["nm"], s["rm"], w["second_gain"])
    dmid = dmid + dout
    dy, grads["sandwich_gain"], grads["sandwich_bias"] = norm_back(dmid, s["ny"], s["ry"], w["sandwich_gain"])
    dy = dy.astype(BF)
    do = heads_of(dot(dy, w["output_weight"], ((1,), (1,))).astype(BF), sequences)
    dprobs = jnp.einsum("bqhd,bkhd->bhqk", do, s["vh"], preferred_element_type=F32)
    dv = jnp.einsum("bhqk,bqhd->bkhd", s["probs"].astype(BF), do, preferred_element_type=F32)
    ds = RELAX * s["probs"] * (dprobs - jnp.sum(dprobs * s["probs"], axis=-1, keepdims=True))
    ds = ds.astype(BF)
    dq = jnp.einsum("bhqk,bkhd->bqhd", ds, s["kh"], preferred_element_type=F32)
    dk = jnp.einsum("bhqk,bqhd->bkhd", ds, s["qh"], preferred_element_type=F32)
    flat = dout.shape
    dmixed = jnp.concatenate([dq.reshape(flat) * QUERY_SCALE, dk.reshape(flat), dv.reshape(flat)], axis=1).astype(BF)
    da = dot(dmixed, w["joint_weight"], ((1,), (1,)))
    dh, grads["norm_gain"], grads["norm_bias"] = norm_back(da, s["n1"], s["r1"], w["norm_gain"])
    din = dmid + dh
    if not want_weights:
        return din, None
    model = flat[1]
    grads["reduce_weight"] = dot(s["g"], de, ((0,), (0,)))
    grads["reduce_bias"] = jnp.sum(de.astype(F32), axis=0)
    grads["expand_weight"] = dot(s["c"], df, ((0,), (0,)))
    grads["expand_bias"] = jnp.sum(df.astype(F32), axis=0)
    grads["output_weight"] = dot(s["o"], dy, ((0,), (0,)))
    grads["output_bias"] = jnp.sum(dy.astype(F32), axis=0)
    grads["joint_weight"] = dot(s["a"], dmixed, ((0,), (0,)))
    sums = jnp.sum(dmixed.astype(F32), axis=0)
    grads["joint_bias"] = jnp.concatenate([sums[:model], sums[2 * model :]])
    return din, grads


def passed_along(block, axis, distance):
    devices = range(lax.axis_size(axis))
    route = [(i - distance, i) for i in devices if i - distance in devices]
    return lax.ppermute(block, axis, route)


def local(tokens, lengths, *parameters):
    cotangent = parameters[-1]
    own = dict(zip(ORDER, parameters[:-1]))
    section = lax.axis_index("section")
    micro, rows, model = tokens.shape
    sequences = lengths.shape[1]
    slots = rows // sequences
    total = micro * rows

    packed = jnp.concatenate([own[name] for name in VECTORS], axis=1)
    packed = lax.all_gather(packed, "batch", axis=0, tiled=True).astype(F32)
    w = {}
    start = 0
    for name in VECTORS:
        width = own[name].shape[1]
        w[name] = packed[:, start : start + width].reshape(-1)
        start += width
    for name in MATRICES:
        w[name] = lax.all_gather(own[name], "batch", axis=1, tiled=True)[0]

    flat_lengths = lengths.reshape(-1)
    seen = lax.broadcasted_iota(jnp.int32, (micro * sequences, slots), 1) < flat_lengths[:, None]
    valid = seen.astype(F32).reshape(total, 1)
    source = tokens.reshape(total, model)
    first_out, _ = layer_fore(source, w, flat_lengths)
    incoming = passed_along(first_out.astype(BF), "section", 1)
    out, s = layer_fore(jnp.where(section == 0, source, incoming), w, flat_lengths)
    section_out = out.astype(BF).reshape(1, micro, rows, model)
    squares = jnp.stack([jnp.sum(s[name] * s[name] * valid) for name in ("y", "e", "out")])

    seed = cotangent.reshape(total, model).astype(F32) * valid
    last_in, _ = layer_back(seed, w, s, False)
    incoming = passed_along(last_in.astype(BF), "section", -1)
    din, grads = layer_back(jnp.where(section == 1, seed, incoming.astype(F32)), w, s, True)
    section_grad = din.reshape(1, micro, rows, model)

    result = {}
    for name in reversed(MATRICES):
        result[name] = lax.psum_scatter(grads[name].astype(BF)[None], "batch", scatter_dimension=1, tiled=True).astype(F32)
    devices = lax.axis_size("batch")
    small = jnp.concatenate([grads[name].reshape(devices, -1) for name in VECTORS], axis=1)
    small = lax.psum_scatter(small, "batch", scatter_dimension=0, tiled=True)
    start = 0
    for name in VECTORS:
        width = own[name].shape[1]
        result[name] = small[:, start : start + width]
        start += width
    count = jnp.sum(lengths).astype(F32)
    square_all, count_all = lax.psum((squares, count), "batch")
    magnitudes = jnp.sqrt(square_all / (count_all * model))[None]
    return (section_out, section_grad, magnitudes) + tuple(result[name] for name in ORDER)


def solution(mesh):
    vector, matrix = P("section", "batch"), P("section", "batch", None)
    kinds = tuple(matrix if name in MATRICES else vector for name in ORDER)
    rows = P(None, "batch", None)
    stacked = P("section", None, "batch", None)
    return jax.shard_map(
        local,
        mesh=mesh,
        in_specs=(rows, P(None, "batch")) + kinds + (rows,),
        out_specs=(stacked, stacked, P("section", None)) + kinds,
        check_vma=False,
    )
```

```python
import functools
import math
from typing import Any, NamedTuple

import jax
import jax.numpy as jnp
from jax import lax
from jax.experimental import pallas as pl
from jax.experimental.pallas import tpu as pltpu
from jax.sharding import PartitionSpec as P

HEADS = 16
HEAD_DIM = 64
EPSILON = 1e-05
RELAX = 32.0
MASKED = -1000000000.0
QUERY_SCALE = 1.0 / (RELAX * math.sqrt(HEAD_DIM))

BF = jnp.bfloat16
F32 = jnp.float32
VMEM_LIMIT = 62 * 2**20

MESH = pl.DeviceIdType.MESH
BLOCKS = 12
PART = 64
SLOTS = 4
GATHER_CROSSED = (3, 11)
SCATTER_ORDER = (8, 9, 10, 11, 4, 5, 6, 7, 3, 0, 1, 2)
UP, DOWN, SIDE = 0, 1, 2


def when(condition, action):
    if condition is True:
        action()
    else:
        pl.when(condition)(action)


def both(first, second):
    if first is True:
        return second
    if second is True:
        return first
    return first & second


class Place:
    def __init__(self, depth):
        index = lax.axis_index("batch")
        self.s = lax.axis_index("section")
        self.depth = depth
        self.z = index // 4
        self.x = (index // 2) % 2
        self.c = index % 2

    def device(self, z, x, c):
        return (self.s, (z * 2 + x) * 2 + c)

    def shard(self, z, x, c):
        return (z * 2 + x) * 2 + c

    def greet(self, across=False):
        z, x, c = self.z, self.x, self.c
        sem = pltpu.get_barrier_semaphore()

        def signal(device):
            pl.semaphore_signal(sem, inc=1, device_id=device, device_id_type=MESH)

        signal(self.device(z, 1 - x, c))
        signal(self.device(z, x, 1 - c))
        if across:
            signal((1 - self.s, self.shard(z, x, c)))
        pl.when(z < self.depth - 1)(lambda: signal(self.device(z + 1, x, c)))
        pl.when(z > 0)(lambda: signal(self.device(z - 1, x, c)))
        chain = (z < self.depth - 1).astype(jnp.int32) + (z > 0).astype(jnp.int32)
        pl.semaphore_wait(sem, (3 if across else 2) + chain)


def spot(item, shard):
    if item < 8:
        return item, pl.multiple_of(shard * PART, 16)
    return 8 + shard // 4, pl.multiple_of((shard % 4) * 4 * PART + (item - 8) * PART, 16)


def shard_view(refs, item, width):
    joint, output, expand, reduce = refs
    if item < 3:
        return joint.at[:, pl.ds(item * width, width)]
    if item == 3:
        return output
    if item < 8:
        return expand.at[:, pl.ds((item - 4) * width, width)]
    return reduce.at[pl.ds((item - 8) * PART, PART)]


class Gather:
    def __init__(self, place, own, store, sems):
        self.p, self.own, self.store = place, own, store
        self.send, self.share, self.recv, self.local = sems
        self.sent = []

    def at(self, item, shard):
        block, row = spot(item, shard)
        return self.store.at[block, pl.ds(row, PART)]

    def copy(self, item, shard, way, first=False):
        p = self.p
        target = self.at(item, shard)
        source = shard_view(self.own, item, self.store.shape[2]) if first else target
        recv = self.recv.at[item, shard]
        if way is None:
            send, device = self.share.at[item, shard // 2], p.device(p.z, p.x, 1 - p.c)
        else:
            send = self.send.at[item, shard // 2, way]
            device = (p.device(p.z + 1, p.x, p.c), p.device(p.z - 1, p.x, p.c), p.device(p.z, 1 - p.x, p.c))[way]
        return pltpu.make_async_remote_copy(source, target, send, recv, device_id=device, device_id_type=MESH)

    def go(self, item, shard, way, condition, first=False):
        self.sent.append((item, shard, way, condition, first))
        when(condition, lambda: self.copy(item, shard, way, first).start())

    def arrived(self, item, shard):
        self.copy(item, shard, None).wait_recv()

    def keep_own(self):
        me = self.p.shard(self.p.z, self.p.x, self.p.c)
        copies = [
            pltpu.make_async_copy(shard_view(self.own, item, self.store.shape[2]), self.at(item, me), self.local.at[item])
            for item in range(BLOCKS)
        ]
        for copy in copies:
            copy.start()
        return copies

    def own_sends(self, item):
        p = self.p
        me = p.shard(p.z, p.x, p.c)
        self.go(item, me, UP, p.z < p.depth - 1, True)
        self.go(item, me, DOWN, p.z > 0, True)
        self.go(item, me, SIDE, True, True)
        self.go(item, me, None, True, True)

    def chain_round(self, item, hop):
        p = self.p
        crossed = item in GATHER_CROSSED
        for x in (p.x, 1 - p.x) if crossed else (p.x,):
            for origin, present, way, onward in (
                (p.z - hop, p.z >= hop, UP, p.z < p.depth - 1),
                (p.z + hop, p.z + hop < p.depth, DOWN, p.z > 0),
            ):
                shard = p.shard(origin, x, p.c)
                when(present, lambda: self.arrived(item, shard))
                self.go(item, shard, way, both(present, onward))
                if not crossed:
                    self.go(item, shard, SIDE, present)
                self.go(item, shard, None, present)

    def side_own(self, item):
        p = self.p
        shard = p.shard(p.z, 1 - p.x, p.c)
        self.arrived(item, shard)
        if item in GATHER_CROSSED:
            self.go(item, shard, UP, p.z < p.depth - 1)
            self.go(item, shard, DOWN, p.z > 0)
        self.go(item, shard, None, True)

    def side_round(self, item, hop):
        p = self.p
        if item in GATHER_CROSSED:
            return
        for origin, present in ((p.z - hop, p.z >= hop), (p.z + hop, p.z + hop < p.depth)):
            shard = p.shard(origin, 1 - p.x, p.c)
            when(present, lambda: self.arrived(item, shard))
            self.go(item, shard, None, present)

    def rest(self, item):
        p = self.p
        for z in range(p.depth):
            for x in range(2):
                self.arrived(item, p.shard(z, x, 1 - p.c))

    def drain(self):
        for item, shard, way, condition, first in self.sent:
            when(condition, lambda: self.copy(item, shard, way, first).wait_send())


def run_gather(gather, ahead, ready):
    depth = gather.p.depth
    kept = gather.keep_own()
    for item in range(ahead):
        gather.own_sends(item)

    def finish(item):
        for hop in range(1, depth):
            gather.side_round(item, hop)
        gather.rest(item)
        kept[item].wait()
        ready(item)

    for item in range(BLOCKS):
        if item in GATHER_CROSSED:
            gather.side_own(item)
        for hop in range(1, depth):
            gather.chain_round(item, hop)
            if hop == 1:
                if item + ahead < BLOCKS:
                    gather.own_sends(item + ahead)
                if item not in GATHER_CROSSED:
                    gather.side_own(item)
        if item >= 1:
            finish(item - 1)
    finish(BLOCKS - 1)


def gather_sems(depth):
    kind = pltpu.SemaphoreType.DMA
    return [kind((BLOCKS, 2 * depth, 3)), kind((BLOCKS, 2 * depth)), kind((BLOCKS, 4 * depth)), kind((BLOCKS,))]


def total(*refs):
    value = refs[0][...].astype(F32)
    for ref in refs[1:]:
        value = value + ref[...].astype(F32)
    return value


class Scatter:
    def __init__(self, place, store, buffers, outs, sems):
        self.p, self.store, self.outs = place, store, outs
        self.core_in, self.side_in, self.chain_in = buffers
        (self.core_send, self.core_recv, self.side_send, self.side_recv, self.chain_send, self.chain_recv,
         self.core_free, self.side_free, self.chain_free) = sems
        depth = place.depth
        self.origins = [q for pair in zip(range(depth - 1, -1, -1), range(depth)) for q in pair][:depth]

    def mine(self, step, z, x, c):
        block, row = spot(SCATTER_ORDER[step], self.p.shard(z, x, c))
        return self.store.at[block, pl.ds(row, PART)]

    def core_copy(self, step, z, x):
        p, slot = self.p, step % SLOTS
        return pltpu.make_async_remote_copy(
            self.mine(step, z, x, 1 - p.c), self.core_in.at[slot, z * 2 + x],
            self.core_send.at[slot, z * 2 + x], self.core_recv.at[slot, z * 2 + x],
            device_id=p.device(p.z, p.x, 1 - p.c), device_id_type=MESH)

    def side_copy(self, step, z):
        p, slot = self.p, step % SLOTS
        return pltpu.make_async_remote_copy(
            self.mine(step, z, 1 - p.x, p.c), self.side_in.at[slot, z],
            self.side_send.at[slot, z], self.side_recv.at[slot, z],
            device_id=p.device(p.z, 1 - p.x, p.c), device_id_type=MESH)

    def chain_copy(self, step, z, up):
        p, slot = self.p, step % SLOTS
        return pltpu.make_async_remote_copy(
            self.mine(step, z, p.x, p.c), self.chain_in.at[slot, 1 - up, z],
            self.chain_send.at[slot, 1 - up, z], self.chain_recv.at[slot, 1 - up, z],
            device_id=p.device(p.z + 2 * up - 1, p.x, p.c), device_id_type=MESH)

    def core_stage(self, step):
        if step >= SLOTS:
            for z in self.origins:
                for x in range(2):
                    self.core_copy(step - SLOTS, z, x).wait_send()
            pl.semaphore_wait(self.core_free, 1)
        for z in self.origins:
            for x in range(2):
                self.core_copy(step, z, x).start()

    def from_core(self, step, z, x):
        self.core_copy(step, z, x).wait_recv()
        return self.core_in.at[step % SLOTS, z * 2 + x]

    def side_stage(self, step):
        p = self.p
        if step >= SLOTS:
            for z in self.origins:
                self.side_copy(step - SLOTS, z).wait_send()
            pl.semaphore_wait(self.side_free, 1)
        for z in self.origins:
            twin = self.from_core(step, z, 1 - p.x)
            mine = self.mine(step, z, 1 - p.x, p.c)
            mine[...] = total(mine, twin).astype(BF)
            self.side_copy(step, z).start()

    def chain_stage(self, step):
        p, slot, last = self.p, step % SLOTS, self.p.depth - 1
        if step >= SLOTS:
            for z in self.origins:
                up = (p.z < z).astype(jnp.int32)
                pl.when(p.z != z)(lambda: self.chain_copy(step - SLOTS, z, up).wait_send())
            pl.when(p.z < last)(lambda: pl.semaphore_wait(self.chain_free.at[0], 1))
            pl.when(p.z > 0)(lambda: pl.semaphore_wait(self.chain_free.at[1], 1))
        for z in self.origins:
            up = (p.z < z).astype(jnp.int32)
            fed = ((p.z < z) & (p.z > 0)) | ((p.z > z) & (p.z < last))

            @pl.when(p.z != z)
            def _():
                twin = self.from_core(step, z, p.x)
                mine = self.mine(step, z, p.x, p.c)
                self.side_copy(step, z).wait_recv()
                side = self.side_in.at[slot, z]

                @pl.when(fed)
                def _():
                    self.chain_copy(step, z, up).wait_recv()
                    mine[...] = total(mine, twin, side, self.chain_in.at[slot, 1 - up, z]).astype(BF)

                @pl.when(jnp.logical_not(fed))
                def _():
                    mine[...] = total(mine, twin, side).astype(BF)

                self.chain_copy(step, z, up).start()

    def own_stage(self, step):
        p, slot, last = self.p, step % SLOTS, self.p.depth - 1
        twin = self.from_core(step, p.z, p.x)
        self.side_copy(step, p.z).wait_recv()
        parts = [self.mine(step, p.z, p.x, p.c), twin, self.side_in.at[slot, p.z]]
        pl.when(p.z > 0)(lambda: self.chain_copy(step, p.z, 1).wait_recv())
        pl.when(p.z < last)(lambda: self.chain_copy(step, p.z, 0).wait_recv())
        below, above = self.chain_in.at[slot, 0, p.z], self.chain_in.at[slot, 1, p.z]
        out = self.outs[SCATTER_ORDER[step]]

        def put(*refs):
            out[...] = total(*refs)

        pl.when(p.z == 0)(lambda: put(*parts, above))
        pl.when(p.z == last)(lambda: put(*parts, below))
        pl.when((p.z > 0) & (p.z < last))(lambda: put(*parts, below, above))
        if step + SLOTS < BLOCKS:
            def signal(sem, device):
                pl.semaphore_signal(sem, inc=1, device_id=device, device_id_type=MESH)

            signal(self.core_free, p.device(p.z, p.x, 1 - p.c))
            signal(self.side_free, p.device(p.z, 1 - p.x, p.c))
            pl.when(p.z > 0)(lambda: signal(self.chain_free.at[0], p.device(p.z - 1, p.x, p.c)))
            pl.when(p.z < last)(lambda: signal(self.chain_free.at[1], p.device(p.z + 1, p.x, p.c)))

    def drain(self):
        p = self.p
        for step in range(BLOCKS - SLOTS, BLOCKS):
            for z in self.origins:
                for x in range(2):
                    self.core_copy(step, z, x).wait_send()
                self.side_copy(step, z).wait_send()
                up = (p.z < z).astype(jnp.int32)
                pl.when(p.z != z)(lambda: self.chain_copy(step, z, up).wait_send())


def run_scatter(scatter, ready):
    for tick in range(BLOCKS + 4):
        if tick < BLOCKS:
            ready(tick)
        if tick >= 4:
            scatter.own_stage(tick - 4)
        if tick < BLOCKS:
            scatter.core_stage(tick)
        if 1 <= tick <= BLOCKS:
            scatter.side_stage(tick - 1)
        if 2 <= tick < BLOCKS + 2:
            scatter.chain_stage(tick - 2)
    scatter.drain()


def scatter_scratch(depth, width):
    dma, plain = pltpu.SemaphoreType.DMA, pltpu.SemaphoreType.REGULAR
    return [
        pltpu.VMEM((SLOTS, 2 * depth, PART, width), BF),
        pltpu.VMEM((SLOTS, depth, PART, width), BF),
        pltpu.VMEM((SLOTS, 2, depth, PART, width), BF),
        dma((SLOTS, 2 * depth)), dma((SLOTS, 2 * depth)), dma((SLOTS, depth)), dma((SLOTS, depth)),
        dma((SLOTS, 2, depth)), dma((SLOTS, 2, depth)), plain, plain, plain((2,)),
    ]


class Layer(NamedTuple):
    norm_gain: Any
    norm_bias: Any
    joint_weight: Any
    joint_bias: Any
    output_weight: Any
    output_bias: Any
    sandwich_gain: Any
    sandwich_bias: Any
    second_gain: Any
    second_bias: Any
    expand_weight: Any
    expand_bias: Any
    reduce_weight: Any
    reduce_bias: Any
    closing_gain: Any
    closing_bias: Any


MATRICES = (2, 4, 10, 12)
VECTORS = tuple(i for i in range(16) if i not in MATRICES)


class Kept(NamedTuple):
    n1: Any
    r1: Any
    a: Any
    qh: Any
    kh: Any
    vh: Any
    probs: Any
    o: Any
    y: Any
    ny: Any
    ry: Any
    nm: Any
    rm: Any
    c: Any
    f: Any
    g: Any
    e: Any
    ne: Any
    re: Any
    out: Any


def dot(left, right, left_dim, right_dim):
    return lax.dot_general(left, right, (((left_dim,), (right_dim,)), ((), ())), preferred_element_type=F32)


def norm_parts(value):
    center = jnp.mean(value, axis=-1, keepdims=True)
    centered = value - center
    rate = lax.rsqrt(jnp.mean(centered * centered, axis=-1, keepdims=True) + EPSILON)
    return centered * rate, rate


def norm_back(grad, normal, rate, gain):
    scaled = grad * gain
    first = jnp.mean(scaled, axis=-1, keepdims=True)
    second = jnp.mean(scaled * normal, axis=-1, keepdims=True)
    gain_grad = jnp.sum(grad * normal, axis=0)
    bias_grad = jnp.sum(grad, axis=0)
    return rate * (scaled - first - normal * second), gain_grad, bias_grad


def heads_of(flat, sequences):
    return flat.reshape(sequences, flat.shape[0] // sequences, HEADS, HEAD_DIM)


def layer_fore(hidden_in, w, lengths):
    sequences = lengths.shape[0]
    model = hidden_in.shape[1]
    hidden = hidden_in.astype(F32)
    n1, r1 = norm_parts(hidden)
    a = (n1 * w.norm_gain + w.norm_bias).astype(BF)
    mixed = dot(a, w.joint_weight, 1, 0)
    q = ((mixed[:, :model] + w.joint_bias[:model]) * QUERY_SCALE).astype(BF)
    k = mixed[:, model : 2 * model].astype(BF)
    v = (mixed[:, 2 * model :] + w.joint_bias[model:]).astype(BF)
    qh, kh, vh = heads_of(q, sequences), heads_of(k, sequences), heads_of(v, sequences)
    scores = jnp.einsum("bqhd,bkhd->bhqk", qh, kh, preferred_element_type=F32)
    slots = scores.shape[-1]
    query_slot = lax.broadcasted_iota(jnp.int32, (sequences, slots, slots), 1)
    key_slot = lax.broadcasted_iota(jnp.int32, (sequences, slots, slots), 2)
    seen = (key_slot <= query_slot) & (key_slot < lengths[:, None, None])
    scores = jnp.where(seen[:, None], scores, MASKED)
    exponent = jnp.exp(RELAX * (scores - jnp.max(scores, axis=-1, keepdims=True)))
    probs = exponent / jnp.sum(exponent, axis=-1, keepdims=True)
    o = jnp.einsum("bhqk,bkhd->bqhd", probs.astype(BF), vh, preferred_element_type=F32)
    o = o.reshape(hidden.shape).astype(BF)
    y = dot(o, w.output_weight, 1, 0) + w.output_bias
    ny, ry = norm_parts(y)
    mid = hidden + ny * w.sandwich_gain + w.sandwich_bias
    nm, rm = norm_parts(mid)
    c = (nm * w.second_gain + w.second_bias).astype(BF)
    f = dot(c, w.expand_weight, 1, 0) + w.expand_bias
    g = jax.nn.gelu(f).astype(BF)
    e = dot(g, w.reduce_weight, 1, 0) + w.reduce_bias
    ne, re = norm_parts(e)
    out = mid + ne * w.closing_gain + w.closing_bias
    return out, Kept(n1, r1, a, qh, kh, vh, probs, o, y, ny, ry, nm, rm, c, f, g, e, ne, re, out)


def layer_back(dout, w, s, want_weights):
    sequences = s.qh.shape[0]
    de, closing_gain, closing_bias = norm_back(dout, s.ne, s.re, w.closing_gain)
    de = de.astype(BF)
    dg = dot(de, w.reduce_weight, 1, 1)
    df = jax.vjp(jax.nn.gelu, s.f)[1](dg)[0].astype(BF)
    dc = dot(df, w.expand_weight, 1, 1)
    dmid, second_gain, second_bias = norm_back(dc, s.nm, s.rm, w.second_gain)
    dmid = dmid + dout
    dy, sandwich_gain, sandwich_bias = norm_back(dmid, s.ny, s.ry, w.sandwich_gain)
    dy = dy.astype(BF)
    do = heads_of(dot(dy, w.output_weight, 1, 1).astype(BF), sequences)
    dprobs = jnp.einsum("bqhd,bkhd->bhqk", do, s.vh, preferred_element_type=F32)
    dv = jnp.einsum("bhqk,bqhd->bkhd", s.probs.astype(BF), do, preferred_element_type=F32)
    ds = RELAX * s.probs * (dprobs - jnp.sum(dprobs * s.probs, axis=-1, keepdims=True))
    ds = ds.astype(BF)
    dq = jnp.einsum("bhqk,bkhd->bqhd", ds, s.kh, preferred_element_type=F32)
    dk = jnp.einsum("bhqk,bqhd->bkhd", ds, s.qh, preferred_element_type=F32)
    flat = dout.shape
    dmixed = jnp.concatenate([dq.reshape(flat) * QUERY_SCALE, dk.reshape(flat), dv.reshape(flat)], axis=1).astype(BF)
    da = dot(dmixed, w.joint_weight, 1, 1)
    dh, norm_gain, norm_bias = norm_back(da, s.n1, s.r1, w.norm_gain)
    din = dmid + dh
    if not want_weights:
        return din, None
    model = flat[1]
    sums = jnp.sum(dmixed.astype(F32), axis=0)
    return din, Layer(
        norm_gain=norm_gain,
        norm_bias=norm_bias,
        joint_weight=dot(s.a, dmixed, 0, 0),
        joint_bias=jnp.concatenate([sums[:model], sums[2 * model :]]),
        output_weight=dot(s.o, dy, 0, 0),
        output_bias=jnp.sum(dy.astype(F32), axis=0),
        sandwich_gain=sandwich_gain,
        sandwich_bias=sandwich_bias,
        second_gain=second_gain,
        second_bias=second_bias,
        expand_weight=dot(s.c, df, 0, 0),
        expand_bias=jnp.sum(df.astype(F32), axis=0),
        reduce_weight=dot(s.g, de, 0, 0),
        reduce_bias=jnp.sum(de.astype(F32), axis=0),
        closing_gain=closing_gain,
        closing_bias=closing_bias,
    )


def passed_along(block, axis, distance):
    devices = range(lax.axis_size(axis))
    route = [(i - distance, i) for i in devices if i - distance in devices]
    return lax.ppermute(block, axis, route)


def local(gather_matrices, scatter_matrices, tokens, lengths, *parameters):
    cotangent = parameters[-1]
    own = parameters[:-1]
    section = lax.axis_index("section")
    micro, rows, model = tokens.shape
    sequences = lengths.shape[1]
    slots = rows // sequences
    total_rows = micro * rows

    packed = jnp.concatenate([own[i] for i in VECTORS], axis=1)
    packed = lax.all_gather(packed, "batch", axis=0, tiled=True).astype(F32)
    w = list(own)
    start = 0
    for i in VECTORS:
        width = own[i].shape[1]
        w[i] = packed[:, start : start + width].reshape(-1)
        start += width
    for i, whole in zip(MATRICES, gather_matrices([own[i] for i in MATRICES])):
        w[i] = whole
    w = Layer(*w)

    flat_lengths = lengths.reshape(-1)
    seen = lax.broadcasted_iota(jnp.int32, (micro * sequences, slots), 1) < flat_lengths[:, None]
    valid = seen.astype(F32).reshape(total_rows, 1)
    source = tokens.reshape(total_rows, model)
    first_out, _ = layer_fore(source, w, flat_lengths)
    incoming = passed_along(first_out.astype(BF), "section", 1)
    out, s = layer_fore(jnp.where(section == 0, source, incoming), w, flat_lengths)
    section_out = out.astype(BF).reshape(1, micro, rows, model)
    squares = jnp.stack([jnp.sum(part * part * valid) for part in (s.y, s.e, s.out)])

    seed = cotangent.reshape(total_rows, model).astype(F32) * valid
    last_in, _ = layer_back(seed, w, s, False)
    incoming = passed_along(last_in.astype(BF), "section", -1)
    din, grads = layer_back(jnp.where(section == 1, seed, incoming.astype(F32)), w, s, True)
    section_grad = din.reshape(1, micro, rows, model)

    result = list(grads)
    for i, part in zip(MATRICES, scatter_matrices([grads[i].astype(BF) for i in MATRICES])):
        result[i] = part
    devices = lax.axis_size("batch")
    small = jnp.concatenate([grads[i].reshape(devices, -1) for i in VECTORS], axis=1)
    small = lax.psum_scatter(small, "batch", scatter_dimension=0, tiled=True)
    start = 0
    for i in VECTORS:
        width = own[i].shape[1]
        result[i] = small[:, start : start + width]
        start += width
    count = jnp.sum(lengths).astype(F32)
    square_all, count_all = lax.psum((squares, count), "batch")
    magnitudes = jnp.sqrt(square_all / (count_all * model))[None]
    return (section_out, section_grad, magnitudes) + tuple(result)


def plain_gather(shards):
    return [lax.all_gather(w, "batch", axis=1, tiled=True)[0] for w in shards]


def plain_scatter(grads):
    return [lax.psum_scatter(g[None], "batch", scatter_dimension=1, tiled=True).astype(F32) for g in grads]


def gather_kernel(depth, *refs):
    own, store, sems = refs[:4], refs[4], refs[5:]
    place = Place(depth)
    place.greet()
    gather = Gather(place, own, store, sems)
    run_gather(gather, 2, lambda item: None)
    gather.drain()


def ring_gather(depth, shards):
    width = shards[1].shape[2]
    whole = pl.pallas_call(
        functools.partial(gather_kernel, depth),
        out_shape=jax.ShapeDtypeStruct((BLOCKS, width, width), BF),
        in_specs=[pl.BlockSpec(memory_space=pl.ANY)] * 4,
        out_specs=pl.BlockSpec(memory_space=pl.ANY),
        scratch_shapes=gather_sems(depth),
        compiler_params=pltpu.CompilerParams(collective_id=1, has_side_effects=True, vmem_limit_bytes=VMEM_LIMIT),
        name="gather",
    )(*[w[0] for w in shards])
    return (
        jnp.concatenate([whole[i] for i in range(3)], axis=1),
        whole[3],
        jnp.concatenate([whole[i] for i in range(4, 8)], axis=1),
        whole[8:].reshape(4 * width, width),
    )


def scatter_kernel(depth, store, joint, output, expand, reduce, *scratch):
    place = Place(depth)
    place.greet()
    outs = [shard_view((joint, output, expand, reduce), item, store.shape[2]) for item in range(BLOCKS)]
    run_scatter(Scatter(place, store, scratch[:3], outs, scratch[3:]), lambda step: None)


def ring_scatter(depth, grads):
    joint, output, expand, reduce = grads
    width = output.shape[1]
    store = jnp.concatenate([
        joint.reshape(width, 3, width).swapaxes(0, 1), output[None],
        expand.reshape(width, 4, width).swapaxes(0, 1), reduce.reshape(4, width, width)])
    shapes = ((PART, 3 * width), (PART, width), (PART, 4 * width), (4 * PART, width))
    parts = pl.pallas_call(
        functools.partial(scatter_kernel, depth),
        out_shape=[jax.ShapeDtypeStruct(shape, F32) for shape in shapes],
        in_specs=[pl.BlockSpec(memory_space=pltpu.VMEM)],
        out_specs=[pl.BlockSpec(memory_space=pltpu.VMEM)] * 4,
        scratch_shapes=scatter_scratch(depth, width),
        compiler_params=pltpu.CompilerParams(collective_id=2, has_side_effects=True, vmem_limit_bytes=VMEM_LIMIT),
        name="scatter",
    )(store)
    return [part[None] for part in parts]


def solution(mesh):
    vector, matrix = P("section", "batch"), P("section", "batch", None)
    kinds = tuple(matrix if i in MATRICES else vector for i in range(16))
    rows = P(None, "batch", None)
    stacked = P("section", None, "batch", None)
    devices = mesh.shape["batch"]
    if devices == 16:
        ways = functools.partial(ring_gather, devices // 4), functools.partial(ring_scatter, devices // 4)
    else:
        ways = plain_gather, plain_scatter
    return jax.shard_map(
        functools.partial(local, *ways),
        mesh=mesh,
        in_specs=(rows, P(None, "batch")) + kinds + (rows,),
        out_specs=(stacked, stacked, P("section", None)) + kinds,
        check_vma=False,
    )
```

```python
import functools
import math
from typing import Any, NamedTuple

import jax
import jax.numpy as jnp
from jax import lax
from jax.experimental import pallas as pl
from jax.experimental.pallas import tpu as pltpu
from jax.sharding import PartitionSpec as P

HEADS = 16
HEAD_DIM = 64
EPSILON = 1e-05
RELAX = 32.0
MASKED = -1000000000.0
QUERY_SCALE = 1.0 / (RELAX * math.sqrt(HEAD_DIM))

BF = jnp.bfloat16
F32 = jnp.float32
VMEM_LIMIT = 62 * 2**20

class Params(NamedTuple):
    norm_gain: Any
    norm_bias: Any
    joint_weight: Any
    joint_bias: Any
    output_weight: Any
    output_bias: Any
    sandwich_gain: Any
    sandwich_bias: Any
    second_gain: Any
    second_bias: Any
    expand_weight: Any
    expand_bias: Any
    reduce_weight: Any
    reduce_bias: Any
    closing_gain: Any
    closing_bias: Any


MATRICES = (2, 4, 10, 12)
VECTORS = tuple(i for i in range(16) if i not in MATRICES)


class Kept(NamedTuple):
    n1: Any
    r1: Any
    a: Any
    qh: Any
    kh: Any
    vh: Any
    probs: Any
    o: Any
    y: Any
    ny: Any
    ry: Any
    nm: Any
    rm: Any
    c: Any
    f: Any
    g: Any
    e: Any
    ne: Any
    re: Any
    out: Any


def dot(left, right, left_dim, right_dim):
    return lax.dot_general(left, right, (((left_dim,), (right_dim,)), ((), ())), preferred_element_type=F32)


def norm_parts(value):
    center = jnp.mean(value, axis=-1, keepdims=True)
    centered = value - center
    rate = lax.rsqrt(jnp.mean(centered * centered, axis=-1, keepdims=True) + EPSILON)
    return centered * rate, rate


def norm_back(grad, normal, rate, gain):
    scaled = grad * gain
    first = jnp.mean(scaled, axis=-1, keepdims=True)
    second = jnp.mean(scaled * normal, axis=-1, keepdims=True)
    gain_grad = jnp.sum(grad * normal, axis=0)
    bias_grad = jnp.sum(grad, axis=0)
    return rate * (scaled - first - normal * second), gain_grad, bias_grad


def heads_of(flat, sequences):
    return flat.reshape(sequences, flat.shape[0] // sequences, HEADS, HEAD_DIM)


def layer_fore(hidden_in, w, lengths):
    sequences = lengths.shape[0]
    model = hidden_in.shape[1]
    hidden = hidden_in.astype(F32)
    n1, r1 = norm_parts(hidden)
    a = (n1 * w.norm_gain + w.norm_bias).astype(BF)
    mixed = dot(a, w.joint_weight, 1, 0)
    q = ((mixed[:, :model] + w.joint_bias[:model]) * QUERY_SCALE).astype(BF)
    k = mixed[:, model : 2 * model].astype(BF)
    v = (mixed[:, 2 * model :] + w.joint_bias[model:]).astype(BF)
    qh, kh, vh = heads_of(q, sequences), heads_of(k, sequences), heads_of(v, sequences)
    scores = jnp.einsum("bqhd,bkhd->bhqk", qh, kh, preferred_element_type=F32)
    slots = scores.shape[-1]
    query_slot = lax.broadcasted_iota(jnp.int32, (sequences, slots, slots), 1)
    key_slot = lax.broadcasted_iota(jnp.int32, (sequences, slots, slots), 2)
    seen = (key_slot <= query_slot) & (key_slot < lengths[:, None, None])
    scores = jnp.where(seen[:, None], scores, MASKED)
    exponent = jnp.exp(RELAX * (scores - jnp.max(scores, axis=-1, keepdims=True)))
    probs = exponent / jnp.sum(exponent, axis=-1, keepdims=True)
    o = jnp.einsum("bhqk,bkhd->bqhd", probs.astype(BF), vh, preferred_element_type=F32)
    o = o.reshape(hidden.shape).astype(BF)
    y = dot(o, w.output_weight, 1, 0) + w.output_bias
    ny, ry = norm_parts(y)
    mid = hidden + ny * w.sandwich_gain + w.sandwich_bias
    nm, rm = norm_parts(mid)
    c = (nm * w.second_gain + w.second_bias).astype(BF)
    f = dot(c, w.expand_weight, 1, 0) + w.expand_bias
    g = jax.nn.gelu(f).astype(BF)
    e = dot(g, w.reduce_weight, 1, 0) + w.reduce_bias
    ne, re = norm_parts(e)
    out = mid + ne * w.closing_gain + w.closing_bias
    return out, Kept(n1, r1, a, qh, kh, vh, probs, o, y, ny, ry, nm, rm, c, f, g, e, ne, re, out)


def layer_back(dout, w, s, want_weights):
    sequences = s.qh.shape[0]
    de, closing_gain, closing_bias = norm_back(dout, s.ne, s.re, w.closing_gain)
    de = de.astype(BF)
    dg = dot(de, w.reduce_weight, 1, 1)
    df = jax.vjp(jax.nn.gelu, s.f)[1](dg)[0].astype(BF)
    dc = dot(df, w.expand_weight, 1, 1)
    dmid, second_gain, second_bias = norm_back(dc, s.nm, s.rm, w.second_gain)
    dmid = dmid + dout
    dy, sandwich_gain, sandwich_bias = norm_back(dmid, s.ny, s.ry, w.sandwich_gain)
    dy = dy.astype(BF)
    do = heads_of(dot(dy, w.output_weight, 1, 1).astype(BF), sequences)
    dprobs = jnp.einsum("bqhd,bkhd->bhqk", do, s.vh, preferred_element_type=F32)
    dv = jnp.einsum("bhqk,bqhd->bkhd", s.probs.astype(BF), do, preferred_element_type=F32)
    ds = RELAX * s.probs * (dprobs - jnp.sum(dprobs * s.probs, axis=-1, keepdims=True))
    ds = ds.astype(BF)
    dq = jnp.einsum("bhqk,bkhd->bqhd", ds, s.kh, preferred_element_type=F32)
    dk = jnp.einsum("bhqk,bqhd->bkhd", ds, s.qh, preferred_element_type=F32)
    flat = dout.shape
    dmixed = jnp.concatenate([dq.reshape(flat) * QUERY_SCALE, dk.reshape(flat), dv.reshape(flat)], axis=1).astype(BF)
    da = dot(dmixed, w.joint_weight, 1, 1)
    dh, norm_gain, norm_bias = norm_back(da, s.n1, s.r1, w.norm_gain)
    din = dmid + dh
    if not want_weights:
        return din, None
    model = flat[1]
    sums = jnp.sum(dmixed.astype(F32), axis=0)
    return din, Params(
        norm_gain=norm_gain,
        norm_bias=norm_bias,
        joint_weight=dot(s.a, dmixed, 0, 0),
        joint_bias=jnp.concatenate([sums[:model], sums[2 * model :]]),
        output_weight=dot(s.o, dy, 0, 0),
        output_bias=jnp.sum(dy.astype(F32), axis=0),
        sandwich_gain=sandwich_gain,
        sandwich_bias=sandwich_bias,
        second_gain=second_gain,
        second_bias=second_bias,
        expand_weight=dot(s.c, df, 0, 0),
        expand_bias=jnp.sum(df.astype(F32), axis=0),
        reduce_weight=dot(s.g, de, 0, 0),
        reduce_bias=jnp.sum(de.astype(F32), axis=0),
        closing_gain=closing_gain,
        closing_bias=closing_bias,
    )


def passed_along(block, axis, distance):
    devices = range(lax.axis_size(axis))
    route = [(i - distance, i) for i in devices if i - distance in devices]
    return lax.ppermute(block, axis, route)


def plain_local(tokens, lengths, *parameters):
    cotangent = parameters[-1]
    own = parameters[:-1]
    section = lax.axis_index("section")
    micro, rows, model = tokens.shape
    sequences = lengths.shape[1]
    slots = rows // sequences
    total_rows = micro * rows

    packed = jnp.concatenate([own[i] for i in VECTORS], axis=1)
    packed = lax.all_gather(packed, "batch", axis=0, tiled=True).astype(F32)
    w = list(own)
    start = 0
    for i in VECTORS:
        width = own[i].shape[1]
        w[i] = packed[:, start : start + width].reshape(-1)
        start += width
    for i, whole in zip(MATRICES, plain_gather([own[i] for i in MATRICES])):
        w[i] = whole
    w = Params(*w)

    flat_lengths = lengths.reshape(-1)
    seen = lax.broadcasted_iota(jnp.int32, (micro * sequences, slots), 1) < flat_lengths[:, None]
    valid = seen.astype(F32).reshape(total_rows, 1)
    source = tokens.reshape(total_rows, model)
    first_out, _ = layer_fore(source, w, flat_lengths)
    incoming = passed_along(first_out.astype(BF), "section", 1)
    out, s = layer_fore(jnp.where(section == 0, source, incoming), w, flat_lengths)
    section_out = out.astype(BF).reshape(1, micro, rows, model)
    squares = jnp.stack([jnp.sum(part * part * valid) for part in (s.y, s.e, s.out)])

    seed = cotangent.reshape(total_rows, model).astype(F32) * valid
    last_in, _ = layer_back(seed, w, s, False)
    incoming = passed_along(last_in.astype(BF), "section", -1)
    din, grads = layer_back(jnp.where(section == 1, seed, incoming.astype(F32)), w, s, True)
    section_grad = din.reshape(1, micro, rows, model)

    result = list(grads)
    for i, part in zip(MATRICES, plain_scatter([grads[i].astype(BF) for i in MATRICES])):
        result[i] = part
    devices = lax.axis_size("batch")
    small = jnp.concatenate([grads[i].reshape(devices, -1) for i in VECTORS], axis=1)
    small = lax.psum_scatter(small, "batch", scatter_dimension=0, tiled=True)
    start = 0
    for i in VECTORS:
        width = own[i].shape[1]
        result[i] = small[:, start : start + width]
        start += width
    count = jnp.sum(lengths).astype(F32)
    square_all, count_all = lax.psum((squares, count), "batch")
    magnitudes = jnp.sqrt(square_all / (count_all * model))[None]
    return (section_out, section_grad, magnitudes) + tuple(result)


def plain_gather(shards):
    return [lax.all_gather(w, "batch", axis=1, tiled=True)[0] for w in shards]


def plain_scatter(grads):
    return [lax.psum_scatter(g[None], "batch", scatter_dimension=1, tiled=True).astype(F32) for g in grads]


MESH = pl.DeviceIdType.MESH
BLOCKS = 12
VECTOR_ITEM = 12
PART = 64
SLOTS = 4
GATHER_ORDER = (VECTOR_ITEM,) + tuple(range(BLOCKS))
GATHER_CROSSED = (3, 11)
GATHER_AHEAD = 3
SCATTER_ORDER = (8, 9, 10, 11, 4, 5, 6, 7, 3, 0, 1, 2)
UP, DOWN, SIDE = 0, 1, 2


def when(condition, action):
    if condition is True:
        action()
    else:
        pl.when(condition)(action)


def both(first, second):
    if first is True:
        return second
    if second is True:
        return first
    return first & second


class Place:
    def __init__(self, depth):
        index = lax.axis_index("batch")
        self.s = lax.axis_index("section")
        self.depth = depth
        self.z = index // 4
        self.x = (index // 2) % 2
        self.c = index % 2

    def device(self, z, x, c):
        return (self.s, (z * 2 + x) * 2 + c)

    def shard(self, z, x, c):
        return (z * 2 + x) * 2 + c

    def me(self):
        return self.shard(self.z, self.x, self.c)

    def across(self):
        return (1 - self.s, self.me())

    def greet(self):
        z, x, c = self.z, self.x, self.c
        sem = pltpu.get_barrier_semaphore()

        def signal(device):
            pl.semaphore_signal(sem, inc=1, device_id=device, device_id_type=MESH)

        signal(self.device(z, 1 - x, c))
        signal(self.device(z, x, 1 - c))
        signal(self.across())
        pl.when(z < self.depth - 1)(lambda: signal(self.device(z + 1, x, c)))
        pl.when(z > 0)(lambda: signal(self.device(z - 1, x, c)))
        chain = (z < self.depth - 1).astype(jnp.int32) + (z > 0).astype(jnp.int32)
        pl.semaphore_wait(sem, 3 + chain)


def spot(item, shard):
    if item < 8:
        return item, pl.multiple_of(shard * PART, 16)
    return 8 + shard // 4, pl.multiple_of((shard % 4) * 4 * PART + (item - 8) * PART, 16)


def shard_view(refs, item, width):
    joint, output, expand, reduce, vectors = refs
    if item < 3:
        return joint.at[:, pl.ds(item * width, width)]
    if item == 3:
        return output
    if item < 8:
        return expand.at[:, pl.ds((item - 4) * width, width)]
    if item < VECTOR_ITEM:
        return reduce.at[pl.ds((item - 8) * PART, PART)]
    return vectors


class Gather:
    def __init__(self, place, own, store, vectors, sems):
        self.p, self.own, self.store, self.vectors = place, own, store, vectors
        self.send, self.share, self.recv, self.local = sems
        self.sent = []

    def at(self, item, shard):
        if item == VECTOR_ITEM:
            return self.vectors.at[shard]
        block, row = spot(item, shard)
        return self.store.at[block, pl.ds(row, PART)]

    def copy(self, item, shard, way, first=False):
        p = self.p
        target = self.at(item, shard)
        source = shard_view(self.own, item, self.store.shape[2]) if first else target
        recv = self.recv.at[item, shard]
        if way is None:
            send, device = self.share.at[item, shard // 2], p.device(p.z, p.x, 1 - p.c)
        else:
            send = self.send.at[item, shard // 2, way]
            device = (p.device(p.z + 1, p.x, p.c), p.device(p.z - 1, p.x, p.c), p.device(p.z, 1 - p.x, p.c))[way]
        return pltpu.make_async_remote_copy(source, target, send, recv, device_id=device, device_id_type=MESH)

    def go(self, item, shard, way, condition, first=False):
        self.sent.append((item, shard, way, condition, first))
        when(condition, lambda: self.copy(item, shard, way, first).start())

    def arrived(self, item, shard):
        self.copy(item, shard, None).wait_recv()

    def keep_own(self):
        me = self.p.me()
        copies = [
            pltpu.make_async_copy(shard_view(self.own, item, self.store.shape[2]), self.at(item, me), self.local.at[item])
            for item in range(BLOCKS + 1)
        ]
        for copy in copies:
            copy.start()
        return copies

    def own_sends(self, item):
        p = self.p
        self.go(item, p.me(), UP, p.z < p.depth - 1, True)
        self.go(item, p.me(), DOWN, p.z > 0, True)
        self.go(item, p.me(), SIDE, True, True)
        self.go(item, p.me(), None, True, True)

    def chain_round(self, item, hop):
        p = self.p
        crossed = item in GATHER_CROSSED
        for x in (p.x, 1 - p.x) if crossed else (p.x,):
            for origin, present, way, onward in (
                (p.z - hop, p.z >= hop, UP, p.z < p.depth - 1),
                (p.z + hop, p.z + hop < p.depth, DOWN, p.z > 0),
            ):
                shard = p.shard(origin, x, p.c)
                when(present, lambda: self.arrived(item, shard))
                self.go(item, shard, way, both(present, onward))
                if not crossed:
                    self.go(item, shard, SIDE, present)
                self.go(item, shard, None, present)

    def side_own(self, item):
        p = self.p
        shard = p.shard(p.z, 1 - p.x, p.c)
        self.arrived(item, shard)
        if item in GATHER_CROSSED:
            self.go(item, shard, UP, p.z < p.depth - 1)
            self.go(item, shard, DOWN, p.z > 0)
        self.go(item, shard, None, True)

    def side_round(self, item, hop):
        p = self.p
        if item in GATHER_CROSSED:
            return
        for origin, present in ((p.z - hop, p.z >= hop), (p.z + hop, p.z + hop < p.depth)):
            shard = p.shard(origin, 1 - p.x, p.c)
            when(present, lambda: self.arrived(item, shard))
            self.go(item, shard, None, present)

    def rest(self, item):
        p = self.p
        for z in range(p.depth):
            for x in range(2):
                self.arrived(item, p.shard(z, x, 1 - p.c))

    def drain(self):
        for item, shard, way, condition, first in self.sent:
            when(condition, lambda: self.copy(item, shard, way, first).wait_send())


def run_gather(gather, ready):
    depth, count = gather.p.depth, len(GATHER_ORDER)
    kept = gather.keep_own()
    for item in GATHER_ORDER[:GATHER_AHEAD]:
        gather.own_sends(item)

    def finish(item):
        for hop in range(1, depth):
            gather.side_round(item, hop)
        gather.rest(item)
        kept[item].wait()
        ready(item)

    for place, item in enumerate(GATHER_ORDER):
        if item in GATHER_CROSSED:
            gather.side_own(item)
        for hop in range(1, depth):
            gather.chain_round(item, hop)
            if hop == 1:
                if place + GATHER_AHEAD < count:
                    gather.own_sends(GATHER_ORDER[place + GATHER_AHEAD])
                if item not in GATHER_CROSSED:
                    gather.side_own(item)
        if place >= 1:
            finish(GATHER_ORDER[place - 1])
    finish(GATHER_ORDER[-1])


def gather_sems(depth):
    kind, items = pltpu.SemaphoreType.DMA, BLOCKS + 1
    return [kind((items, 2 * depth, 3)), kind((items, 2 * depth)), kind((items, 4 * depth)), kind((items,))]


def total(*refs):
    value = refs[0][...].astype(F32)
    for ref in refs[1:]:
        value = value + ref[...].astype(F32)
    return value


class Scatter:
    def __init__(self, place, part, count, slots, buffers, outs, sems):
        self.p, self.part, self.count, self.slots, self.outs = place, part, count, slots, outs
        self.core_in, self.side_in, self.chain_in = buffers
        (self.core_send, self.core_recv, self.side_send, self.side_recv, self.chain_send, self.chain_recv,
         self.core_free, self.side_free, self.chain_free) = sems
        depth = place.depth
        self.origins = [q for pair in zip(range(depth - 1, -1, -1), range(depth)) for q in pair][:depth]

    def mine(self, step, z, x, c):
        return self.part(step, self.p.shard(z, x, c))

    def core_copy(self, step, z, x):
        p, slot = self.p, step % self.slots
        return pltpu.make_async_remote_copy(
            self.mine(step, z, x, 1 - p.c), self.core_in.at[slot, z * 2 + x],
            self.core_send.at[slot, z * 2 + x], self.core_recv.at[slot, z * 2 + x],
            device_id=p.device(p.z, p.x, 1 - p.c), device_id_type=MESH)

    def side_copy(self, step, z):
        p, slot = self.p, step % self.slots
        return pltpu.make_async_remote_copy(
            self.mine(step, z, 1 - p.x, p.c), self.side_in.at[slot, z],
            self.side_send.at[slot, z], self.side_recv.at[slot, z],
            device_id=p.device(p.z, 1 - p.x, p.c), device_id_type=MESH)

    def chain_copy(self, step, z, up):
        p, slot = self.p, step % self.slots
        return pltpu.make_async_remote_copy(
            self.mine(step, z, p.x, p.c), self.chain_in.at[slot, 1 - up, z],
            self.chain_send.at[slot, 1 - up, z], self.chain_recv.at[slot, 1 - up, z],
            device_id=p.device(p.z + 2 * up - 1, p.x, p.c), device_id_type=MESH)

    def core_stage(self, step):
        if step >= self.slots:
            for z in self.origins:
                for x in range(2):
                    self.core_copy(step - self.slots, z, x).wait_send()
            pl.semaphore_wait(self.core_free, 1)
        for z in self.origins:
            for x in range(2):
                self.core_copy(step, z, x).start()

    def from_core(self, step, z, x):
        self.core_copy(step, z, x).wait_recv()
        return self.core_in.at[step % self.slots, z * 2 + x]

    def side_stage(self, step):
        p = self.p
        if step >= self.slots:
            for z in self.origins:
                self.side_copy(step - self.slots, z).wait_send()
            pl.semaphore_wait(self.side_free, 1)
        for z in self.origins:
            twin = self.from_core(step, z, 1 - p.x)
            mine = self.mine(step, z, 1 - p.x, p.c)
            mine[...] = total(mine, twin).astype(mine.dtype)
            self.side_copy(step, z).start()

    def chain_stage(self, step):
        p, slot, last = self.p, step % self.slots, self.p.depth - 1
        if step >= self.slots:
            for z in self.origins:
                up = (p.z < z).astype(jnp.int32)
                pl.when(p.z != z)(lambda: self.chain_copy(step - self.slots, z, up).wait_send())
            pl.when(p.z < last)(lambda: pl.semaphore_wait(self.chain_free.at[0], 1))
            pl.when(p.z > 0)(lambda: pl.semaphore_wait(self.chain_free.at[1], 1))
        for z in self.origins:
            up = (p.z < z).astype(jnp.int32)
            fed = ((p.z < z) & (p.z > 0)) | ((p.z > z) & (p.z < last))

            @pl.when(p.z != z)
            def _():
                twin = self.from_core(step, z, p.x)
                mine = self.mine(step, z, p.x, p.c)
                self.side_copy(step, z).wait_recv()
                side = self.side_in.at[slot, z]

                @pl.when(fed)
                def _():
                    self.chain_copy(step, z, up).wait_recv()
                    mine[...] = total(mine, twin, side, self.chain_in.at[slot, 1 - up, z]).astype(mine.dtype)

                @pl.when(jnp.logical_not(fed))
                def _():
                    mine[...] = total(mine, twin, side).astype(mine.dtype)

                self.chain_copy(step, z, up).start()

    def own_stage(self, step):
        p, slot, last = self.p, step % self.slots, self.p.depth - 1
        twin = self.from_core(step, p.z, p.x)
        self.side_copy(step, p.z).wait_recv()
        parts = [self.mine(step, p.z, p.x, p.c), twin, self.side_in.at[slot, p.z]]
        pl.when(p.z > 0)(lambda: self.chain_copy(step, p.z, 1).wait_recv())
        pl.when(p.z < last)(lambda: self.chain_copy(step, p.z, 0).wait_recv())
        below, above = self.chain_in.at[slot, 0, p.z], self.chain_in.at[slot, 1, p.z]
        out = self.outs[step]

        def put(*refs):
            out[...] = total(*refs)

        pl.when(p.z == 0)(lambda: put(*parts, above))
        pl.when(p.z == last)(lambda: put(*parts, below))
        pl.when((p.z > 0) & (p.z < last))(lambda: put(*parts, below, above))
        if step + self.slots < self.count:
            def signal(sem, device):
                pl.semaphore_signal(sem, inc=1, device_id=device, device_id_type=MESH)

            signal(self.core_free, p.device(p.z, p.x, 1 - p.c))
            signal(self.side_free, p.device(p.z, 1 - p.x, p.c))
            pl.when(p.z > 0)(lambda: signal(self.chain_free.at[0], p.device(p.z - 1, p.x, p.c)))
            pl.when(p.z < last)(lambda: signal(self.chain_free.at[1], p.device(p.z + 1, p.x, p.c)))

    def drain(self):
        p = self.p
        for step in range(self.count - self.slots, self.count):
            for z in self.origins:
                for x in range(2):
                    self.core_copy(step, z, x).wait_send()
                self.side_copy(step, z).wait_send()
                up = (p.z < z).astype(jnp.int32)
                pl.when(p.z != z)(lambda: self.chain_copy(step, z, up).wait_send())


def run_scatter(scatter, vector_scatter, ready):
    for tick in range(BLOCKS + 4):
        if tick < BLOCKS:
            ready(tick)
        if tick >= 4:
            scatter.own_stage(tick - 4)
        if tick < BLOCKS:
            scatter.core_stage(tick)
        if 1 <= tick <= BLOCKS:
            scatter.side_stage(tick - 1)
        if 2 <= tick < BLOCKS + 2:
            scatter.chain_stage(tick - 2)
        if tick == BLOCKS - 1:
            vector_scatter.core_stage(0)
        if tick == BLOCKS:
            vector_scatter.side_stage(0)
        if tick == BLOCKS + 1:
            vector_scatter.chain_stage(0)
    vector_scatter.own_stage(0)
    scatter.drain()
    vector_scatter.drain()


def scatter_scratch(depth, slots, rows, width, dtype):
    dma, plain = pltpu.SemaphoreType.DMA, pltpu.SemaphoreType.REGULAR
    return [
        pltpu.VMEM((slots, 2 * depth, rows, width), dtype),
        pltpu.VMEM((slots, depth, rows, width), dtype),
        pltpu.VMEM((slots, 2, depth, rows, width), dtype),
        dma((slots, 2 * depth)), dma((slots, 2 * depth)), dma((slots, depth)), dma((slots, depth)),
        dma((slots, 2, depth)), dma((slots, 2, depth)), plain, plain, plain((2,)),
    ]


(NORM_GAIN, NORM_BIAS, OUTPUT_BIAS, SANDWICH_GAIN, SANDWICH_BIAS, SECOND_GAIN, SECOND_BIAS, REDUCE_BIAS,
 CLOSING_GAIN, CLOSING_BIAS, QUERY_BIAS, VALUE_BIAS, EXPAND_BIAS) = range(13)
NARROW = 10
VECTOR_ROWS = 16
FIGURES = 13
LANES = 128
TILE = 256
CHUNK = 32
CURVE = math.sqrt(2.0 / math.pi)
BEND = 0.044715


class Work(NamedTuple):
    vec: Any
    dvec: Any
    h: Any
    a: Any
    q: Any
    k: Any
    v: Any
    p: Any
    o: Any
    n_h: Any
    r_h: Any
    n_y: Any
    r_y: Any
    n_m: Any
    r_m: Any
    n_e: Any
    r_e: Any
    mid: Any
    c: Any
    g: Any
    slope: Any
    de: Any
    dy: Any
    do: Any
    din: Any
    sums: Any


def mxu(left, right, left_dim, right_dim):
    return lax.dot_general(left, right, (((left_dim,), (right_dim,)), ((), ())), preferred_element_type=F32)


def mean_of(value):
    return jnp.mean(value, axis=-1, keepdims=True)


def norm_of(value):
    centered = value - mean_of(value)
    rate = lax.rsqrt(mean_of(centered * centered) + EPSILON)
    return centered * rate, rate


def norm_pull(grad, normal, rate, gain):
    scaled = grad * gain
    return rate * (scaled - mean_of(scaled) - normal * mean_of(scaled * normal))


def column_sum(value):
    return jnp.sum(value, axis=0, keepdims=True)


class Layer:
    def __init__(self, work, store, lengths):
        self.w, self.store, self.lengths = work, store, lengths
        self.tokens, self.width = work.h.shape
        self.sequences = lengths.shape[0]
        self.slots = self.tokens // self.sequences

    def row(self, index):
        return self.w.vec[index : index + 1, :]

    def add(self, index, value):
        self.w.dvec[index : index + 1, :] += value

    def chunks(self, body, first=0, last=None):
        last = self.tokens if last is None else last

        def step(i, carry):
            body(pl.ds(pl.multiple_of(i * CHUNK, CHUNK), CHUNK), i)
            return carry

        lax.fori_loop(first // CHUNK, last // CHUNK, step, 0)

    def tiles(self, body):
        def step(i, carry):
            body(pl.ds(pl.multiple_of(i * TILE, TILE), TILE))
            return carry

        lax.fori_loop(0, self.width // TILE, step, 0)

    def valid(self, i):
        per = self.slots // CHUNK
        slot = (i % per) * CHUNK + lax.broadcasted_iota(jnp.int32, (CHUNK, 1), 0)
        return jnp.where(slot < self.lengths[i // per], 1.0, 0.0)


    def fore_start(self, source, first=0, last=None):
        w = self.w

        def body(rows, i):
            h = source[rows, :]
            w.h[rows, :] = h
            normal, rate = norm_of(h.astype(F32))
            w.n_h[rows, :] = normal
            w.r_h[rows, :] = rate
            w.a[rows, :] = (normal * self.row(NORM_GAIN) + self.row(NORM_BIAS)).astype(BF)

        self.chunks(body, first, last)

    def fore_joint(self, block):
        w = self.w
        bias = (QUERY_BIAS, None, VALUE_BIAS)[block]
        target = (w.q, w.k, w.v)[block]

        def body(tile):
            mixed = mxu(w.a[...], self.store[block, :, tile], 1, 0)
            if bias is not None:
                mixed = mixed + w.vec[bias : bias + 1, tile]
            if block == 0:
                mixed = mixed * QUERY_SCALE
            target[:, tile] = mixed.astype(BF)

        self.tiles(body)

    def pairs(self, body):
        count = self.width // LANES

        def step(i, carry):
            sequence, pair = i // count, i % count
            rows = pl.ds(pl.multiple_of(sequence * self.slots, self.slots), self.slots)
            lanes = pl.ds(pl.multiple_of(pair * LANES, LANES), LANES)
            body(rows, lanes, i, self.lengths[sequence])
            return carry

        lax.fori_loop(0, self.sequences * count, step, 0, unroll=2)

    def split(self, value):
        low = lax.broadcasted_iota(jnp.int32, value.shape, 1) < HEAD_DIM
        zero = jnp.zeros_like(value)
        return jnp.concatenate([jnp.where(low, value, zero), jnp.where(low, zero, value)], axis=0)

    def fore_attention(self):
        w, slots = self.w, self.slots

        def body(rows, lanes, i, length):
            scores = mxu(self.split(w.q[rows, lanes]), w.k[rows, lanes], 1, 1)
            query = lax.broadcasted_iota(jnp.int32, (2 * slots, slots), 0) % slots
            key = lax.broadcasted_iota(jnp.int32, (2 * slots, slots), 1)
            scores = jnp.where((key <= query) & (key < length), scores, MASKED)
            weight = jnp.exp(RELAX * (scores - jnp.max(scores, axis=-1, keepdims=True)))
            probs = (weight / jnp.sum(weight, axis=-1, keepdims=True)).astype(BF)
            w.p[i] = probs
            wide = jnp.concatenate([probs[:slots], probs[slots:]], axis=1)
            w.o[rows, lanes] = mxu(wide, self.split(w.v[rows, lanes]), 1, 0).astype(BF)

        self.pairs(body)

    def fore_output(self):
        w = self.w

        def body(tile):
            w.n_y[:, tile] = mxu(w.o[...], self.store[3, :, tile], 1, 0) + w.vec[OUTPUT_BIAS : OUTPUT_BIAS + 1, tile]

        self.tiles(body)

        def middle(rows, i):
            y = w.n_y[rows, :]
            w.sums[0:1, :] += column_sum(y * y * self.valid(i))
            normal, rate = norm_of(y)
            w.n_y[rows, :] = normal
            w.r_y[rows, :] = rate
            mid = w.h[rows, :].astype(F32) + (normal * self.row(SANDWICH_GAIN) + self.row(SANDWICH_BIAS))
            w.mid[rows, :] = mid
            normal, rate = norm_of(mid)
            w.n_m[rows, :] = normal
            w.r_m[rows, :] = rate
            w.c[rows, :] = (normal * self.row(SECOND_GAIN) + self.row(SECOND_BIAS)).astype(BF)

        self.chunks(middle)

    def fore_expand(self, block):
        w = self.w

        def body(tile):
            f = mxu(w.c[...], self.store[4 + block, :, tile], 1, 0)
            f = f + w.vec[EXPAND_BIAS + block : EXPAND_BIAS + block + 1, tile]
            square = f * f
            bent = jnp.tanh(CURVE * f * (1.0 + BEND * square))
            half = 0.5 * (1.0 + bent)
            w.g[block, :, tile] = (f * half).astype(BF)
            slope = half + 0.5 * f * (1.0 - bent * bent) * (CURVE * (1.0 + 3.0 * BEND * square))
            w.slope[block, :, tile] = slope.astype(BF)

        self.tiles(body)

    def fore_reduce(self):
        w = self.w

        def body(tile):
            e = mxu(w.g[0], self.store[8, :, tile], 1, 0)
            for block in range(1, 4):
                e = e + mxu(w.g[block], self.store[8 + block, :, tile], 1, 0)
            w.n_e[:, tile] = e + w.vec[REDUCE_BIAS : REDUCE_BIAS + 1, tile]

        self.tiles(body)

    def fore_end(self, target, first=0, last=None):
        w = self.w

        def body(rows, i):
            e = w.n_e[rows, :]
            valid = self.valid(i)
            w.sums[1:2, :] += column_sum(e * e * valid)
            normal, rate = norm_of(e)
            w.n_e[rows, :] = normal
            w.r_e[rows, :] = rate
            out = w.mid[rows, :] + (normal * self.row(CLOSING_GAIN) + self.row(CLOSING_BIAS))
            w.sums[2:3, :] += column_sum(out * out * valid)
            target[rows, :] = out.astype(BF)

        self.chunks(body, first, last)


    def back_start(self, seed, masked):
        w = self.w

        def body(rows, i):
            dout = seed[rows, :].astype(F32)
            if masked:
                dout = dout * self.valid(i)
            w.din[rows, :] = dout
            normal = w.n_e[rows, :]
            self.add(CLOSING_GAIN, column_sum(dout * normal))
            self.add(CLOSING_BIAS, column_sum(dout))
            de = norm_pull(dout, normal, w.r_e[rows, :], self.row(CLOSING_GAIN)).astype(BF)
            w.de[rows, :] = de
            self.add(REDUCE_BIAS, column_sum(de.astype(F32)))

        self.chunks(body)

    def back_reduce(self, block):
        w = self.w

        def body(tile):
            df = (mxu(w.de[...], self.store[8 + block, tile, :], 1, 1) * w.slope[block, :, tile].astype(F32)).astype(BF)
            w.slope[block, :, tile] = df
            w.dvec[EXPAND_BIAS + block : EXPAND_BIAS + block + 1, tile] = column_sum(df.astype(F32))

        self.tiles(body)

    def back_expand(self):
        w = self.w

        def body(tile):
            dc = mxu(w.slope[0], self.store[4, tile, :], 1, 1)
            for block in range(1, 4):
                dc = dc + mxu(w.slope[block], self.store[4 + block, tile, :], 1, 1)
            w.mid[:, tile] = dc

        self.tiles(body)

        def middle(rows, i):
            dc = w.mid[rows, :]
            normal = w.n_m[rows, :]
            self.add(SECOND_GAIN, column_sum(dc * normal))
            self.add(SECOND_BIAS, column_sum(dc))
            dmid = w.din[rows, :] + norm_pull(dc, normal, w.r_m[rows, :], self.row(SECOND_GAIN))
            w.din[rows, :] = dmid
            normal = w.n_y[rows, :]
            self.add(SANDWICH_GAIN, column_sum(dmid * normal))
            self.add(SANDWICH_BIAS, column_sum(dmid))
            dy = norm_pull(dmid, normal, w.r_y[rows, :], self.row(SANDWICH_GAIN)).astype(BF)
            w.dy[rows, :] = dy
            self.add(OUTPUT_BIAS, column_sum(dy.astype(F32)))

        self.chunks(middle)

    def back_output(self):
        w = self.w

        def body(tile):
            w.do[:, tile] = mxu(w.dy[...], self.store[3, tile, :], 1, 1).astype(BF)

        self.tiles(body)

    def back_attention(self):
        w, slots = self.w, self.slots

        def body(rows, lanes, i, length):
            grad = self.split(w.do[rows, lanes])
            probs = w.p[i]
            value = probs.astype(F32)
            dprobs = mxu(grad, w.v[rows, lanes], 1, 1)
            inner = jnp.sum(dprobs * value, axis=-1, keepdims=True)
            ds = (RELAX * value * (dprobs - inner)).astype(BF)
            wide = jnp.concatenate([ds[:slots], ds[slots:]], axis=1)
            dv = mxu(probs, grad, 0, 0)
            dk = mxu(ds, self.split(w.q[rows, lanes]), 0, 0)
            dq = mxu(wide, self.split(w.k[rows, lanes]), 1, 0) * QUERY_SCALE
            w.q[rows, lanes] = dq.astype(BF)
            w.k[rows, lanes] = dk.astype(BF)
            w.v[rows, lanes] = dv.astype(BF)

        self.pairs(body)

    def back_joint(self):
        w = self.w

        def body(tile):
            da = mxu(w.q[...], self.store[0, tile, :], 1, 1)
            da = da + mxu(w.k[...], self.store[1, tile, :], 1, 1)
            w.mid[:, tile] = da + mxu(w.v[...], self.store[2, tile, :], 1, 1)

        self.tiles(body)

    def back_end(self, target, first=0, last=None):
        w = self.w

        def body(rows, i):
            da = w.mid[rows, :]
            normal = w.n_h[rows, :]
            self.add(NORM_GAIN, column_sum(da * normal))
            self.add(NORM_BIAS, column_sum(da))
            self.add(QUERY_BIAS, column_sum(w.q[rows, :].astype(F32)))
            self.add(VALUE_BIAS, column_sum(w.v[rows, :].astype(F32)))
            din = w.din[rows, :] + norm_pull(da, normal, w.r_h[rows, :], self.row(NORM_GAIN))
            w.din[rows, :] = din
            target[rows, :] = din.astype(BF)

        self.chunks(body, first, last)


    def weight_grad(self, block):
        w = self.w
        if block < 3:
            left, right = w.a, (w.q, w.k, w.v)[block]
        elif block == 3:
            left, right = w.o, w.dy
        elif block < 8:
            left, right = w.c, w.slope.at[block - 4]
        else:
            left, right = w.g.at[block - 8], w.de

        def body(tile):
            self.store[block, tile, :] = mxu(left[:, tile], right[...], 0, 0).astype(BF)

        self.tiles(body)


def unfold_vectors(tiles, vec, count):
    for pair in range(count // 2):
        vec[:NARROW, pair * LANES : (pair + 1) * LANES] = tiles[2 * pair, :NARROW, :] + tiles[2 * pair + 1, :NARROW, :]
    half, quarter = count // 2, count // 4
    for shard in range(count):
        row, lane = QUERY_BIAS + shard // half, (shard % half) * LANES
        vec[row : row + 1, lane : lane + LANES] = tiles[shard, NARROW : NARROW + 1, :]
        for part in range(2):
            row, lane = EXPAND_BIAS + shard // quarter, ((shard % quarter) * 2 + part) * LANES
            source = NARROW + 1 + part
            vec[row : row + 1, lane : lane + LANES] = tiles[shard, source : source + 1, :]


def fold_vectors(tiles, dvec, figures, count):
    half, quarter = count // 2, count // 4
    for shard in range(count):
        pair = shard // 2
        tiles[shard, :NARROW, :] = dvec[:NARROW, pair * LANES : (pair + 1) * LANES]
        row, lane = QUERY_BIAS + shard // half, (shard % half) * LANES
        tiles[shard, NARROW : NARROW + 1, :] = dvec[row : row + 1, lane : lane + LANES]
        for part in range(2):
            row, lane = EXPAND_BIAS + shard // quarter, ((shard % quarter) * 2 + part) * LANES
            target = NARROW + 1 + part
            tiles[shard, target : target + 1, :] = dvec[row : row + 1, lane : lane + LANES]
        tiles[shard, FIGURES : FIGURES + 1, :] = figures
        tiles[shard, FIGURES + 1 :, :] = jnp.zeros((VECTOR_ROWS - FIGURES - 1, LANES), F32)


def figures_of(sums, lengths):
    lane = lax.broadcasted_iota(jnp.int32, (1, LANES), 1)
    row = jnp.zeros((1, LANES), F32)
    for i in range(3):
        row = jnp.where(lane == i, jnp.sum(sums[i : i + 1, :], axis=1, keepdims=True), row)
    seen = lengths[0]
    for i in range(1, lengths.shape[0]):
        seen = seen + lengths[i]
    return jnp.where(lane == 3, seen.astype(F32), row)


def relay_kernel(depth, lengths, tokens, cotangent, joint, output, expand, reduce, vectors,
                 section_out, section_grad, joint_out, output_out, expand_out, reduce_out, vector_out,
                 store, tiles, vec, dvec, sums, h, a, q, k, v, p, o, n_h, r_h, n_y, r_y, n_m, r_m, n_e, r_e,
                 mid, c, g, slope, de, dy, do, incoming, pass_sems, *rest):
    place = Place(depth)
    width = store.shape[2]
    count = 4 * depth
    gather_parts, rest = rest[:4], rest[4:]
    scatter_parts, vector_parts = rest[:12], rest[12:]
    work = Work(vec, dvec, h, a, q, k, v, p, o, n_h, r_h, n_y, r_y, n_m, r_m, n_e, r_e, mid, c, g, slope,
                de, dy, do, section_grad, sums)
    layer = Layer(work, store, lengths)
    slots = layer.slots
    first, second = place.s == 0, place.s == 1

    def passing(source, target, part, way):
        rows = pl.ds(part * slots, slots)
        return pltpu.make_async_remote_copy(
            source.at[rows], target.at[rows], pass_sems.at[way, 0, part], pass_sems.at[way, 1, part],
            device_id=place.across(), device_id_type=MESH)

    def forward(part):
        return passing(section_out, incoming, part, 0)

    def backward(part):
        return passing(do, incoming, part, 1)

    place.greet()
    dvec[...] = jnp.zeros_like(dvec)
    sums[...] = jnp.zeros_like(sums)

    def ready(item):
        if item == VECTOR_ITEM:
            unfold_vectors(tiles, vec, count)

        @pl.when(first)
        def _():
            if item == VECTOR_ITEM:
                layer.fore_start(tokens)
            elif item < 3:
                layer.fore_joint(item)
                if item == 2:
                    layer.fore_attention()
            elif item == 3:
                layer.fore_output()
            elif item < 8:
                layer.fore_expand(item - 4)
            elif item == BLOCKS - 1:
                layer.fore_reduce()
                for part in range(layer.sequences):
                    layer.fore_end(section_out, part * slots, (part + 1) * slots)
                    forward(part).start()

    gather = Gather(place, (joint, output, expand, reduce, vectors), store, tiles, gather_parts)
    run_gather(gather, ready)
    gather.drain()

    def chain(step):
        block = SCATTER_ORDER[step]
        if step == 0:
            for part in range(4):
                layer.back_reduce(part)
        elif step == 4:
            layer.back_expand()
        elif block == 3:
            layer.back_output()
        elif step == 9:
            layer.back_attention()
            layer.back_joint()

    @pl.when(second)
    def _():
        for part in range(layer.sequences):
            forward(part).wait_recv()
            layer.fore_start(incoming, part * slots, (part + 1) * slots)
        for block in range(3):
            layer.fore_joint(block)
        layer.fore_attention()
        layer.fore_output()
        for block in range(4):
            layer.fore_expand(block)
        layer.fore_reduce()
        layer.fore_end(section_out)
        layer.back_start(cotangent, True)
        for step in range(BLOCKS):
            chain(step)
        for part in range(layer.sequences):
            layer.back_end(do, part * slots, (part + 1) * slots)
            backward(part).start()

    @pl.when(first)
    def _():
        for part in range(layer.sequences):
            backward(part).wait_recv()
        layer.back_start(incoming, False)

    def fill(step):
        block = SCATTER_ORDER[step]

        @pl.when(first)
        def _():
            chain(step)
            if step == 9:
                layer.back_end(do)

        if step == 0:
            for part in range(4):
                layer.weight_grad(8 + part)
        elif step >= 4:
            layer.weight_grad(block)
        if step == BLOCKS - 1:
            fold_vectors(tiles, dvec, figures_of(sums, lengths), count)

    def part_of(step, shard):
        block, row = spot(SCATTER_ORDER[step], shard)
        return store.at[block, pl.ds(row, PART)]

    outs = [shard_view((joint_out, output_out, expand_out, reduce_out, vector_out), item, width) for item in SCATTER_ORDER]
    scatter = Scatter(place, part_of, BLOCKS, SLOTS, scatter_parts[:3], outs, scatter_parts[3:])
    vector_scatter = Scatter(place, lambda step, shard: tiles.at[shard], 1, 1, vector_parts[:3], [vector_out], vector_parts[3:])
    run_scatter(scatter, vector_scatter, fill)

    @pl.when(first)
    def _():
        for part in range(layer.sequences):
            forward(part).wait_send()

    @pl.when(second)
    def _():
        for part in range(layer.sequences):
            backward(part).wait_send()


def relay_local(depth, tokens, lengths, *parameters):
    cotangent, own = parameters[-1], Params(*parameters[:-1])
    micro, rows, width = tokens.shape
    sequences = lengths.shape[1] * micro
    count = micro * rows
    core = lax.axis_index("batch") % 2

    narrow = jnp.concatenate([
        own.norm_gain, own.norm_bias, own.output_bias, own.sandwich_gain, own.sandwich_bias, own.second_gain,
        own.second_bias, own.reduce_bias, own.closing_gain, own.closing_bias]).astype(F32)
    zero = jnp.zeros_like(narrow)
    narrow = jnp.where(core == 0, jnp.concatenate([narrow, zero], axis=1), jnp.concatenate([zero, narrow], axis=1))
    vectors = jnp.concatenate([
        narrow, own.joint_bias.astype(F32), own.expand_bias.astype(F32).reshape(2, LANES),
        jnp.zeros((VECTOR_ROWS - NARROW - 3, LANES), F32)])

    square = jax.ShapeDtypeStruct((count, width), F32)
    low, high, rate = (pltpu.VMEM((count, width), BF), pltpu.VMEM((count, width), F32), pltpu.VMEM((count, 1), F32))
    wide = pltpu.VMEM((4, count, width), BF)
    shards = 4 * depth
    dma = pltpu.SemaphoreType.DMA
    vmem, anywhere = pl.BlockSpec(memory_space=pltpu.VMEM), pl.BlockSpec(memory_space=pl.ANY)
    results = pl.pallas_call(
        functools.partial(relay_kernel, depth),
        out_shape=[
            jax.ShapeDtypeStruct((count, width), BF), square,
            jax.ShapeDtypeStruct((PART, 3 * width), F32), jax.ShapeDtypeStruct((PART, width), F32),
            jax.ShapeDtypeStruct((PART, 4 * width), F32), jax.ShapeDtypeStruct((4 * PART, width), F32),
            jax.ShapeDtypeStruct((VECTOR_ROWS, LANES), F32)],
        in_specs=[pl.BlockSpec(memory_space=pltpu.SMEM), vmem, vmem] + [anywhere] * 5,
        out_specs=[vmem] * 7,
        scratch_shapes=[
            pltpu.VMEM((BLOCKS, width, width), BF), pltpu.VMEM((shards, VECTOR_ROWS, LANES), F32),
            pltpu.VMEM((VECTOR_ROWS, width), F32), pltpu.VMEM((VECTOR_ROWS, width), F32), pltpu.VMEM((8, width), F32),
            low, low, low, low, low, pltpu.VMEM((sequences * width // LANES, 2 * rows // lengths.shape[1], rows // lengths.shape[1]), BF), low,
            high, rate, high, rate, high, rate, high, rate,
            high, low, wide, wide, low, low, low, low, dma((2, 2, sequences)),
        ] + gather_sems(depth) + scatter_scratch(depth, SLOTS, PART, width, BF) + scatter_scratch(depth, 1, VECTOR_ROWS, LANES, F32),
        compiler_params=pltpu.CompilerParams(collective_id=1, has_side_effects=True, vmem_limit_bytes=VMEM_LIMIT),
        cost_estimate=pl.CostEstimate(flops=6 * count * BLOCKS * width * width, bytes_accessed=2 * BLOCKS * width * width, transcendentals=0),
        name="relay",
    )(lengths.reshape(-1), tokens.reshape(count, width), cotangent.reshape(count, width),
      own.joint_weight[0], own.output_weight[0], own.expand_weight[0], own.reduce_weight[0], vectors)
    section_out, section_grad, joint, output, expand, reduce, tile = results

    halves = jnp.where(core == 0, tile[:NARROW, :HEAD_DIM], tile[:NARROW, HEAD_DIM:])
    narrow = [halves[i : i + 1] for i in range(NARROW)]
    figures = tile[FIGURES]
    magnitudes = jnp.sqrt(figures[:3] / (figures[3] * width))[None]
    grads = Params(
        norm_gain=narrow[NORM_GAIN], norm_bias=narrow[NORM_BIAS], joint_weight=joint[None],
        joint_bias=tile[NARROW : NARROW + 1], output_weight=output[None], output_bias=narrow[OUTPUT_BIAS],
        sandwich_gain=narrow[SANDWICH_GAIN], sandwich_bias=narrow[SANDWICH_BIAS], second_gain=narrow[SECOND_GAIN],
        second_bias=narrow[SECOND_BIAS], expand_weight=expand[None],
        expand_bias=tile[NARROW + 1 : NARROW + 3].reshape(1, -1), reduce_weight=reduce[None],
        reduce_bias=narrow[REDUCE_BIAS], closing_gain=narrow[CLOSING_GAIN], closing_bias=narrow[CLOSING_BIAS])
    shape = (1, micro, rows, width)
    return (section_out.reshape(shape), section_grad.reshape(shape), magnitudes) + tuple(grads)


def solution(mesh):
    vector, matrix = P("section", "batch"), P("section", "batch", None)
    kinds = tuple(matrix if i in MATRICES else vector for i in range(16))
    rows = P(None, "batch", None)
    stacked = P("section", None, "batch", None)
    devices = mesh.shape["batch"]
    body = functools.partial(relay_local, devices // 4) if devices == 16 else plain_local
    return jax.shard_map(
        body,
        mesh=mesh,
        in_specs=(rows, P(None, "batch")) + kinds + (rows,),
        out_specs=(stacked, stacked, P("section", None)) + kinds,
        check_vma=False,
    )
```

```python
import functools
import math
from typing import Any, NamedTuple

import jax
import jax.numpy as jnp
from jax import lax
from jax.experimental import pallas as pl
from jax.experimental.pallas import tpu as pltpu
from jax.sharding import PartitionSpec as P

HEADS = 16
HEAD_DIM = 64
EPSILON = 1e-05
RELAX = 32.0
MASKED = -1000000000.0
QUERY_SCALE = 1.0 / (RELAX * math.sqrt(HEAD_DIM))

BF = jnp.bfloat16
F32 = jnp.float32
VMEM_LIMIT = 62 * 2**20

class Params(NamedTuple):
    norm_gain: Any
    norm_bias: Any
    joint_weight: Any
    joint_bias: Any
    output_weight: Any
    output_bias: Any
    sandwich_gain: Any
    sandwich_bias: Any
    second_gain: Any
    second_bias: Any
    expand_weight: Any
    expand_bias: Any
    reduce_weight: Any
    reduce_bias: Any
    closing_gain: Any
    closing_bias: Any


MATRICES = (2, 4, 10, 12)
VECTORS = tuple(i for i in range(16) if i not in MATRICES)


class Kept(NamedTuple):
    n1: Any
    r1: Any
    a: Any
    qh: Any
    kh: Any
    vh: Any
    probs: Any
    o: Any
    y: Any
    ny: Any
    ry: Any
    nm: Any
    rm: Any
    c: Any
    f: Any
    g: Any
    e: Any
    ne: Any
    re: Any
    out: Any


def dot(left, right, left_dim, right_dim):
    return lax.dot_general(left, right, (((left_dim,), (right_dim,)), ((), ())), preferred_element_type=F32)


def norm_parts(value):
    center = jnp.mean(value, axis=-1, keepdims=True)
    centered = value - center
    rate = lax.rsqrt(jnp.mean(centered * centered, axis=-1, keepdims=True) + EPSILON)
    return centered * rate, rate


def norm_back(grad, normal, rate, gain):
    scaled = grad * gain
    first = jnp.mean(scaled, axis=-1, keepdims=True)
    second = jnp.mean(scaled * normal, axis=-1, keepdims=True)
    gain_grad = jnp.sum(grad * normal, axis=0)
    bias_grad = jnp.sum(grad, axis=0)
    return rate * (scaled - first - normal * second), gain_grad, bias_grad


def heads_of(flat, sequences):
    return flat.reshape(sequences, flat.shape[0] // sequences, HEADS, HEAD_DIM)


def layer_fore(hidden_in, w, lengths):
    sequences = lengths.shape[0]
    model = hidden_in.shape[1]
    hidden = hidden_in.astype(F32)
    n1, r1 = norm_parts(hidden)
    a = (n1 * w.norm_gain + w.norm_bias).astype(BF)
    mixed = dot(a, w.joint_weight, 1, 0)
    q = ((mixed[:, :model] + w.joint_bias[:model]) * QUERY_SCALE).astype(BF)
    k = mixed[:, model : 2 * model].astype(BF)
    v = (mixed[:, 2 * model :] + w.joint_bias[model:]).astype(BF)
    qh, kh, vh = heads_of(q, sequences), heads_of(k, sequences), heads_of(v, sequences)
    scores = jnp.einsum("bqhd,bkhd->bhqk", qh, kh, preferred_element_type=F32)
    slots = scores.shape[-1]
    query_slot = lax.broadcasted_iota(jnp.int32, (sequences, slots, slots), 1)
    key_slot = lax.broadcasted_iota(jnp.int32, (sequences, slots, slots), 2)
    seen = (key_slot <= query_slot) & (key_slot < lengths[:, None, None])
    scores = jnp.where(seen[:, None], scores, MASKED)
    exponent = jnp.exp(RELAX * (scores - jnp.max(scores, axis=-1, keepdims=True)))
    probs = exponent / jnp.sum(exponent, axis=-1, keepdims=True)
    o = jnp.einsum("bhqk,bkhd->bqhd", probs.astype(BF), vh, preferred_element_type=F32)
    o = o.reshape(hidden.shape).astype(BF)
    y = dot(o, w.output_weight, 1, 0) + w.output_bias
    ny, ry = norm_parts(y)
    mid = hidden + ny * w.sandwich_gain + w.sandwich_bias
    nm, rm = norm_parts(mid)
    c = (nm * w.second_gain + w.second_bias).astype(BF)
    f = dot(c, w.expand_weight, 1, 0) + w.expand_bias
    g = jax.nn.gelu(f).astype(BF)
    e = dot(g, w.reduce_weight, 1, 0) + w.reduce_bias
    ne, re = norm_parts(e)
    out = mid + ne * w.closing_gain + w.closing_bias
    return out, Kept(n1, r1, a, qh, kh, vh, probs, o, y, ny, ry, nm, rm, c, f, g, e, ne, re, out)


def layer_back(dout, w, s, want_weights):
    sequences = s.qh.shape[0]
    de, closing_gain, closing_bias = norm_back(dout, s.ne, s.re, w.closing_gain)
    de = de.astype(BF)
    dg = dot(de, w.reduce_weight, 1, 1)
    df = jax.vjp(jax.nn.gelu, s.f)[1](dg)[0].astype(BF)
    dc = dot(df, w.expand_weight, 1, 1)
    dmid, second_gain, second_bias = norm_back(dc, s.nm, s.rm, w.second_gain)
    dmid = dmid + dout
    dy, sandwich_gain, sandwich_bias = norm_back(dmid, s.ny, s.ry, w.sandwich_gain)
    dy = dy.astype(BF)
    do = heads_of(dot(dy, w.output_weight, 1, 1).astype(BF), sequences)
    dprobs = jnp.einsum("bqhd,bkhd->bhqk", do, s.vh, preferred_element_type=F32)
    dv = jnp.einsum("bhqk,bqhd->bkhd", s.probs.astype(BF), do, preferred_element_type=F32)
    ds = RELAX * s.probs * (dprobs - jnp.sum(dprobs * s.probs, axis=-1, keepdims=True))
    ds = ds.astype(BF)
    dq = jnp.einsum("bhqk,bkhd->bqhd", ds, s.kh, preferred_element_type=F32)
    dk = jnp.einsum("bhqk,bqhd->bkhd", ds, s.qh, preferred_element_type=F32)
    flat = dout.shape
    dmixed = jnp.concatenate([dq.reshape(flat) * QUERY_SCALE, dk.reshape(flat), dv.reshape(flat)], axis=1).astype(BF)
    da = dot(dmixed, w.joint_weight, 1, 1)
    dh, norm_gain, norm_bias = norm_back(da, s.n1, s.r1, w.norm_gain)
    din = dmid + dh
    if not want_weights:
        return din, None
    model = flat[1]
    sums = jnp.sum(dmixed.astype(F32), axis=0)
    return din, Params(
        norm_gain=norm_gain,
        norm_bias=norm_bias,
        joint_weight=dot(s.a, dmixed, 0, 0),
        joint_bias=jnp.concatenate([sums[:model], sums[2 * model :]]),
        output_weight=dot(s.o, dy, 0, 0),
        output_bias=jnp.sum(dy.astype(F32), axis=0),
        sandwich_gain=sandwich_gain,
        sandwich_bias=sandwich_bias,
        second_gain=second_gain,
        second_bias=second_bias,
        expand_weight=dot(s.c, df, 0, 0),
        expand_bias=jnp.sum(df.astype(F32), axis=0),
        reduce_weight=dot(s.g, de, 0, 0),
        reduce_bias=jnp.sum(de.astype(F32), axis=0),
        closing_gain=closing_gain,
        closing_bias=closing_bias,
    )


def passed_along(block, axis, distance):
    devices = range(lax.axis_size(axis))
    route = [(i - distance, i) for i in devices if i - distance in devices]
    return lax.ppermute(block, axis, route)


def plain_local(tokens, lengths, *parameters):
    cotangent = parameters[-1]
    own = parameters[:-1]
    section = lax.axis_index("section")
    micro, rows, model = tokens.shape
    sequences = lengths.shape[1]
    slots = rows // sequences
    total_rows = micro * rows

    packed = jnp.concatenate([own[i] for i in VECTORS], axis=1)
    packed = lax.all_gather(packed, "batch", axis=0, tiled=True).astype(F32)
    w = list(own)
    start = 0
    for i in VECTORS:
        width = own[i].shape[1]
        w[i] = packed[:, start : start + width].reshape(-1)
        start += width
    for i, whole in zip(MATRICES, plain_gather([own[i] for i in MATRICES])):
        w[i] = whole
    w = Params(*w)

    flat_lengths = lengths.reshape(-1)
    seen = lax.broadcasted_iota(jnp.int32, (micro * sequences, slots), 1) < flat_lengths[:, None]
    valid = seen.astype(F32).reshape(total_rows, 1)
    source = tokens.reshape(total_rows, model)
    first_out, _ = layer_fore(source, w, flat_lengths)
    incoming = passed_along(first_out.astype(BF), "section", 1)
    out, s = layer_fore(jnp.where(section == 0, source, incoming), w, flat_lengths)
    section_out = out.astype(BF).reshape(1, micro, rows, model)
    squares = jnp.stack([jnp.sum(part * part * valid) for part in (s.y, s.e, s.out)])

    seed = cotangent.reshape(total_rows, model).astype(F32) * valid
    last_in, _ = layer_back(seed, w, s, False)
    incoming = passed_along(last_in.astype(BF), "section", -1)
    din, grads = layer_back(jnp.where(section == 1, seed, incoming.astype(F32)), w, s, True)
    section_grad = din.reshape(1, micro, rows, model)

    result = list(grads)
    for i, part in zip(MATRICES, plain_scatter([grads[i].astype(BF) for i in MATRICES])):
        result[i] = part
    devices = lax.axis_size("batch")
    small = jnp.concatenate([grads[i].reshape(devices, -1) for i in VECTORS], axis=1)
    small = lax.psum_scatter(small, "batch", scatter_dimension=0, tiled=True)
    start = 0
    for i in VECTORS:
        width = own[i].shape[1]
        result[i] = small[:, start : start + width]
        start += width
    count = jnp.sum(lengths).astype(F32)
    square_all, count_all = lax.psum((squares, count), "batch")
    magnitudes = jnp.sqrt(square_all / (count_all * model))[None]
    return (section_out, section_grad, magnitudes) + tuple(result)


def plain_gather(shards):
    return [lax.all_gather(w, "batch", axis=1, tiled=True)[0] for w in shards]


def plain_scatter(grads):
    return [lax.psum_scatter(g[None], "batch", scatter_dimension=1, tiled=True).astype(F32) for g in grads]


MESH = pl.DeviceIdType.MESH
BLOCKS = 12
VECTOR_ITEM = 12
PART = 64
SLOTS = 4
GATHER_ORDER = (VECTOR_ITEM,) + tuple(range(BLOCKS))
GATHER_CROSSED = (3, 11)
GATHER_AHEAD = 4
SIDE_LAG, REST_LAG = 2, 3
SCATTER_ORDER = (8, 9, 10, 11, 4, 5, 6, 7, 3, 0, 1, 2)
UP, DOWN, SIDE = 0, 1, 2


def when(condition, action):
    if condition is True:
        action()
    else:
        pl.when(condition)(action)


def both(first, second):
    if first is True:
        return second
    if second is True:
        return first
    return first & second


class Place:
    def __init__(self, depth):
        index = lax.axis_index("batch")
        self.s = lax.axis_index("section")
        self.depth = depth
        self.z = index // 4
        self.x = (index // 2) % 2
        self.c = index % 2

    def device(self, z, x, c):
        return (self.s, (z * 2 + x) * 2 + c)

    def shard(self, z, x, c):
        return (z * 2 + x) * 2 + c

    def me(self):
        return self.shard(self.z, self.x, self.c)

    def across(self):
        return (1 - self.s, self.me())

    def greet(self):
        z, x, c = self.z, self.x, self.c
        sem = pltpu.get_barrier_semaphore()

        def signal(device):
            pl.semaphore_signal(sem, inc=1, device_id=device, device_id_type=MESH)

        signal(self.device(z, 1 - x, c))
        signal(self.device(z, x, 1 - c))
        signal(self.across())
        pl.when(z < self.depth - 1)(lambda: signal(self.device(z + 1, x, c)))
        pl.when(z > 0)(lambda: signal(self.device(z - 1, x, c)))
        chain = (z < self.depth - 1).astype(jnp.int32) + (z > 0).astype(jnp.int32)
        pl.semaphore_wait(sem, 3 + chain)


def spot(item, shard):
    if item < 8:
        return item, pl.multiple_of(shard * PART, 16)
    return 8 + shard // 4, pl.multiple_of((shard % 4) * 4 * PART + (item - 8) * PART, 16)


def shard_view(refs, item, width):
    joint, output, expand, reduce, vectors = refs
    if item < 3:
        return joint.at[:, pl.ds(item * width, width)]
    if item == 3:
        return output
    if item < 8:
        return expand.at[:, pl.ds((item - 4) * width, width)]
    if item < VECTOR_ITEM:
        return reduce.at[pl.ds((item - 8) * PART, PART)]
    return vectors


class Gather:
    def __init__(self, place, own, store, vectors, sems):
        self.p, self.own, self.store, self.vectors = place, own, store, vectors
        self.send, self.share, self.recv, self.local = sems
        self.sent = []

    def at(self, item, shard):
        if item == VECTOR_ITEM:
            return self.vectors.at[shard]
        block, row = spot(item, shard)
        return self.store.at[block, pl.ds(row, PART)]

    def copy(self, item, shard, way, first=False):
        p = self.p
        target = self.at(item, shard)
        source = shard_view(self.own, item, self.store.shape[2]) if first else target
        recv = self.recv.at[item, shard]
        if way is None:
            send, device = self.share.at[item, shard // 2], p.device(p.z, p.x, 1 - p.c)
        else:
            send = self.send.at[item, shard // 2, way]
            device = (p.device(p.z + 1, p.x, p.c), p.device(p.z - 1, p.x, p.c), p.device(p.z, 1 - p.x, p.c))[way]
        return pltpu.make_async_remote_copy(source, target, send, recv, device_id=device, device_id_type=MESH)

    def go(self, item, shard, way, condition, first=False):
        self.sent.append((item, shard, way, condition, first))
        when(condition, lambda: self.copy(item, shard, way, first).start())

    def arrived(self, item, shard):
        self.copy(item, shard, None).wait_recv()

    def keep_own(self):
        me = self.p.me()
        copies = [
            pltpu.make_async_copy(shard_view(self.own, item, self.store.shape[2]), self.at(item, me), self.local.at[item])
            for item in range(BLOCKS + 1)
        ]
        for copy in copies:
            copy.start()
        return copies

    def own_sends(self, item):
        p = self.p
        self.go(item, p.me(), UP, p.z < p.depth - 1, True)
        self.go(item, p.me(), DOWN, p.z > 0, True)
        self.go(item, p.me(), SIDE, True, True)
        self.go(item, p.me(), None, True, True)

    def chain_round(self, item, hop):
        p = self.p
        crossed = item in GATHER_CROSSED
        for x in (p.x, 1 - p.x) if crossed else (p.x,):
            for origin, present, way, onward in (
                (p.z - hop, p.z >= hop, UP, p.z < p.depth - 1),
                (p.z + hop, p.z + hop < p.depth, DOWN, p.z > 0),
            ):
                shard = p.shard(origin, x, p.c)
                when(present, lambda: self.arrived(item, shard))
                self.go(item, shard, way, both(present, onward))
                if not crossed:
                    self.go(item, shard, SIDE, present)
                self.go(item, shard, None, present)

    def side_own(self, item):
        p = self.p
        shard = p.shard(p.z, 1 - p.x, p.c)
        self.arrived(item, shard)
        if item in GATHER_CROSSED:
            self.go(item, shard, UP, p.z < p.depth - 1)
            self.go(item, shard, DOWN, p.z > 0)
        self.go(item, shard, None, True)

    def side_round(self, item, hop):
        p = self.p
        if item in GATHER_CROSSED:
            return
        for origin, present in ((p.z - hop, p.z >= hop), (p.z + hop, p.z + hop < p.depth)):
            shard = p.shard(origin, 1 - p.x, p.c)
            when(present, lambda: self.arrived(item, shard))
            self.go(item, shard, None, present)

    def rest(self, item):
        p = self.p
        for z in range(p.depth):
            for x in range(2):
                self.arrived(item, p.shard(z, x, 1 - p.c))

    def drain(self):
        for item, shard, way, condition, first in self.sent:
            when(condition, lambda: self.copy(item, shard, way, first).wait_send())


def run_gather(gather, ready):
    depth, count = gather.p.depth, len(GATHER_ORDER)
    kept = gather.keep_own()
    for item in GATHER_ORDER[:GATHER_AHEAD]:
        gather.own_sends(item)

    def sides(item):
        for hop in range(1, depth):
            gather.side_round(item, hop)

    def finish(item):
        gather.rest(item)
        kept[item].wait()
        ready(item)

    for place, item in enumerate(GATHER_ORDER):
        if item in GATHER_CROSSED:
            gather.side_own(item)
        for hop in range(1, depth):
            gather.chain_round(item, hop)
            if hop == 1:
                if place + GATHER_AHEAD < count:
                    gather.own_sends(GATHER_ORDER[place + GATHER_AHEAD])
                if item not in GATHER_CROSSED:
                    gather.side_own(item)
        if place >= SIDE_LAG:
            sides(GATHER_ORDER[place - SIDE_LAG])
        if place >= REST_LAG:
            finish(GATHER_ORDER[place - REST_LAG])
    for item in GATHER_ORDER[count - SIDE_LAG :]:
        sides(item)
    for item in GATHER_ORDER[count - REST_LAG :]:
        finish(item)


def gather_sems(depth):
    kind, items = pltpu.SemaphoreType.DMA, BLOCKS + 1
    return [kind((items, 2 * depth, 3)), kind((items, 2 * depth)), kind((items, 4 * depth)), kind((items,))]


def total(*refs):
    value = refs[0][...].astype(F32)
    for ref in refs[1:]:
        value = value + ref[...].astype(F32)
    return value


class Scatter:
    def __init__(self, place, part, count, slots, buffers, outs, sems):
        self.p, self.part, self.count, self.slots, self.outs = place, part, count, slots, outs
        self.core_in, self.side_in, self.chain_in = buffers
        (self.core_send, self.core_recv, self.side_send, self.side_recv, self.chain_send, self.chain_recv,
         self.core_free, self.side_free, self.chain_free) = sems
        depth = place.depth
        self.origins = [q for pair in zip(range(depth - 1, -1, -1), range(depth)) for q in pair][:depth]

    def mine(self, step, z, x, c):
        return self.part(step, self.p.shard(z, x, c))

    def core_copy(self, step, z, x):
        p, slot = self.p, step % self.slots
        return pltpu.make_async_remote_copy(
            self.mine(step, z, x, 1 - p.c), self.core_in.at[slot, z * 2 + x],
            self.core_send.at[slot, z * 2 + x], self.core_recv.at[slot, z * 2 + x],
            device_id=p.device(p.z, p.x, 1 - p.c), device_id_type=MESH)

    def side_copy(self, step, z):
        p, slot = self.p, step % self.slots
        return pltpu.make_async_remote_copy(
            self.mine(step, z, 1 - p.x, p.c), self.side_in.at[slot, z],
            self.side_send.at[slot, z], self.side_recv.at[slot, z],
            device_id=p.device(p.z, 1 - p.x, p.c), device_id_type=MESH)

    def chain_copy(self, step, z, up):
        p, slot = self.p, step % self.slots
        return pltpu.make_async_remote_copy(
            self.mine(step, z, p.x, p.c), self.chain_in.at[slot, 1 - up, z],
            self.chain_send.at[slot, 1 - up, z], self.chain_recv.at[slot, 1 - up, z],
            device_id=p.device(p.z + 2 * up - 1, p.x, p.c), device_id_type=MESH)

    def core_stage(self, step):
        if step >= self.slots:
            for z in self.origins:
                for x in range(2):
                    self.core_copy(step - self.slots, z, x).wait_send()
            pl.semaphore_wait(self.core_free, 1)
        for z in self.origins:
            for x in range(2):
                self.core_copy(step, z, x).start()

    def from_core(self, step, z, x):
        self.core_copy(step, z, x).wait_recv()
        return self.core_in.at[step % self.slots, z * 2 + x]

    def side_stage(self, step):
        p = self.p
        if step >= self.slots:
            for z in self.origins:
                self.side_copy(step - self.slots, z).wait_send()
            pl.semaphore_wait(self.side_free, 1)
        for z in self.origins:
            twin = self.from_core(step, z, 1 - p.x)
            mine = self.mine(step, z, 1 - p.x, p.c)
            mine[...] = total(mine, twin).astype(mine.dtype)
            self.side_copy(step, z).start()

    def chain_stage(self, step):
        p, slot, last = self.p, step % self.slots, self.p.depth - 1
        if step >= self.slots:
            for z in self.origins:
                up = (p.z < z).astype(jnp.int32)
                pl.when(p.z != z)(lambda: self.chain_copy(step - self.slots, z, up).wait_send())
            pl.when(p.z < last)(lambda: pl.semaphore_wait(self.chain_free.at[0], 1))
            pl.when(p.z > 0)(lambda: pl.semaphore_wait(self.chain_free.at[1], 1))
        for z in self.origins:
            up = (p.z < z).astype(jnp.int32)
            fed = ((p.z < z) & (p.z > 0)) | ((p.z > z) & (p.z < last))

            @pl.when(p.z != z)
            def _():
                twin = self.from_core(step, z, p.x)
                mine = self.mine(step, z, p.x, p.c)
                self.side_copy(step, z).wait_recv()
                side = self.side_in.at[slot, z]

                @pl.when(fed)
                def _():
                    self.chain_copy(step, z, up).wait_recv()
                    mine[...] = total(mine, twin, side, self.chain_in.at[slot, 1 - up, z]).astype(mine.dtype)

                @pl.when(jnp.logical_not(fed))
                def _():
                    mine[...] = total(mine, twin, side).astype(mine.dtype)

                self.chain_copy(step, z, up).start()

    def own_stage(self, step):
        p, slot, last = self.p, step % self.slots, self.p.depth - 1
        twin = self.from_core(step, p.z, p.x)
        self.side_copy(step, p.z).wait_recv()
        parts = [self.mine(step, p.z, p.x, p.c), twin, self.side_in.at[slot, p.z]]
        pl.when(p.z > 0)(lambda: self.chain_copy(step, p.z, 1).wait_recv())
        pl.when(p.z < last)(lambda: self.chain_copy(step, p.z, 0).wait_recv())
        below, above = self.chain_in.at[slot, 0, p.z], self.chain_in.at[slot, 1, p.z]
        out = self.outs[step]

        def put(*refs):
            out[...] = total(*refs)

        pl.when(p.z == 0)(lambda: put(*parts, above))
        pl.when(p.z == last)(lambda: put(*parts, below))
        pl.when((p.z > 0) & (p.z < last))(lambda: put(*parts, below, above))
        if step + self.slots < self.count:
            def signal(sem, device):
                pl.semaphore_signal(sem, inc=1, device_id=device, device_id_type=MESH)

            signal(self.core_free, p.device(p.z, p.x, 1 - p.c))
            signal(self.side_free, p.device(p.z, 1 - p.x, p.c))
            pl.when(p.z > 0)(lambda: signal(self.chain_free.at[0], p.device(p.z - 1, p.x, p.c)))
            pl.when(p.z < last)(lambda: signal(self.chain_free.at[1], p.device(p.z + 1, p.x, p.c)))

    def drain(self):
        p = self.p
        for step in range(self.count - self.slots, self.count):
            for z in self.origins:
                for x in range(2):
                    self.core_copy(step, z, x).wait_send()
                self.side_copy(step, z).wait_send()
                up = (p.z < z).astype(jnp.int32)
                pl.when(p.z != z)(lambda: self.chain_copy(step, z, up).wait_send())


def run_scatter(scatter, vector_scatter, ready, done):
    for tick in range(BLOCKS + 4):
        if tick < BLOCKS:
            ready(tick)
        if tick >= 4:
            scatter.own_stage(tick - 4)
            done(tick - 4)
        if tick < BLOCKS:
            scatter.core_stage(tick)
        if 1 <= tick <= BLOCKS:
            scatter.side_stage(tick - 1)
        if 2 <= tick < BLOCKS + 2:
            scatter.chain_stage(tick - 2)
        if tick == BLOCKS - 1:
            vector_scatter.core_stage(0)
        if tick == BLOCKS:
            vector_scatter.side_stage(0)
        if tick == BLOCKS + 1:
            vector_scatter.chain_stage(0)
    vector_scatter.own_stage(0)
    scatter.drain()
    vector_scatter.drain()


def scatter_scratch(depth, slots, rows, width, dtype):
    dma, plain = pltpu.SemaphoreType.DMA, pltpu.SemaphoreType.REGULAR
    return [
        pltpu.VMEM((slots, 2 * depth, rows, width), dtype),
        pltpu.VMEM((slots, depth, rows, width), dtype),
        pltpu.VMEM((slots, 2, depth, rows, width), dtype),
        dma((slots, 2 * depth)), dma((slots, 2 * depth)), dma((slots, depth)), dma((slots, depth)),
        dma((slots, 2, depth)), dma((slots, 2, depth)), plain, plain, plain((2,)),
    ]


(NORM_GAIN, NORM_BIAS, OUTPUT_BIAS, SANDWICH_GAIN, SANDWICH_BIAS, SECOND_GAIN, SECOND_BIAS, REDUCE_BIAS,
 CLOSING_GAIN, CLOSING_BIAS, QUERY_BIAS, VALUE_BIAS, EXPAND_BIAS) = range(13)
NARROW = 10
VECTOR_ROWS = 16
FIGURES = 13
LANES = 128
TILE = 256
CHUNK = 64
CURVE = math.sqrt(2.0 / math.pi)
BEND = 0.044715


class Work(NamedTuple):
    vec: Any
    dvec: Any
    h: Any
    a: Any
    q: Any
    k: Any
    v: Any
    p: Any
    o: Any
    n_h: Any
    r_h: Any
    n_y: Any
    r_y: Any
    n_m: Any
    r_m: Any
    n_e: Any
    r_e: Any
    mid: Any
    c: Any
    g: Any
    slope: Any
    de: Any
    dy: Any
    do: Any
    din: Any
    sums: Any


def mxu(left, right, left_dim, right_dim):
    return lax.dot_general(left, right, (((left_dim,), (right_dim,)), ((), ())), preferred_element_type=F32)


def mean_of(value):
    return jnp.mean(value, axis=-1, keepdims=True)


def norm_of(value):
    centered = value - mean_of(value)
    rate = lax.rsqrt(mean_of(centered * centered) + EPSILON)
    return centered * rate, rate


def norm_pull(grad, normal, rate, gain):
    scaled = grad * gain
    return rate * (scaled - mean_of(scaled) - normal * mean_of(scaled * normal))


def column_sum(value):
    return jnp.sum(value, axis=0, keepdims=True)


class Layer:
    def __init__(self, work, store, lengths):
        self.w, self.store, self.lengths = work, store, lengths
        self.tokens, self.width = work.h.shape
        self.sequences = lengths.shape[0]
        self.slots = self.tokens // self.sequences

    def row(self, index):
        return self.w.vec[index : index + 1, :]

    def add(self, index, value):
        self.w.dvec[index : index + 1, :] += value

    def chunks(self, body, first=0, last=None):
        last = self.tokens if last is None else last

        def step(i, carry):
            body(pl.ds(pl.multiple_of(i * CHUNK, CHUNK), CHUNK), i)
            return carry

        lax.fori_loop(first // CHUNK, last // CHUNK, step, 0)

    def tiles(self, body):
        def step(i, carry):
            body(pl.ds(pl.multiple_of(i * TILE, TILE), TILE))
            return carry

        lax.fori_loop(0, self.width // TILE, step, 0, unroll=True)

    def valid(self, i):
        per = self.slots // CHUNK
        slot = (i % per) * CHUNK + lax.broadcasted_iota(jnp.int32, (CHUNK, 1), 0)
        return jnp.where(slot < self.lengths[i // per], 1.0, 0.0)


    def fore_start(self, source, first=0, last=None):
        w = self.w

        def body(rows, i):
            h = source[rows, :]
            w.h[rows, :] = h
            normal, rate = norm_of(h.astype(F32))
            w.n_h[rows, :] = normal
            w.r_h[rows, :] = rate
            w.a[rows, :] = (normal * self.row(NORM_GAIN) + self.row(NORM_BIAS)).astype(BF)

        self.chunks(body, first, last)

    def part(self, index):
        return pl.ds(index * self.slots, self.slots)

    def fore_joint(self, block, rows):
        w = self.w
        bias = (QUERY_BIAS, None, VALUE_BIAS)[block]
        target = (w.q, w.k, w.v)[block]

        def body(tile):
            mixed = mxu(w.a[rows, :], self.store[block, :, tile], 1, 0)
            if bias is not None:
                mixed = mixed + w.vec[bias : bias + 1, tile]
            if block == 0:
                mixed = mixed * QUERY_SCALE
            target[rows, tile] = mixed.astype(BF)

        self.tiles(body)

    def pairs(self, sequence, body):
        count = self.width // LANES
        rows, length = self.part(sequence), self.lengths[sequence]

        def step(i, carry):
            body(rows, pl.ds(pl.multiple_of(i * LANES, LANES), LANES), sequence * count + i, length)
            return carry

        lax.fori_loop(0, count, step, 0, unroll=8)

    def split(self, value):
        low = lax.broadcasted_iota(jnp.int32, value.shape, 1) < HEAD_DIM
        zero = jnp.zeros_like(value)
        return jnp.concatenate([jnp.where(low, value, zero), jnp.where(low, zero, value)], axis=0)

    def fore_attention(self, sequence):
        w, slots = self.w, self.slots

        def body(rows, lanes, i, length):
            scores = mxu(self.split(w.q[rows, lanes]), w.k[rows, lanes], 1, 1)
            query = lax.broadcasted_iota(jnp.int32, (2 * slots, slots), 0) % slots
            key = lax.broadcasted_iota(jnp.int32, (2 * slots, slots), 1)
            scores = jnp.where((key <= query) & (key < length), scores, MASKED)
            weight = jnp.exp(RELAX * (scores - jnp.max(scores, axis=-1, keepdims=True)))
            probs = (weight / jnp.sum(weight, axis=-1, keepdims=True)).astype(BF)
            w.p[i] = probs
            wide = jnp.concatenate([probs[:slots], probs[slots:]], axis=1)
            w.o[rows, lanes] = mxu(wide, self.split(w.v[rows, lanes]), 1, 0).astype(BF)

        self.pairs(sequence, body)

    def fore_output(self):
        w = self.w

        def body(tile):
            w.n_y[:, tile] = mxu(w.o[...], self.store[3, :, tile], 1, 0) + w.vec[OUTPUT_BIAS : OUTPUT_BIAS + 1, tile]

        self.tiles(body)

        def middle(rows, i):
            y = w.n_y[rows, :]
            w.sums[0:1, :] += column_sum(y * y * self.valid(i))
            normal, rate = norm_of(y)
            w.n_y[rows, :] = normal
            w.r_y[rows, :] = rate
            mid = w.h[rows, :].astype(F32) + (normal * self.row(SANDWICH_GAIN) + self.row(SANDWICH_BIAS))
            w.mid[rows, :] = mid
            normal, rate = norm_of(mid)
            w.n_m[rows, :] = normal
            w.r_m[rows, :] = rate
            w.c[rows, :] = (normal * self.row(SECOND_GAIN) + self.row(SECOND_BIAS)).astype(BF)

        self.chunks(middle)

    def fore_expand(self, block):
        w = self.w

        def body(tile):
            f = mxu(w.c[...], self.store[4 + block, :, tile], 1, 0)
            f = f + w.vec[EXPAND_BIAS + block : EXPAND_BIAS + block + 1, tile]
            square = f * f
            bent = jnp.tanh(CURVE * f * (1.0 + BEND * square))
            half = 0.5 * (1.0 + bent)
            w.g[block, :, tile] = (f * half).astype(BF)
            slope = half + 0.5 * f * (1.0 - bent * bent) * (CURVE * (1.0 + 3.0 * BEND * square))
            w.slope[block, :, tile] = slope.astype(BF)

        self.tiles(body)

    def fore_reduce(self, rows):
        w = self.w

        def body(tile):
            e = mxu(w.g[0, rows, :], self.store[8, :, tile], 1, 0)
            for block in range(1, 4):
                e = e + mxu(w.g[block, rows, :], self.store[8 + block, :, tile], 1, 0)
            w.n_e[rows, tile] = e + w.vec[REDUCE_BIAS : REDUCE_BIAS + 1, tile]

        self.tiles(body)

    def fore_end(self, target, first=0, last=None):
        w = self.w

        def body(rows, i):
            e = w.n_e[rows, :]
            valid = self.valid(i)
            w.sums[1:2, :] += column_sum(e * e * valid)
            normal, rate = norm_of(e)
            w.n_e[rows, :] = normal
            w.r_e[rows, :] = rate
            out = w.mid[rows, :] + (normal * self.row(CLOSING_GAIN) + self.row(CLOSING_BIAS))
            w.sums[2:3, :] += column_sum(out * out * valid)
            target[rows, :] = out.astype(BF)

        self.chunks(body, first, last)


    def back_start(self, seed, masked, first=0, last=None):
        w = self.w

        def body(rows, i):
            dout = seed[rows, :].astype(F32)
            if masked:
                dout = dout * self.valid(i)
            w.din[rows, :] = dout
            normal = w.n_e[rows, :]
            self.add(CLOSING_GAIN, column_sum(dout * normal))
            self.add(CLOSING_BIAS, column_sum(dout))
            de = norm_pull(dout, normal, w.r_e[rows, :], self.row(CLOSING_GAIN)).astype(BF)
            w.de[rows, :] = de
            self.add(REDUCE_BIAS, column_sum(de.astype(F32)))

        self.chunks(body, first, last)

    def back_reduce(self, block, rows):
        w = self.w

        def body(tile):
            dg = mxu(w.de[rows, :], self.store[8 + block, tile, :], 1, 1)
            df = (dg * w.slope[block, rows, tile].astype(F32)).astype(BF)
            w.slope[block, rows, tile] = df
            w.dvec[EXPAND_BIAS + block : EXPAND_BIAS + block + 1, tile] += column_sum(df.astype(F32))

        self.tiles(body)

    def back_expand(self):
        w = self.w

        def body(tile):
            dc = mxu(w.slope[0], self.store[4, tile, :], 1, 1)
            for block in range(1, 4):
                dc = dc + mxu(w.slope[block], self.store[4 + block, tile, :], 1, 1)
            w.mid[:, tile] = dc

        self.tiles(body)

        def middle(rows, i):
            dc = w.mid[rows, :]
            normal = w.n_m[rows, :]
            self.add(SECOND_GAIN, column_sum(dc * normal))
            self.add(SECOND_BIAS, column_sum(dc))
            dmid = w.din[rows, :] + norm_pull(dc, normal, w.r_m[rows, :], self.row(SECOND_GAIN))
            w.din[rows, :] = dmid
            normal = w.n_y[rows, :]
            self.add(SANDWICH_GAIN, column_sum(dmid * normal))
            self.add(SANDWICH_BIAS, column_sum(dmid))
            dy = norm_pull(dmid, normal, w.r_y[rows, :], self.row(SANDWICH_GAIN)).astype(BF)
            w.dy[rows, :] = dy
            self.add(OUTPUT_BIAS, column_sum(dy.astype(F32)))

        self.chunks(middle)

    def back_output(self):
        w = self.w

        def body(tile):
            w.do[:, tile] = mxu(w.dy[...], self.store[3, tile, :], 1, 1).astype(BF)

        self.tiles(body)

    def back_attention(self, sequence):
        w, slots = self.w, self.slots

        def body(rows, lanes, i, length):
            grad = self.split(w.do[rows, lanes])
            probs = w.p[i]
            value = probs.astype(F32)
            dprobs = mxu(grad, w.v[rows, lanes], 1, 1)
            inner = jnp.sum(dprobs * value, axis=-1, keepdims=True)
            ds = (RELAX * value * (dprobs - inner)).astype(BF)
            wide = jnp.concatenate([ds[:slots], ds[slots:]], axis=1)
            dv = mxu(probs, grad, 0, 0)
            dk = mxu(ds, self.split(w.q[rows, lanes]), 0, 0)
            dq = mxu(wide, self.split(w.k[rows, lanes]), 1, 0) * QUERY_SCALE
            w.q[rows, lanes] = dq.astype(BF)
            w.k[rows, lanes] = dk.astype(BF)
            w.v[rows, lanes] = dv.astype(BF)

        self.pairs(sequence, body)

    def back_joint(self, rows):
        w = self.w

        def body(tile):
            da = mxu(w.q[rows, :], self.store[0, tile, :], 1, 1)
            da = da + mxu(w.k[rows, :], self.store[1, tile, :], 1, 1)
            w.mid[rows, tile] = da + mxu(w.v[rows, :], self.store[2, tile, :], 1, 1)

        self.tiles(body)

    def back_end(self, target, first=0, last=None):
        w = self.w

        def body(rows, i):
            da = w.mid[rows, :]
            normal = w.n_h[rows, :]
            self.add(NORM_GAIN, column_sum(da * normal))
            self.add(NORM_BIAS, column_sum(da))
            self.add(QUERY_BIAS, column_sum(w.q[rows, :].astype(F32)))
            self.add(VALUE_BIAS, column_sum(w.v[rows, :].astype(F32)))
            din = w.din[rows, :] + norm_pull(da, normal, w.r_h[rows, :], self.row(NORM_GAIN))
            w.din[rows, :] = din
            target[rows, :] = din.astype(BF)

        self.chunks(body, first, last)


    def weight_grad(self, block):
        w = self.w
        if block < 3:
            left, right = w.a, (w.q, w.k, w.v)[block]
        elif block == 3:
            left, right = w.o, w.dy
        elif block < 8:
            left, right = w.c, w.slope.at[block - 4]
        else:
            left, right = w.g.at[block - 8], w.de

        def body(tile):
            self.store[block, tile, :] = mxu(left[:, tile], right[...], 0, 0).astype(BF)

        self.tiles(body)


def unfold_vectors(tiles, vec, count):
    for pair in range(count // 2):
        vec[:NARROW, pair * LANES : (pair + 1) * LANES] = tiles[2 * pair, :NARROW, :] + tiles[2 * pair + 1, :NARROW, :]
    half, quarter = count // 2, count // 4
    for shard in range(count):
        row, lane = QUERY_BIAS + shard // half, (shard % half) * LANES
        vec[row : row + 1, lane : lane + LANES] = tiles[shard, NARROW : NARROW + 1, :]
        for part in range(2):
            row, lane = EXPAND_BIAS + shard // quarter, ((shard % quarter) * 2 + part) * LANES
            source = NARROW + 1 + part
            vec[row : row + 1, lane : lane + LANES] = tiles[shard, source : source + 1, :]


def fold_vectors(tiles, dvec, figures, count):
    half, quarter = count // 2, count // 4
    for shard in range(count):
        pair = shard // 2
        tiles[shard, :NARROW, :] = dvec[:NARROW, pair * LANES : (pair + 1) * LANES]
        row, lane = QUERY_BIAS + shard // half, (shard % half) * LANES
        tiles[shard, NARROW : NARROW + 1, :] = dvec[row : row + 1, lane : lane + LANES]
        for part in range(2):
            row, lane = EXPAND_BIAS + shard // quarter, ((shard % quarter) * 2 + part) * LANES
            target = NARROW + 1 + part
            tiles[shard, target : target + 1, :] = dvec[row : row + 1, lane : lane + LANES]
        tiles[shard, FIGURES : FIGURES + 1, :] = figures
        tiles[shard, FIGURES + 1 :, :] = jnp.zeros((VECTOR_ROWS - FIGURES - 1, LANES), F32)


def figures_of(sums, lengths):
    lane = lax.broadcasted_iota(jnp.int32, (1, LANES), 1)
    row = jnp.zeros((1, LANES), F32)
    for i in range(3):
        row = jnp.where(lane == i, jnp.sum(sums[i : i + 1, :], axis=1, keepdims=True), row)
    seen = lengths[0]
    for i in range(1, lengths.shape[0]):
        seen = seen + lengths[i]
    return jnp.where(lane == 3, seen.astype(F32), row)


def relay_kernel(depth, lengths, tokens, cotangent, joint, output, expand, reduce, vectors,
                 section_out, section_grad, joint_out, output_out, expand_out, reduce_out, vector_out,
                 store, tiles, vec, dvec, sums, h, a, q, k, v, p, o, n_h, r_h, n_y, r_y, n_m, r_m, n_e, r_e,
                 mid, c, g, slope, de, dy, do, din, result, staged, incoming, pass_sems, out_sems, *rest):
    place = Place(depth)
    width = store.shape[2]
    count = 4 * depth
    gather_parts, rest = rest[:4], rest[4:]
    scatter_parts, vector_parts = rest[:12], rest[12:]
    work = Work(vec, dvec, h, a, q, k, v, p, o, n_h, r_h, n_y, r_y, n_m, r_m, n_e, r_e, mid, c, g, slope,
                de, dy, do, din, sums)
    layer = Layer(work, store, lengths)
    slots, parts = layer.slots, range(layer.sequences)
    whole = pl.ds(0, layer.tokens)
    first, second = place.s == 0, place.s == 1

    def passing(source, part, way):
        rows = pl.ds(part * slots, slots)
        return pltpu.make_async_remote_copy(
            source.at[rows], incoming.at[rows], pass_sems.at[way, 0, part], pass_sems.at[way, 1, part],
            device_id=place.across(), device_id_type=MESH)

    def forward(part):
        return passing(result, part, 0)

    def backward(part):
        return passing(do, part, 1)

    out_copy = pltpu.make_async_copy(result, section_out, out_sems.at[BLOCKS])
    grad_copy = pltpu.make_async_copy(din, section_grad, out_sems.at[BLOCKS + 1])

    place.greet()
    dvec[...] = jnp.zeros_like(dvec)
    sums[...] = jnp.zeros_like(sums)

    def fore_first(part, source):
        layer.fore_start(source, part * slots, (part + 1) * slots)

    def fore_last(part):
        layer.fore_reduce(layer.part(part))
        layer.fore_end(result, part * slots, (part + 1) * slots)

    def back_first(part, seed, masked):
        layer.back_start(seed, masked, part * slots, (part + 1) * slots)
        for block in range(4):
            layer.back_reduce(block, layer.part(part))

    def back_last(part):
        layer.back_attention(part)
        layer.back_joint(layer.part(part))
        layer.back_end(do, part * slots, (part + 1) * slots)

    def ready(item):
        if item == VECTOR_ITEM:
            unfold_vectors(tiles, vec, count)

        @pl.when(first)
        def _():
            if item == VECTOR_ITEM:
                layer.fore_start(tokens)
            elif item < 3:
                layer.fore_joint(item, whole)
                if item == 2:
                    for part in parts:
                        layer.fore_attention(part)
            elif item == 3:
                layer.fore_output()
            elif item < 8:
                layer.fore_expand(item - 4)
            elif item == BLOCKS - 1:
                for part in parts:
                    fore_last(part)
                    forward(part).start()

    gather = Gather(place, (joint, output, expand, reduce, vectors), store, tiles, gather_parts)
    run_gather(gather, ready)
    gather.drain()

    @pl.when(second)
    def _():
        for part in parts:
            forward(part).wait_recv()
            fore_first(part, incoming)
            for block in range(3):
                layer.fore_joint(block, layer.part(part))
            layer.fore_attention(part)
        layer.fore_output()
        for block in range(4):
            layer.fore_expand(block)
        layer.fore_reduce(whole)
        layer.fore_end(result)
        layer.back_start(cotangent, True)
        for block in range(4):
            layer.back_reduce(block, whole)
        layer.back_expand()
        layer.back_output()
        for part in parts:
            back_last(part)
            backward(part).start()

    out_copy.start()

    @pl.when(first)
    def _():
        for part in parts:
            backward(part).wait_recv()
            back_first(part, incoming, False)

    def fill(step):
        block = SCATTER_ORDER[step]

        @pl.when(first)
        def _():
            if step == 4:
                layer.back_expand()
            elif block == 3:
                layer.back_output()
            elif step == 9:
                for part in parts:
                    back_last(part)

        if step == 0:
            for part in range(4):
                layer.weight_grad(8 + part)
        elif step >= 4:
            layer.weight_grad(block)
        if step == 9:
            grad_copy.start()
        if step == BLOCKS - 1:
            fold_vectors(tiles, dvec, figures_of(sums, lengths), count)

    def part_of(step, shard):
        block, row = spot(SCATTER_ORDER[step], shard)
        return store.at[block, pl.ds(row, PART)]

    targets = [shard_view((joint_out, output_out, expand_out, reduce_out, None), item, width) for item in SCATTER_ORDER]
    outs = [staged.at[step] for step in range(BLOCKS)]
    copies = [pltpu.make_async_copy(outs[step], targets[step], out_sems.at[step]) for step in range(BLOCKS)]
    scatter = Scatter(place, part_of, BLOCKS, SLOTS, scatter_parts[:3], outs, scatter_parts[3:])
    vector_scatter = Scatter(place, lambda step, shard: tiles.at[shard], 1, 1, vector_parts[:3], [vector_out], vector_parts[3:])
    run_scatter(scatter, vector_scatter, fill, lambda step: copies[step].start())

    @pl.when(first)
    def _():
        for part in parts:
            forward(part).wait_send()

    @pl.when(second)
    def _():
        for part in parts:
            backward(part).wait_send()

    for copy in copies + [out_copy, grad_copy]:
        copy.wait()


def finish_kernel(core, tile, *refs):
    sources, targets, rest = refs[:6], refs[6:12], refs[12:]
    magnitudes, joint_bias, expand_bias, narrow = rest[0], rest[1], rest[2], rest[3:-7]
    held, sems = rest[-7:-1], rest[-1]
    loads = [pltpu.make_async_copy(source, buffer, sems.at[0, i]) for i, (source, buffer) in enumerate(zip(sources, held))]
    copies = [pltpu.make_async_copy(buffer, target, sems.at[1, i]) for i, (buffer, target) in enumerate(zip(held, targets))]
    for load in loads:
        load.start()
    halves = jnp.where(core[0] == 0, tile[:NARROW, :HEAD_DIM], tile[:NARROW, HEAD_DIM:])
    for i, ref in enumerate(narrow):
        ref[...] = halves[i : i + 1]
    figures = tile[FIGURES : FIGURES + 1, :]
    magnitudes[...] = jnp.sqrt(figures[:, :3] / (figures[:, 3:4] * sources[0].shape[1]))
    joint_bias[...] = tile[NARROW : NARROW + 1, :]
    for part in range(2):
        expand_bias[:, part * LANES : (part + 1) * LANES] = tile[NARROW + 1 + part : NARROW + 2 + part, :]
    for load, copy in zip(loads, copies):
        load.wait()
        copy.start()
    for copy in copies:
        copy.wait()


def relay_local(depth, tokens, lengths, *parameters):
    cotangent, own = parameters[-1], Params(*parameters[:-1])
    micro, rows, width = tokens.shape
    sequences = lengths.shape[1] * micro
    count = micro * rows
    core = lax.axis_index("batch") % 2

    narrow = jnp.concatenate([
        own.norm_gain, own.norm_bias, own.output_bias, own.sandwich_gain, own.sandwich_bias, own.second_gain,
        own.second_bias, own.reduce_bias, own.closing_gain, own.closing_bias]).astype(F32)
    zero = jnp.zeros_like(narrow)
    narrow = jnp.where(core == 0, jnp.concatenate([narrow, zero], axis=1), jnp.concatenate([zero, narrow], axis=1))
    vectors = jnp.concatenate([
        narrow, own.joint_bias.astype(F32), own.expand_bias.astype(F32).reshape(2, LANES),
        jnp.zeros((VECTOR_ROWS - NARROW - 3, LANES), F32)])

    low, high, rate = (pltpu.VMEM((count, width), BF), pltpu.VMEM((count, width), F32), pltpu.VMEM((count, 1), F32))
    wide = pltpu.VMEM((4, count, width), BF)
    shards = 4 * depth
    dma = pltpu.SemaphoreType.DMA
    vmem, anywhere = pl.BlockSpec(memory_space=pltpu.VMEM), pl.BlockSpec(memory_space=pl.ANY)
    shapes = [
        jax.ShapeDtypeStruct((count, width), BF), jax.ShapeDtypeStruct((count, width), F32),
        jax.ShapeDtypeStruct((PART, 3 * width), F32), jax.ShapeDtypeStruct((PART, width), F32),
        jax.ShapeDtypeStruct((PART, 4 * width), F32), jax.ShapeDtypeStruct((4 * PART, width), F32)]
    slots = rows // lengths.shape[1]
    results = pl.pallas_call(
        functools.partial(relay_kernel, depth),
        out_shape=shapes + [jax.ShapeDtypeStruct((VECTOR_ROWS, LANES), F32)],
        in_specs=[pl.BlockSpec(memory_space=pltpu.SMEM), vmem, vmem] + [anywhere] * 5,
        out_specs=[anywhere] * 6 + [vmem],
        scratch_shapes=[
            pltpu.VMEM((BLOCKS, width, width), BF), pltpu.VMEM((shards, VECTOR_ROWS, LANES), F32),
            pltpu.VMEM((VECTOR_ROWS, width), F32), pltpu.VMEM((VECTOR_ROWS, width), F32), pltpu.VMEM((8, width), F32),
            low, low, low, low, low, pltpu.VMEM((sequences * width // LANES, 2 * slots, slots), BF), low,
            high, rate, high, rate, high, rate, high, rate,
            high, low, wide, wide, low, low, low, high, low, pltpu.VMEM((BLOCKS, PART, width), F32), low,
            dma((2, 2, sequences)), dma((BLOCKS + 2,)),
        ] + gather_sems(depth) + scatter_scratch(depth, SLOTS, PART, width, BF) + scatter_scratch(depth, 1, VECTOR_ROWS, LANES, F32),
        compiler_params=pltpu.CompilerParams(collective_id=1, has_side_effects=True, vmem_limit_bytes=VMEM_LIMIT),
        cost_estimate=pl.CostEstimate(flops=6 * count * BLOCKS * width * width, bytes_accessed=2 * BLOCKS * width * width, transcendentals=0),
        name="relay",
    )(lengths.reshape(-1), tokens.reshape(count, width), cotangent.reshape(count, width),
      own.joint_weight[0], own.output_weight[0], own.expand_weight[0], own.reduce_weight[0], vectors)

    vector = jax.ShapeDtypeStruct((1, HEAD_DIM), F32)
    small = [jax.ShapeDtypeStruct((1, 3), F32), jax.ShapeDtypeStruct((1, LANES), F32),
             jax.ShapeDtypeStruct((1, 2 * LANES), F32)] + [vector] * NARROW
    final = pl.pallas_call(
        finish_kernel,
        out_shape=shapes + small,
        in_specs=[pl.BlockSpec(memory_space=pltpu.SMEM), vmem] + [anywhere] * 6,
        out_specs=[anywhere] * 6 + [vmem] * len(small),
        scratch_shapes=[pltpu.VMEM(s.shape, s.dtype) for s in shapes] + [dma((2, 6))],
        compiler_params=pltpu.CompilerParams(vmem_limit_bytes=VMEM_LIMIT),
        name="finish",
    )(core.reshape(1), results[6], *results[:6])
    section_out, section_grad, joint, output, expand, reduce, magnitudes, joint_bias, expand_bias = final[:9]
    narrow = final[9:]
    grads = Params(
        norm_gain=narrow[NORM_GAIN], norm_bias=narrow[NORM_BIAS], joint_weight=joint[None],
        joint_bias=joint_bias, output_weight=output[None], output_bias=narrow[OUTPUT_BIAS],
        sandwich_gain=narrow[SANDWICH_GAIN], sandwich_bias=narrow[SANDWICH_BIAS], second_gain=narrow[SECOND_GAIN],
        second_bias=narrow[SECOND_BIAS], expand_weight=expand[None],
        expand_bias=expand_bias, reduce_weight=reduce[None],
        reduce_bias=narrow[REDUCE_BIAS], closing_gain=narrow[CLOSING_GAIN], closing_bias=narrow[CLOSING_BIAS])
    shape = (1, micro, rows, width)
    return (section_out.reshape(shape), section_grad.reshape(shape), magnitudes) + tuple(grads)


def solution(mesh):
    vector, matrix = P("section", "batch"), P("section", "batch", None)
    kinds = tuple(matrix if i in MATRICES else vector for i in range(16))
    rows = P(None, "batch", None)
    stacked = P("section", None, "batch", None)
    devices = mesh.shape["batch"]
    body = functools.partial(relay_local, devices // 4) if devices == 16 else plain_local
    return jax.shard_map(
        body,
        mesh=mesh,
        in_specs=(rows, P(None, "batch")) + kinds + (rows,),
        out_specs=(stacked, stacked, P("section", None)) + kinds,
        check_vma=False,
    )
```

```python
import functools
import math
from typing import Any, NamedTuple

import jax
import jax.numpy as jnp
from jax import lax
from jax.experimental import pallas as pl
from jax.experimental.pallas import tpu as pltpu
from jax.sharding import PartitionSpec as P

HEADS = 16
HEAD_DIM = 64
EPSILON = 1e-05
RELAX = 32.0
MASKED = -1000000000.0
QUERY_SCALE = 1.0 / (RELAX * math.sqrt(HEAD_DIM))

BF = jnp.bfloat16
F32 = jnp.float32
VMEM_LIMIT = 62 * 2**20

class Params(NamedTuple):
    norm_gain: Any
    norm_bias: Any
    joint_weight: Any
    joint_bias: Any
    output_weight: Any
    output_bias: Any
    sandwich_gain: Any
    sandwich_bias: Any
    second_gain: Any
    second_bias: Any
    expand_weight: Any
    expand_bias: Any
    reduce_weight: Any
    reduce_bias: Any
    closing_gain: Any
    closing_bias: Any


MATRICES = (2, 4, 10, 12)
VECTORS = tuple(i for i in range(16) if i not in MATRICES)


class Kept(NamedTuple):
    n1: Any
    r1: Any
    a: Any
    qh: Any
    kh: Any
    vh: Any
    probs: Any
    o: Any
    y: Any
    ny: Any
    ry: Any
    nm: Any
    rm: Any
    c: Any
    f: Any
    g: Any
    e: Any
    ne: Any
    re: Any
    out: Any


def dot(left, right, left_dim, right_dim):
    return lax.dot_general(left, right, (((left_dim,), (right_dim,)), ((), ())), preferred_element_type=F32)


def norm_parts(value):
    center = jnp.mean(value, axis=-1, keepdims=True)
    centered = value - center
    rate = lax.rsqrt(jnp.mean(centered * centered, axis=-1, keepdims=True) + EPSILON)
    return centered * rate, rate


def norm_back(grad, normal, rate, gain):
    scaled = grad * gain
    first = jnp.mean(scaled, axis=-1, keepdims=True)
    second = jnp.mean(scaled * normal, axis=-1, keepdims=True)
    gain_grad = jnp.sum(grad * normal, axis=0)
    bias_grad = jnp.sum(grad, axis=0)
    return rate * (scaled - first - normal * second), gain_grad, bias_grad


def heads_of(flat, sequences):
    return flat.reshape(sequences, flat.shape[0] // sequences, HEADS, HEAD_DIM)


def layer_fore(hidden_in, w, lengths):
    sequences = lengths.shape[0]
    model = hidden_in.shape[1]
    hidden = hidden_in.astype(F32)
    n1, r1 = norm_parts(hidden)
    a = (n1 * w.norm_gain + w.norm_bias).astype(BF)
    mixed = dot(a, w.joint_weight, 1, 0)
    q = ((mixed[:, :model] + w.joint_bias[:model]) * QUERY_SCALE).astype(BF)
    k = mixed[:, model : 2 * model].astype(BF)
    v = (mixed[:, 2 * model :] + w.joint_bias[model:]).astype(BF)
    qh, kh, vh = heads_of(q, sequences), heads_of(k, sequences), heads_of(v, sequences)
    scores = jnp.einsum("bqhd,bkhd->bhqk", qh, kh, preferred_element_type=F32)
    slots = scores.shape[-1]
    query_slot = lax.broadcasted_iota(jnp.int32, (sequences, slots, slots), 1)
    key_slot = lax.broadcasted_iota(jnp.int32, (sequences, slots, slots), 2)
    seen = (key_slot <= query_slot) & (key_slot < lengths[:, None, None])
    scores = jnp.where(seen[:, None], scores, MASKED)
    exponent = jnp.exp(RELAX * (scores - jnp.max(scores, axis=-1, keepdims=True)))
    probs = exponent / jnp.sum(exponent, axis=-1, keepdims=True)
    o = jnp.einsum("bhqk,bkhd->bqhd", probs.astype(BF), vh, preferred_element_type=F32)
    o = o.reshape(hidden.shape).astype(BF)
    y = dot(o, w.output_weight, 1, 0) + w.output_bias
    ny, ry = norm_parts(y)
    mid = hidden + ny * w.sandwich_gain + w.sandwich_bias
    nm, rm = norm_parts(mid)
    c = (nm * w.second_gain + w.second_bias).astype(BF)
    f = dot(c, w.expand_weight, 1, 0) + w.expand_bias
    g = jax.nn.gelu(f).astype(BF)
    e = dot(g, w.reduce_weight, 1, 0) + w.reduce_bias
    ne, re = norm_parts(e)
    out = mid + ne * w.closing_gain + w.closing_bias
    return out, Kept(n1, r1, a, qh, kh, vh, probs, o, y, ny, ry, nm, rm, c, f, g, e, ne, re, out)


def layer_back(dout, w, s, want_weights):
    sequences = s.qh.shape[0]
    de, closing_gain, closing_bias = norm_back(dout, s.ne, s.re, w.closing_gain)
    de = de.astype(BF)
    dg = dot(de, w.reduce_weight, 1, 1)
    df = jax.vjp(jax.nn.gelu, s.f)[1](dg)[0].astype(BF)
    dc = dot(df, w.expand_weight, 1, 1)
    dmid, second_gain, second_bias = norm_back(dc, s.nm, s.rm, w.second_gain)
    dmid = dmid + dout
    dy, sandwich_gain, sandwich_bias = norm_back(dmid, s.ny, s.ry, w.sandwich_gain)
    dy = dy.astype(BF)
    do = heads_of(dot(dy, w.output_weight, 1, 1).astype(BF), sequences)
    dprobs = jnp.einsum("bqhd,bkhd->bhqk", do, s.vh, preferred_element_type=F32)
    dv = jnp.einsum("bhqk,bqhd->bkhd", s.probs.astype(BF), do, preferred_element_type=F32)
    ds = RELAX * s.probs * (dprobs - jnp.sum(dprobs * s.probs, axis=-1, keepdims=True))
    ds = ds.astype(BF)
    dq = jnp.einsum("bhqk,bkhd->bqhd", ds, s.kh, preferred_element_type=F32)
    dk = jnp.einsum("bhqk,bqhd->bkhd", ds, s.qh, preferred_element_type=F32)
    flat = dout.shape
    dmixed = jnp.concatenate([dq.reshape(flat) * QUERY_SCALE, dk.reshape(flat), dv.reshape(flat)], axis=1).astype(BF)
    da = dot(dmixed, w.joint_weight, 1, 1)
    dh, norm_gain, norm_bias = norm_back(da, s.n1, s.r1, w.norm_gain)
    din = dmid + dh
    if not want_weights:
        return din, None
    model = flat[1]
    sums = jnp.sum(dmixed.astype(F32), axis=0)
    return din, Params(
        norm_gain=norm_gain,
        norm_bias=norm_bias,
        joint_weight=dot(s.a, dmixed, 0, 0),
        joint_bias=jnp.concatenate([sums[:model], sums[2 * model :]]),
        output_weight=dot(s.o, dy, 0, 0),
        output_bias=jnp.sum(dy.astype(F32), axis=0),
        sandwich_gain=sandwich_gain,
        sandwich_bias=sandwich_bias,
        second_gain=second_gain,
        second_bias=second_bias,
        expand_weight=dot(s.c, df, 0, 0),
        expand_bias=jnp.sum(df.astype(F32), axis=0),
        reduce_weight=dot(s.g, de, 0, 0),
        reduce_bias=jnp.sum(de.astype(F32), axis=0),
        closing_gain=closing_gain,
        closing_bias=closing_bias,
    )


def passed_along(block, axis, distance):
    devices = range(lax.axis_size(axis))
    route = [(i - distance, i) for i in devices if i - distance in devices]
    return lax.ppermute(block, axis, route)


def plain_local(tokens, lengths, *parameters):
    cotangent = parameters[-1]
    own = parameters[:-1]
    section = lax.axis_index("section")
    micro, rows, model = tokens.shape
    sequences = lengths.shape[1]
    slots = rows // sequences
    total_rows = micro * rows

    packed = jnp.concatenate([own[i] for i in VECTORS], axis=1)
    packed = lax.all_gather(packed, "batch", axis=0, tiled=True).astype(F32)
    w = list(own)
    start = 0
    for i in VECTORS:
        width = own[i].shape[1]
        w[i] = packed[:, start : start + width].reshape(-1)
        start += width
    for i, whole in zip(MATRICES, plain_gather([own[i] for i in MATRICES])):
        w[i] = whole
    w = Params(*w)

    flat_lengths = lengths.reshape(-1)
    seen = lax.broadcasted_iota(jnp.int32, (micro * sequences, slots), 1) < flat_lengths[:, None]
    valid = seen.astype(F32).reshape(total_rows, 1)
    source = tokens.reshape(total_rows, model)
    first_out, _ = layer_fore(source, w, flat_lengths)
    incoming = passed_along(first_out.astype(BF), "section", 1)
    out, s = layer_fore(jnp.where(section == 0, source, incoming), w, flat_lengths)
    section_out = out.astype(BF).reshape(1, micro, rows, model)
    squares = jnp.stack([jnp.sum(part * part * valid) for part in (s.y, s.e, s.out)])

    seed = cotangent.reshape(total_rows, model).astype(F32) * valid
    last_in, _ = layer_back(seed, w, s, False)
    incoming = passed_along(last_in.astype(BF), "section", -1)
    din, grads = layer_back(jnp.where(section == 1, seed, incoming.astype(F32)), w, s, True)
    section_grad = din.reshape(1, micro, rows, model)

    result = list(grads)
    for i, part in zip(MATRICES, plain_scatter([grads[i].astype(BF) for i in MATRICES])):
        result[i] = part
    devices = lax.axis_size("batch")
    small = jnp.concatenate([grads[i].reshape(devices, -1) for i in VECTORS], axis=1)
    small = lax.psum_scatter(small, "batch", scatter_dimension=0, tiled=True)
    start = 0
    for i in VECTORS:
        width = own[i].shape[1]
        result[i] = small[:, start : start + width]
        start += width
    count = jnp.sum(lengths).astype(F32)
    square_all, count_all = lax.psum((squares, count), "batch")
    magnitudes = jnp.sqrt(square_all / (count_all * model))[None]
    return (section_out, section_grad, magnitudes) + tuple(result)


def plain_gather(shards):
    return [lax.all_gather(w, "batch", axis=1, tiled=True)[0] for w in shards]


def plain_scatter(grads):
    return [lax.psum_scatter(g[None], "batch", scatter_dimension=1, tiled=True).astype(F32) for g in grads]


MESH = pl.DeviceIdType.MESH
BLOCKS = 12
VECTOR_ITEM = 12
PART = 64
SLOTS, EARLY_SLOTS = 5, 3
CROSS = 16
LAGS = (1, 2, 3, 4, 5)
GATHER_ORDER = (VECTOR_ITEM,) + tuple(range(BLOCKS))
GATHER_CROSSED = (3, 11)
GATHER_AHEAD = 4
SIDE_LAG, REST_LAG = 2, 3
SCATTER_ORDER = (8, 9, 10, 11, 4, 5, 6, 7, 3, 0, 1, 2)
UP, DOWN, SIDE = 0, 1, 2


def when(condition, action):
    if condition is True:
        action()
    else:
        pl.when(condition)(action)


def both(first, second):
    if first is True:
        return second
    if second is True:
        return first
    return first & second


class Place:
    def __init__(self, depth):
        index = lax.axis_index("batch")
        self.s = lax.axis_index("section")
        self.depth = depth
        self.z = index // 4
        self.x = (index // 2) % 2
        self.c = index % 2

    def device(self, z, x, c):
        return (self.s, (z * 2 + x) * 2 + c)

    def shard(self, z, x, c):
        return (z * 2 + x) * 2 + c

    def me(self):
        return self.shard(self.z, self.x, self.c)

    def across(self):
        return (1 - self.s, self.me())

    def greet(self):
        z, x, c = self.z, self.x, self.c
        sem = pltpu.get_barrier_semaphore()

        def signal(device):
            pl.semaphore_signal(sem, inc=1, device_id=device, device_id_type=MESH)

        signal(self.device(z, 1 - x, c))
        signal(self.device(z, x, 1 - c))
        signal(self.across())
        pl.when(z < self.depth - 1)(lambda: signal(self.device(z + 1, x, c)))
        pl.when(z > 0)(lambda: signal(self.device(z - 1, x, c)))
        chain = (z < self.depth - 1).astype(jnp.int32) + (z > 0).astype(jnp.int32)
        pl.semaphore_wait(sem, 3 + chain)


def spot(item, shard):
    if item < 8:
        return item, pl.multiple_of(shard * PART, 16)
    return 8 + shard // 4, pl.multiple_of((shard % 4) * 4 * PART + (item - 8) * PART, 16)


def shard_view(refs, item, width):
    joint, output, expand, reduce, vectors = refs
    if item < 3:
        return joint.at[:, pl.ds(item * width, width)]
    if item == 3:
        return output
    if item < 8:
        return expand.at[:, pl.ds((item - 4) * width, width)]
    if item < VECTOR_ITEM:
        return reduce.at[pl.ds((item - 8) * PART, PART)]
    return vectors


class Gather:
    def __init__(self, place, own, store, vectors, sems):
        self.p, self.own, self.store, self.vectors = place, own, store, vectors
        self.send, self.share, self.recv, self.local = sems
        self.sent = []

    def at(self, item, shard):
        if item == VECTOR_ITEM:
            return self.vectors.at[shard]
        block, row = spot(item, shard)
        return self.store.at[block, pl.ds(row, PART)]

    def copy(self, item, shard, way, first=False):
        p = self.p
        target = self.at(item, shard)
        source = shard_view(self.own, item, self.store.shape[2]) if first else target
        recv = self.recv.at[item, shard]
        if way is None:
            send, device = self.share.at[item, shard // 2], p.device(p.z, p.x, 1 - p.c)
        else:
            send = self.send.at[item, shard // 2, way]
            device = (p.device(p.z + 1, p.x, p.c), p.device(p.z - 1, p.x, p.c), p.device(p.z, 1 - p.x, p.c))[way]
        return pltpu.make_async_remote_copy(source, target, send, recv, device_id=device, device_id_type=MESH)

    def go(self, item, shard, way, condition, first=False):
        self.sent.append((item, shard, way, condition, first))
        when(condition, lambda: self.copy(item, shard, way, first).start())

    def arrived(self, item, shard):
        self.copy(item, shard, None).wait_recv()

    def keep_own(self):
        me = self.p.me()
        copies = [
            pltpu.make_async_copy(shard_view(self.own, item, self.store.shape[2]), self.at(item, me), self.local.at[item])
            for item in range(BLOCKS + 1)
        ]
        for copy in copies:
            copy.start()
        return copies

    def own_sends(self, item):
        p = self.p
        self.go(item, p.me(), UP, p.z < p.depth - 1, True)
        self.go(item, p.me(), DOWN, p.z > 0, True)
        self.go(item, p.me(), SIDE, True, True)
        self.go(item, p.me(), None, True, True)

    def chain_round(self, item, hop):
        p = self.p
        crossed = item in GATHER_CROSSED
        for x in (p.x, 1 - p.x) if crossed else (p.x,):
            for origin, present, way, onward in (
                (p.z - hop, p.z >= hop, UP, p.z < p.depth - 1),
                (p.z + hop, p.z + hop < p.depth, DOWN, p.z > 0),
            ):
                shard = p.shard(origin, x, p.c)
                when(present, lambda: self.arrived(item, shard))
                self.go(item, shard, way, both(present, onward))
                if not crossed:
                    self.go(item, shard, SIDE, present)
                self.go(item, shard, None, present)

    def side_own(self, item):
        p = self.p
        shard = p.shard(p.z, 1 - p.x, p.c)
        self.arrived(item, shard)
        if item in GATHER_CROSSED:
            self.go(item, shard, UP, p.z < p.depth - 1)
            self.go(item, shard, DOWN, p.z > 0)
        self.go(item, shard, None, True)

    def side_round(self, item, hop):
        p = self.p
        if item in GATHER_CROSSED:
            return
        for origin, present in ((p.z - hop, p.z >= hop), (p.z + hop, p.z + hop < p.depth)):
            shard = p.shard(origin, 1 - p.x, p.c)
            when(present, lambda: self.arrived(item, shard))
            self.go(item, shard, None, present)

    def rest(self, item):
        p = self.p
        for z in range(p.depth):
            for x in range(2):
                self.arrived(item, p.shard(z, x, 1 - p.c))

    def drain(self):
        for item, shard, way, condition, first in self.sent:
            when(condition, lambda: self.copy(item, shard, way, first).wait_send())


def run_gather(gather, ready):
    depth, count = gather.p.depth, len(GATHER_ORDER)
    kept = gather.keep_own()
    for item in GATHER_ORDER[:GATHER_AHEAD]:
        gather.own_sends(item)

    def sides(item):
        for hop in range(1, depth):
            gather.side_round(item, hop)

    def finish(item):
        gather.rest(item)
        kept[item].wait()
        ready(item)

    for place, item in enumerate(GATHER_ORDER):
        if item in GATHER_CROSSED:
            gather.side_own(item)
        for hop in range(1, depth):
            gather.chain_round(item, hop)
            if hop == 1:
                if place + GATHER_AHEAD < count:
                    gather.own_sends(GATHER_ORDER[place + GATHER_AHEAD])
                if item not in GATHER_CROSSED:
                    gather.side_own(item)
        if place >= SIDE_LAG:
            sides(GATHER_ORDER[place - SIDE_LAG])
        if place >= REST_LAG:
            finish(GATHER_ORDER[place - REST_LAG])
    for item in GATHER_ORDER[count - SIDE_LAG :]:
        sides(item)
    for item in GATHER_ORDER[count - REST_LAG :]:
        finish(item)


def gather_sems(depth):
    kind, items = pltpu.SemaphoreType.DMA, BLOCKS + 1
    return [kind((items, 2 * depth, 3)), kind((items, 2 * depth)), kind((items, 4 * depth)), kind((items,))]


def total(*refs):
    value = refs[0][...].astype(F32)
    for ref in refs[1:]:
        value = value + ref[...].astype(F32)
    return value


def crossing(step, rows):
    return 0 if rows <= CROSS or step % 3 == 2 else CROSS


class Scatter:
    def __init__(self, place, part, count, slots, early, buffers, outs, sems):
        self.p, self.part, self.count, self.slots, self.early, self.outs = place, part, count, slots, early, outs
        self.core_in, self.side_in, self.chain_in, self.cross_in, self.last_in = buffers
        (self.core_send, self.core_recv, self.side_send, self.side_recv, self.chain_send, self.chain_recv,
         self.cross_send, self.cross_recv, self.last_send, self.last_recv,
         self.core_free, self.side_free, self.chain_free) = sems
        depth = place.depth
        self.rows = self.core_in.shape[2]
        self.origins = [q for pair in zip(range(depth - 1, -1, -1), range(depth)) for q in pair][:depth]

    def main(self, step):
        return pl.ds(0, self.rows - crossing(step, self.rows))

    def tail(self, step):
        cut = crossing(step, self.rows)
        return pl.ds(self.rows - cut, cut)

    def mine(self, step, z, x, c):
        return self.part(step, self.p.shard(z, x, c))

    def core_copy(self, step, z, x):
        p, slot = self.p, step % self.early
        return pltpu.make_async_remote_copy(
            self.mine(step, z, x, 1 - p.c), self.core_in.at[slot, z * 2 + x],
            self.core_send.at[slot, z * 2 + x], self.core_recv.at[slot, z * 2 + x],
            device_id=p.device(p.z, p.x, 1 - p.c), device_id_type=MESH)

    def side_copy(self, step, z):
        p, slot, rows = self.p, step % self.early, self.main(step)
        return pltpu.make_async_remote_copy(
            self.mine(step, z, 1 - p.x, p.c).at[rows], self.side_in.at[slot, z, rows],
            self.side_send.at[slot, z], self.side_recv.at[slot, z],
            device_id=p.device(p.z, 1 - p.x, p.c), device_id_type=MESH)

    def chain_copy(self, step, z, up):
        p, slot = self.p, step % self.slots
        return pltpu.make_async_remote_copy(
            self.mine(step, z, p.x, p.c), self.chain_in.at[slot, 1 - up, z],
            self.chain_send.at[slot, 1 - up, z], self.chain_recv.at[slot, 1 - up, z],
            device_id=p.device(p.z + 2 * up - 1, p.x, p.c), device_id_type=MESH)

    def cross_copy(self, step, z, up):
        p, slot, rows = self.p, step % self.slots, self.tail(step)
        return pltpu.make_async_remote_copy(
            self.mine(step, z, 1 - p.x, p.c).at[rows], self.cross_in.at[slot, 1 - up, z, pl.ds(0, rows.size)],
            self.cross_send.at[slot, 1 - up, z], self.cross_recv.at[slot, 1 - up, z],
            device_id=p.device(p.z + 2 * up - 1, p.x, p.c), device_id_type=MESH)

    def last_copy(self, step):
        p, slot, rows = self.p, step % self.slots, self.tail(step)
        return pltpu.make_async_remote_copy(
            self.mine(step, p.z, 1 - p.x, p.c).at[rows], self.last_in.at[slot, pl.ds(0, rows.size)],
            self.last_send.at[slot], self.last_recv.at[slot],
            device_id=p.device(p.z, 1 - p.x, p.c), device_id_type=MESH)

    def core_stage(self, step):
        p = self.p
        if step >= self.early:
            self.core_drain(step - self.early)
            pl.semaphore_wait(self.core_free, 1)
        for x in (1 - p.x, p.x):
            for z in self.origins:
                self.core_copy(step, z, x).start()

    def core_drain(self, step):
        for z in self.origins:
            for x in range(2):
                self.core_copy(step, z, x).wait_send()

    def from_core(self, step, z, x):
        self.core_copy(step, z, x).wait_recv()
        return self.core_in.at[step % self.early, z * 2 + x]

    def side_stage(self, step):
        p = self.p
        if step >= self.early:
            self.side_drain(step - self.early)
            pl.semaphore_wait(self.side_free, 1)
        for z in self.origins:
            twin = self.from_core(step, z, 1 - p.x)
            mine = self.mine(step, z, 1 - p.x, p.c)
            mine[...] = total(mine, twin).astype(mine.dtype)
            self.side_copy(step, z).start()

    def side_drain(self, step):
        for z in self.origins:
            self.side_copy(step, z).wait_send()

    def ways(self, z):
        p, last = self.p, self.p.depth - 1
        return (p.z < z).astype(jnp.int32), ((p.z < z) & (p.z > 0)) | ((p.z > z) & (p.z < last))

    def chain_stage(self, step, near):
        p, slot, last = self.p, step % self.slots, self.p.depth - 1
        cut = crossing(step, self.rows)
        if near and step >= self.slots:
            self.chain_drain(step - self.slots)
            pl.when(p.z < last)(lambda: pl.semaphore_wait(self.chain_free.at[0], 1))
            pl.when(p.z > 0)(lambda: pl.semaphore_wait(self.chain_free.at[1], 1))
        for z in self.origins:
            up, fed = self.ways(z)
            begun = jnp.where(p.z < z, p.z, last - p.z)
            if near:
                self.sum_side(step, z)

            @pl.when((p.z != z) & ((begun <= 1) if near else (begun > 1)))
            def _():
                mine = self.mine(step, z, p.x, p.c)
                other = self.mine(step, z, 1 - p.x, p.c)

                @pl.when(fed)
                def _():
                    self.chain_copy(step, z, up).wait_recv()
                    mine[...] = total(mine, self.chain_in.at[slot, 1 - up, z]).astype(mine.dtype)

                self.chain_copy(step, z, up).start()
                if cut:
                    @pl.when(fed)
                    def _():
                        self.cross_copy(step, z, up).wait_recv()
                        here = other.at[self.tail(step)]
                        here[...] = total(here, self.cross_in.at[slot, 1 - up, z, pl.ds(0, cut)]).astype(here.dtype)

                    self.cross_copy(step, z, up).start()
        if near and step + self.early < self.count:
            self.signal(self.core_free, p.device(p.z, p.x, 1 - p.c))
            self.signal(self.side_free, p.device(p.z, 1 - p.x, p.c))

    @staticmethod
    def signal(sem, device):
        pl.semaphore_signal(sem, inc=1, device_id=device, device_id_type=MESH)

    def sum_side(self, step, z):
        p, main = self.p, self.main(step)
        mine, twin = self.mine(step, z, p.x, p.c), self.from_core(step, z, p.x)
        self.side_copy(step, z).wait_recv()
        here = mine.at[main]
        here[...] = total(here, twin.at[main], self.side_in.at[step % self.early, z, main]).astype(mine.dtype)
        if crossing(step, self.rows):
            here = mine.at[self.tail(step)]
            here[...] = total(here, twin.at[self.tail(step)]).astype(mine.dtype)

    def chain_drain(self, step):
        p = self.p
        for z in self.origins:
            up, _ = self.ways(z)

            @pl.when(p.z != z)
            def _():
                self.chain_copy(step, z, up).wait_send()
                if crossing(step, self.rows):
                    self.cross_copy(step, z, up).wait_send()
        if crossing(step, self.rows):
            self.last_copy(step).wait_send()

    def incoming(self, copy):
        p = self.p
        pl.when(p.z > 0)(lambda: copy(1).wait_recv())
        pl.when(p.z < p.depth - 1)(lambda: copy(0).wait_recv())

    def outcome(self, put, parts, below, above):
        p, last = self.p, self.p.depth - 1
        pl.when(p.z == 0)(lambda: put(*parts, above))
        pl.when(p.z == last)(lambda: put(*parts, below))
        pl.when((p.z > 0) & (p.z < last))(lambda: put(*parts, below, above))

    def last_stage(self, step):
        p, slot, cut = self.p, step % self.slots, crossing(step, self.rows)
        if not cut:
            return
        self.incoming(lambda up: self.cross_copy(step, p.z, up))
        here = self.mine(step, p.z, 1 - p.x, p.c).at[self.tail(step)]

        def put(*refs):
            here[...] = total(*refs).astype(here.dtype)

        self.outcome(put, [here], *(self.cross_in.at[slot, way, p.z, pl.ds(0, cut)] for way in range(2)))
        self.last_copy(step).start()

    def own_stage(self, step):
        p, slot, last, cut = self.p, step % self.slots, self.p.depth - 1, crossing(step, self.rows)
        self.incoming(lambda up: self.chain_copy(step, p.z, up))
        mine, out = self.mine(step, p.z, p.x, p.c), self.outs[step]
        if cut:
            self.last_copy(step).wait_recv()
        for rows, extra in ((self.main(step), []), (self.tail(step), [self.last_in.at[slot, pl.ds(0, cut)]] if cut else None)):
            if extra is None:
                continue

            def put(*refs):
                out[rows] = total(*refs)

            self.outcome(put, [mine.at[rows]] + extra, *(self.chain_in.at[slot, way, p.z, rows] for way in range(2)))
        if step + self.slots < self.count:
            pl.when(p.z > 0)(lambda: self.signal(self.chain_free.at[0], p.device(p.z - 1, p.x, p.c)))
            pl.when(p.z < last)(lambda: self.signal(self.chain_free.at[1], p.device(p.z + 1, p.x, p.c)))

    def drain(self):
        for step in range(self.count - self.early, self.count):
            self.core_drain(step)
            self.side_drain(step)
        for step in range(self.count - self.slots, self.count):
            self.chain_drain(step)


def run_scatter(scatter, vector_scatter, ready, done):
    side_lag, near_lag, far_lag, last_lag, own_lag = LAGS
    for tick in range(BLOCKS + own_lag):
        if tick < BLOCKS:
            ready(tick)
        if tick >= own_lag:
            scatter.own_stage(tick - own_lag)
            done(tick - own_lag)
        if 0 <= tick - last_lag < BLOCKS:
            scatter.last_stage(tick - last_lag)
        if tick < BLOCKS:
            scatter.core_stage(tick)
        if 0 <= tick - side_lag < BLOCKS:
            scatter.side_stage(tick - side_lag)
        if 0 <= tick - far_lag < BLOCKS:
            scatter.chain_stage(tick - far_lag, False)
        if 0 <= tick - near_lag < BLOCKS:
            scatter.chain_stage(tick - near_lag, True)
        if tick == BLOCKS - 1:
            vector_scatter.core_stage(0)
        if tick == BLOCKS:
            vector_scatter.side_stage(0)
        if tick == BLOCKS + 1:
            vector_scatter.chain_stage(0, True)
            vector_scatter.chain_stage(0, False)
    vector_scatter.own_stage(0)
    scatter.drain()
    vector_scatter.drain()


def scatter_scratch(depth, slots, early, rows, width, dtype):
    dma, plain = pltpu.SemaphoreType.DMA, pltpu.SemaphoreType.REGULAR
    cross = min(CROSS, rows)
    return [
        pltpu.VMEM((early, 2 * depth, rows, width), dtype),
        pltpu.VMEM((early, depth, rows, width), dtype),
        pltpu.VMEM((slots, 2, depth, rows, width), dtype),
        pltpu.VMEM((slots, 2, depth, cross, width), dtype), pltpu.VMEM((slots, cross, width), dtype),
        dma((early, 2 * depth)), dma((early, 2 * depth)), dma((early, depth)), dma((early, depth)),
        dma((slots, 2, depth)), dma((slots, 2, depth)), dma((slots, 2, depth)), dma((slots, 2, depth)),
        dma((slots,)), dma((slots,)), plain, plain, plain((2,)),
    ]


(NORM_GAIN, NORM_BIAS, OUTPUT_BIAS, SANDWICH_GAIN, SANDWICH_BIAS, SECOND_GAIN, SECOND_BIAS, REDUCE_BIAS,
 CLOSING_GAIN, CLOSING_BIAS, QUERY_BIAS, VALUE_BIAS, EXPAND_BIAS) = range(13)
NARROW = 10
VECTOR_ROWS = 16
FIGURES = 13
LANES = 128
TILE = 256
STAGED = 3
CHUNK = 64
CURVE = math.sqrt(2.0 / math.pi)
BEND = 0.044715


class Work(NamedTuple):
    vec: Any
    dvec: Any
    h: Any
    a: Any
    q: Any
    k: Any
    v: Any
    p: Any
    o: Any
    n_h: Any
    r_h: Any
    n_y: Any
    r_y: Any
    n_m: Any
    r_m: Any
    n_e: Any
    r_e: Any
    mid: Any
    c: Any
    g: Any
    slope: Any
    de: Any
    dy: Any
    do: Any
    din: Any
    sums: Any


def mxu(left, right, left_dim, right_dim):
    return lax.dot_general(left, right, (((left_dim,), (right_dim,)), ((), ())), preferred_element_type=F32)


def mean_of(value):
    return jnp.mean(value, axis=-1, keepdims=True)


def norm_of(value):
    centered = value - mean_of(value)
    rate = lax.rsqrt(mean_of(centered * centered) + EPSILON)
    return centered * rate, rate


def norm_pull(grad, normal, rate, gain):
    scaled = grad * gain
    return rate * (scaled - mean_of(scaled) - normal * mean_of(scaled * normal))


def column_sum(value):
    return jnp.sum(value, axis=0, keepdims=True)


class Layer:
    def __init__(self, work, store, lengths, swift=True):
        self.w, self.store, self.lengths, self.swift = work, store, lengths, swift
        self.tokens, self.width = work.h.shape
        self.sequences = lengths.shape[0]
        self.slots = self.tokens // self.sequences

    def row(self, index):
        return self.w.vec[index : index + 1, :]

    def add(self, index, value):
        self.w.dvec[index : index + 1, :] += value

    def chunks(self, body, first=0, last=None):
        last = self.tokens if last is None else last

        def step(i, carry):
            body(pl.ds(pl.multiple_of(i * CHUNK, CHUNK), CHUNK), i)
            return carry

        lax.fori_loop(first // CHUNK, last // CHUNK, step, 0)

    def tiles(self, body):
        def step(i, carry):
            body(pl.ds(pl.multiple_of(i * TILE, TILE), TILE))
            return carry

        lax.fori_loop(0, self.width // TILE, step, 0, unroll=self.swift)

    def valid(self, i):
        per = self.slots // CHUNK
        slot = (i % per) * CHUNK + lax.broadcasted_iota(jnp.int32, (CHUNK, 1), 0)
        return jnp.where(slot < self.lengths[i // per], 1.0, 0.0)


    def fore_start(self, source, first=0, last=None):
        w = self.w

        def body(rows, i):
            h = source[rows, :]
            if source is not w.h:
                w.h[rows, :] = h
            normal, rate = norm_of(h.astype(F32))
            w.n_h[rows, :] = normal
            w.r_h[rows, :] = rate
            w.a[rows, :] = (normal * self.row(NORM_GAIN) + self.row(NORM_BIAS)).astype(BF)

        self.chunks(body, first, last)

    def part(self, index):
        return pl.ds(index * self.slots, self.slots)

    def fore_joint(self, block, rows):
        w = self.w
        bias = (QUERY_BIAS, None, VALUE_BIAS)[block]
        target = (w.q, w.k, w.v)[block]

        def body(tile):
            mixed = mxu(w.a[rows, :], self.store[block, :, tile], 1, 0)
            if bias is not None:
                mixed = mixed + w.vec[bias : bias + 1, tile]
            if block == 0:
                mixed = mixed * QUERY_SCALE
            target[rows, tile] = mixed.astype(BF)

        self.tiles(body)

    def pairs(self, sequence, body):
        count = self.width // LANES
        rows, length = self.part(sequence), self.lengths[sequence]

        def step(i, carry):
            body(rows, pl.ds(pl.multiple_of(i * LANES, LANES), LANES), sequence * count + i, length)
            return carry

        lax.fori_loop(0, count, step, 0, unroll=8 if self.swift else 2)

    def split(self, value):
        low = lax.broadcasted_iota(jnp.int32, value.shape, 1) < HEAD_DIM
        zero = jnp.zeros_like(value)
        return jnp.concatenate([jnp.where(low, value, zero), jnp.where(low, zero, value)], axis=0)

    def fore_attention(self, sequence):
        w, slots = self.w, self.slots

        def body(rows, lanes, i, length):
            scores = mxu(self.split(w.q[rows, lanes]), w.k[rows, lanes], 1, 1)
            query = lax.broadcasted_iota(jnp.int32, (2 * slots, slots), 0) % slots
            key = lax.broadcasted_iota(jnp.int32, (2 * slots, slots), 1)
            scores = jnp.where((key <= query) & (key < length), scores, MASKED)
            weight = jnp.exp(RELAX * (scores - jnp.max(scores, axis=-1, keepdims=True)))
            probs = (weight / jnp.sum(weight, axis=-1, keepdims=True)).astype(BF)
            w.p[i] = probs
            wide = jnp.concatenate([probs[:slots], probs[slots:]], axis=1)
            w.o[rows, lanes] = mxu(wide, self.split(w.v[rows, lanes]), 1, 0).astype(BF)

        self.pairs(sequence, body)

    def fore_output(self):
        w = self.w

        def body(tile):
            w.n_y[:, tile] = mxu(w.o[...], self.store[3, :, tile], 1, 0) + w.vec[OUTPUT_BIAS : OUTPUT_BIAS + 1, tile]

        self.tiles(body)

        def middle(rows, i):
            y = w.n_y[rows, :]
            w.sums[0:1, :] += column_sum(y * y * self.valid(i))
            normal, rate = norm_of(y)
            w.n_y[rows, :] = normal
            w.r_y[rows, :] = rate
            mid = w.h[rows, :].astype(F32) + (normal * self.row(SANDWICH_GAIN) + self.row(SANDWICH_BIAS))
            w.mid[rows, :] = mid
            normal, rate = norm_of(mid)
            w.n_m[rows, :] = normal
            w.r_m[rows, :] = rate
            w.c[rows, :] = (normal * self.row(SECOND_GAIN) + self.row(SECOND_BIAS)).astype(BF)

        self.chunks(middle)

    def fore_expand(self, block):
        w = self.w

        def body(tile):
            f = mxu(w.c[...], self.store[4 + block, :, tile], 1, 0)
            f = f + w.vec[EXPAND_BIAS + block : EXPAND_BIAS + block + 1, tile]
            square = f * f
            bent = jnp.tanh(CURVE * f * (1.0 + BEND * square))
            half = 0.5 * (1.0 + bent)
            w.g[block, :, tile] = (f * half).astype(BF)
            slope = half + 0.5 * f * (1.0 - bent * bent) * (CURVE * (1.0 + 3.0 * BEND * square))
            w.slope[block, :, tile] = slope.astype(BF)

        self.tiles(body)

    def fore_reduce(self, rows):
        w = self.w

        def body(tile):
            e = mxu(w.g[0, rows, :], self.store[8, :, tile], 1, 0)
            for block in range(1, 4):
                e = e + mxu(w.g[block, rows, :], self.store[8 + block, :, tile], 1, 0)
            w.n_e[rows, tile] = e + w.vec[REDUCE_BIAS : REDUCE_BIAS + 1, tile]

        self.tiles(body)

    def fore_end(self, target, first=0, last=None):
        w = self.w

        def body(rows, i):
            e = w.n_e[rows, :]
            valid = self.valid(i)
            w.sums[1:2, :] += column_sum(e * e * valid)
            normal, rate = norm_of(e)
            w.n_e[rows, :] = normal
            w.r_e[rows, :] = rate
            out = w.mid[rows, :] + (normal * self.row(CLOSING_GAIN) + self.row(CLOSING_BIAS))
            w.sums[2:3, :] += column_sum(out * out * valid)
            target[rows, :] = out.astype(BF)

        self.chunks(body, first, last)


    def back_start(self, seed, masked, first=0, last=None):
        w = self.w

        def body(rows, i):
            dout = seed[rows, :].astype(F32)
            if masked:
                dout = dout * self.valid(i)
            w.din[rows, :] = dout
            normal = w.n_e[rows, :]
            self.add(CLOSING_GAIN, column_sum(dout * normal))
            self.add(CLOSING_BIAS, column_sum(dout))
            de = norm_pull(dout, normal, w.r_e[rows, :], self.row(CLOSING_GAIN)).astype(BF)
            w.de[rows, :] = de
            self.add(REDUCE_BIAS, column_sum(de.astype(F32)))

        self.chunks(body, first, last)

    def back_reduce(self, block, rows):
        w = self.w

        def body(tile):
            dg = mxu(w.de[rows, :], self.store[8 + block, tile, :], 1, 1)
            df = (dg * w.slope[block, rows, tile].astype(F32)).astype(BF)
            w.slope[block, rows, tile] = df
            w.dvec[EXPAND_BIAS + block : EXPAND_BIAS + block + 1, tile] += column_sum(df.astype(F32))

        self.tiles(body)

    def back_expand(self):
        w = self.w

        def body(tile):
            dc = mxu(w.slope[0], self.store[4, tile, :], 1, 1)
            for block in range(1, 4):
                dc = dc + mxu(w.slope[block], self.store[4 + block, tile, :], 1, 1)
            w.mid[:, tile] = dc

        self.tiles(body)

        def middle(rows, i):
            dc = w.mid[rows, :]
            normal = w.n_m[rows, :]
            self.add(SECOND_GAIN, column_sum(dc * normal))
            self.add(SECOND_BIAS, column_sum(dc))
            dmid = w.din[rows, :] + norm_pull(dc, normal, w.r_m[rows, :], self.row(SECOND_GAIN))
            w.din[rows, :] = dmid
            normal = w.n_y[rows, :]
            self.add(SANDWICH_GAIN, column_sum(dmid * normal))
            self.add(SANDWICH_BIAS, column_sum(dmid))
            dy = norm_pull(dmid, normal, w.r_y[rows, :], self.row(SANDWICH_GAIN)).astype(BF)
            w.dy[rows, :] = dy
            self.add(OUTPUT_BIAS, column_sum(dy.astype(F32)))

        self.chunks(middle)

    def back_output(self):
        w = self.w

        def body(tile):
            w.do[:, tile] = mxu(w.dy[...], self.store[3, tile, :], 1, 1).astype(BF)

        self.tiles(body)

    def back_attention(self, sequence):
        w, slots = self.w, self.slots

        def body(rows, lanes, i, length):
            grad = self.split(w.do[rows, lanes])
            probs = w.p[i]
            value = probs.astype(F32)
            dprobs = mxu(grad, w.v[rows, lanes], 1, 1)
            inner = jnp.sum(dprobs * value, axis=-1, keepdims=True)
            ds = (RELAX * value * (dprobs - inner)).astype(BF)
            wide = jnp.concatenate([ds[:slots], ds[slots:]], axis=1)
            dv = mxu(probs, grad, 0, 0)
            dk = mxu(ds, self.split(w.q[rows, lanes]), 0, 0)
            dq = mxu(wide, self.split(w.k[rows, lanes]), 1, 0) * QUERY_SCALE
            w.q[rows, lanes] = dq.astype(BF)
            w.k[rows, lanes] = dk.astype(BF)
            w.v[rows, lanes] = dv.astype(BF)

        self.pairs(sequence, body)

    def back_joint(self, rows):
        w = self.w

        def body(tile):
            da = mxu(w.q[rows, :], self.store[0, tile, :], 1, 1)
            da = da + mxu(w.k[rows, :], self.store[1, tile, :], 1, 1)
            w.mid[rows, tile] = da + mxu(w.v[rows, :], self.store[2, tile, :], 1, 1)

        self.tiles(body)

    def back_end(self, target, first=0, last=None):
        w = self.w

        def body(rows, i):
            da = w.mid[rows, :]
            normal = w.n_h[rows, :]
            self.add(NORM_GAIN, column_sum(da * normal))
            self.add(NORM_BIAS, column_sum(da))
            self.add(QUERY_BIAS, column_sum(w.q[rows, :].astype(F32)))
            self.add(VALUE_BIAS, column_sum(w.v[rows, :].astype(F32)))
            din = w.din[rows, :] + norm_pull(da, normal, w.r_h[rows, :], self.row(NORM_GAIN))
            w.din[rows, :] = din
            target[rows, :] = din.astype(BF)

        self.chunks(body, first, last)


    def weight_grad(self, block):
        w = self.w
        if block < 3:
            left, right = w.a, (w.q, w.k, w.v)[block]
        elif block == 3:
            left, right = w.o, w.dy
        elif block < 8:
            left, right = w.c, w.slope.at[block - 4]
        else:
            left, right = w.g.at[block - 8], w.de

        def body(tile):
            self.store[block, tile, :] = mxu(left[:, tile], right[...], 0, 0).astype(BF)

        self.tiles(body)


def unfold_vectors(tiles, vec, count):
    for pair in range(count // 2):
        vec[:NARROW, pair * LANES : (pair + 1) * LANES] = tiles[2 * pair, :NARROW, :] + tiles[2 * pair + 1, :NARROW, :]
    half, quarter = count // 2, count // 4
    for shard in range(count):
        row, lane = QUERY_BIAS + shard // half, (shard % half) * LANES
        vec[row : row + 1, lane : lane + LANES] = tiles[shard, NARROW : NARROW + 1, :]
        for part in range(2):
            row, lane = EXPAND_BIAS + shard // quarter, ((shard % quarter) * 2 + part) * LANES
            source = NARROW + 1 + part
            vec[row : row + 1, lane : lane + LANES] = tiles[shard, source : source + 1, :]


def fold_vectors(tiles, dvec, figures, count):
    half, quarter = count // 2, count // 4
    for shard in range(count):
        pair = shard // 2
        tiles[shard, :NARROW, :] = dvec[:NARROW, pair * LANES : (pair + 1) * LANES]
        row, lane = QUERY_BIAS + shard // half, (shard % half) * LANES
        tiles[shard, NARROW : NARROW + 1, :] = dvec[row : row + 1, lane : lane + LANES]
        for part in range(2):
            row, lane = EXPAND_BIAS + shard // quarter, ((shard % quarter) * 2 + part) * LANES
            target = NARROW + 1 + part
            tiles[shard, target : target + 1, :] = dvec[row : row + 1, lane : lane + LANES]
        tiles[shard, FIGURES : FIGURES + 1, :] = figures
        tiles[shard, FIGURES + 1 :, :] = jnp.zeros((VECTOR_ROWS - FIGURES - 1, LANES), F32)


def figures_of(sums, lengths):
    lane = lax.broadcasted_iota(jnp.int32, (1, LANES), 1)
    row = jnp.zeros((1, LANES), F32)
    for i in range(3):
        row = jnp.where(lane == i, jnp.sum(sums[i : i + 1, :], axis=1, keepdims=True), row)
    seen = lengths[0]
    for i in range(1, lengths.shape[0]):
        seen = seen + lengths[i]
    return jnp.where(lane == 3, seen.astype(F32), row)


def relay_kernel(depth, lengths, tokens, cotangent, joint, output, expand, reduce, vectors,
                 section_out, section_grad, joint_out, output_out, expand_out, reduce_out, vector_out,
                 store, tiles, vec, dvec, sums, h, a, q, k, v, p, o, n_h, r_h, n_y, r_y, n_m, r_m, n_e, r_e,
                 mid, c, g, slope, de, dy, do, din, result, staged, incoming, pass_sems, out_sems, *rest):
    place = Place(depth)
    width = store.shape[2]
    count = 4 * depth
    gather_parts, rest = rest[:4], rest[4:]
    scatter_parts, vector_parts = rest[:18], rest[18:]
    work = Work(vec, dvec, h, a, q, k, v, p, o, n_h, r_h, n_y, r_y, n_m, r_m, n_e, r_e, mid, c, g, slope,
                de, dy, do, din, sums)
    layer, hidden = Layer(work, store, lengths), Layer(work, store, lengths, swift=False)
    slots, parts = layer.slots, range(layer.sequences)
    whole = pl.ds(0, layer.tokens)
    first, second = place.s == 0, place.s == 1

    def passing(source, part, way):
        rows = pl.ds(part * slots, slots)
        return pltpu.make_async_remote_copy(
            source.at[rows], incoming.at[rows], pass_sems.at[way, 0, part], pass_sems.at[way, 1, part],
            device_id=place.across(), device_id_type=MESH)

    def forward(part):
        return passing(result, part, 0)

    def backward(part):
        return passing(do, part, 1)

    out_copy = pltpu.make_async_copy(result, section_out, out_sems.at[BLOCKS])
    grad_copy = pltpu.make_async_copy(din, section_grad, out_sems.at[BLOCKS + 1])

    token_copy = pltpu.make_async_copy(tokens, h, out_sems.at[BLOCKS + 2])
    seed_copy = pltpu.make_async_copy(cotangent, dy, out_sems.at[BLOCKS + 3])
    pl.when(first)(lambda: token_copy.start())
    pl.when(second)(lambda: seed_copy.start())
    place.greet()
    dvec[...] = jnp.zeros_like(dvec)
    sums[...] = jnp.zeros_like(sums)

    def fore_first(part, source):
        layer.fore_start(source, part * slots, (part + 1) * slots)

    def fore_last(part):
        layer.fore_reduce(layer.part(part))
        layer.fore_end(result, part * slots, (part + 1) * slots)

    def back_first(part, seed, masked):
        layer.back_start(seed, masked, part * slots, (part + 1) * slots)
        for block in range(4):
            layer.back_reduce(block, layer.part(part))

    def back_last(part, layer):
        layer.back_attention(part)
        layer.back_joint(layer.part(part))
        layer.back_end(do, part * slots, (part + 1) * slots)

    def ready(item):
        if item == VECTOR_ITEM:
            unfold_vectors(tiles, vec, count)

        @pl.when(first)
        def _():
            if item == VECTOR_ITEM:
                token_copy.wait()
                hidden.fore_start(h)
            elif item < 3:
                hidden.fore_joint(item, whole)
                if item == 2:
                    for part in parts:
                        hidden.fore_attention(part)
            elif item == 3:
                hidden.fore_output()
            elif item < 8:
                hidden.fore_expand(item - 4)
            elif item == BLOCKS - 1:
                for part in parts:
                    fore_last(part)
                    forward(part).start()

    gather = Gather(place, (joint, output, expand, reduce, vectors), store, tiles, gather_parts)
    run_gather(gather, ready)
    gather.drain()

    @pl.when(second)
    def _():
        for part in parts:
            forward(part).wait_recv()
            fore_first(part, incoming)
            for block in range(3):
                layer.fore_joint(block, layer.part(part))
            layer.fore_attention(part)
        layer.fore_output()
        for block in range(4):
            layer.fore_expand(block)
        layer.fore_reduce(whole)
        layer.fore_end(result)
        seed_copy.wait()
        layer.back_start(dy, True)
        for block in range(4):
            layer.back_reduce(block, whole)
        layer.back_expand()
        layer.back_output()
        for part in parts:
            back_last(part, layer)
            backward(part).start()

    out_copy.start()

    @pl.when(first)
    def _():
        for part in parts:
            backward(part).wait_recv()
            back_first(part, incoming, False)

    def fill(step):
        block = SCATTER_ORDER[step]

        @pl.when(first)
        def _():
            if step == 4:
                hidden.back_expand()
            elif block == 3:
                hidden.back_output()
            elif step == 9:
                for part in parts:
                    back_last(part, hidden)

        if step == 0:
            for part in range(4):
                layer.weight_grad(8 + part)
        elif step >= 4:
            layer.weight_grad(block)
        if step == 9:
            grad_copy.start()
        if step == BLOCKS - 1:
            fold_vectors(tiles, dvec, figures_of(sums, lengths), count)

    def part_of(step, shard):
        block, row = spot(SCATTER_ORDER[step], shard)
        return store.at[block, pl.ds(row, PART)]

    targets = [shard_view((joint_out, output_out, expand_out, reduce_out, None), item, width) for item in SCATTER_ORDER]
    outs = [staged.at[step % STAGED] for step in range(BLOCKS)]
    copies = [pltpu.make_async_copy(outs[step], targets[step], out_sems.at[step]) for step in range(BLOCKS)]
    scatter = Scatter(place, part_of, BLOCKS, SLOTS, EARLY_SLOTS, scatter_parts[:5], outs, scatter_parts[5:])
    vector_scatter = Scatter(place, lambda step, shard: tiles.at[shard], 1, 1, 1, vector_parts[:5], [vector_out], vector_parts[5:])

    def done(step):
        copies[step].start()
        if step + 1 >= STAGED and step + 1 < BLOCKS:
            copies[step + 1 - STAGED].wait()

    run_scatter(scatter, vector_scatter, fill, done)

    @pl.when(first)
    def _():
        for part in parts:
            forward(part).wait_send()

    @pl.when(second)
    def _():
        for part in parts:
            backward(part).wait_send()

    for copy in copies[BLOCKS - STAGED :] + [out_copy, grad_copy]:
        copy.wait()


def finish_kernel(core, tile, *refs):
    sources, targets, rest = refs[:6], refs[6:12], refs[12:]
    magnitudes, joint_bias, expand_bias, narrow = rest[0], rest[1], rest[2], rest[3:-7]
    held, sems = rest[-7:-1], rest[-1]
    loads = [pltpu.make_async_copy(source, buffer, sems.at[0, i]) for i, (source, buffer) in enumerate(zip(sources, held))]
    copies = [pltpu.make_async_copy(buffer, target, sems.at[1, i]) for i, (buffer, target) in enumerate(zip(held, targets))]
    for load in loads:
        load.start()
    halves = jnp.where(core[0] == 0, tile[:NARROW, :HEAD_DIM], tile[:NARROW, HEAD_DIM:])
    for i, ref in enumerate(narrow):
        ref[...] = halves[i : i + 1]
    figures = tile[FIGURES : FIGURES + 1, :]
    magnitudes[...] = jnp.sqrt(figures[:, :3] / (figures[:, 3:4] * sources[0].shape[1]))
    joint_bias[...] = tile[NARROW : NARROW + 1, :]
    for part in range(2):
        expand_bias[:, part * LANES : (part + 1) * LANES] = tile[NARROW + 1 + part : NARROW + 2 + part, :]
    for load, copy in zip(loads, copies):
        load.wait()
        copy.start()
    for copy in copies:
        copy.wait()


def relay_local(depth, tokens, lengths, *parameters):
    cotangent, own = parameters[-1], Params(*parameters[:-1])
    micro, rows, width = tokens.shape
    sequences = lengths.shape[1] * micro
    count = micro * rows
    core = lax.axis_index("batch") % 2

    narrow = jnp.concatenate([
        own.norm_gain, own.norm_bias, own.output_bias, own.sandwich_gain, own.sandwich_bias, own.second_gain,
        own.second_bias, own.reduce_bias, own.closing_gain, own.closing_bias]).astype(F32)
    zero = jnp.zeros_like(narrow)
    narrow = jnp.where(core == 0, jnp.concatenate([narrow, zero], axis=1), jnp.concatenate([zero, narrow], axis=1))
    vectors = jnp.concatenate([
        narrow, own.joint_bias.astype(F32), own.expand_bias.astype(F32).reshape(2, LANES),
        jnp.zeros((VECTOR_ROWS - NARROW - 3, LANES), F32)])

    low, high, rate = (pltpu.VMEM((count, width), BF), pltpu.VMEM((count, width), F32), pltpu.VMEM((count, 1), F32))
    wide = pltpu.VMEM((4, count, width), BF)
    shards = 4 * depth
    dma = pltpu.SemaphoreType.DMA
    vmem, anywhere = pl.BlockSpec(memory_space=pltpu.VMEM), pl.BlockSpec(memory_space=pl.ANY)
    shapes = [
        jax.ShapeDtypeStruct((count, width), BF), jax.ShapeDtypeStruct((count, width), F32),
        jax.ShapeDtypeStruct((PART, 3 * width), F32), jax.ShapeDtypeStruct((PART, width), F32),
        jax.ShapeDtypeStruct((PART, 4 * width), F32), jax.ShapeDtypeStruct((4 * PART, width), F32)]
    slots = rows // lengths.shape[1]
    results = pl.pallas_call(
        functools.partial(relay_kernel, depth),
        out_shape=shapes + [jax.ShapeDtypeStruct((VECTOR_ROWS, LANES), F32)],
        in_specs=[pl.BlockSpec(memory_space=pltpu.SMEM)] + [anywhere] * 7,
        out_specs=[anywhere] * 6 + [vmem],
        scratch_shapes=[
            pltpu.VMEM((BLOCKS, width, width), BF), pltpu.VMEM((shards, VECTOR_ROWS, LANES), F32),
            pltpu.VMEM((VECTOR_ROWS, width), F32), pltpu.VMEM((VECTOR_ROWS, width), F32), pltpu.VMEM((8, width), F32),
            low, low, low, low, low, pltpu.VMEM((sequences * width // LANES, 2 * slots, slots), BF), low,
            high, rate, high, rate, high, rate, high, rate,
            high, low, wide, wide, low, low, low, high, low, pltpu.VMEM((STAGED, PART, width), F32), low,
            dma((2, 2, sequences)), dma((BLOCKS + 4,)),
        ] + gather_sems(depth) + scatter_scratch(depth, SLOTS, EARLY_SLOTS, PART, width, BF) + scatter_scratch(depth, 1, 1, VECTOR_ROWS, LANES, F32),
        compiler_params=pltpu.CompilerParams(collective_id=1, has_side_effects=True, vmem_limit_bytes=VMEM_LIMIT),
        cost_estimate=pl.CostEstimate(flops=6 * count * BLOCKS * width * width, bytes_accessed=2 * BLOCKS * width * width, transcendentals=0),
        name="relay",
    )(lengths.reshape(-1), tokens.reshape(count, width), cotangent.reshape(count, width),
      own.joint_weight[0], own.output_weight[0], own.expand_weight[0], own.reduce_weight[0], vectors)

    vector = jax.ShapeDtypeStruct((1, HEAD_DIM), F32)
    small = [jax.ShapeDtypeStruct((1, 3), F32), jax.ShapeDtypeStruct((1, LANES), F32),
             jax.ShapeDtypeStruct((1, 2 * LANES), F32)] + [vector] * NARROW
    final = pl.pallas_call(
        finish_kernel,
        out_shape=shapes + small,
        in_specs=[pl.BlockSpec(memory_space=pltpu.SMEM), vmem] + [anywhere] * 6,
        out_specs=[anywhere] * 6 + [vmem] * len(small),
        scratch_shapes=[pltpu.VMEM(s.shape, s.dtype) for s in shapes] + [dma((2, 6))],
        compiler_params=pltpu.CompilerParams(vmem_limit_bytes=VMEM_LIMIT),
        name="finish",
    )(core.reshape(1), results[6], *results[:6])
    section_out, section_grad, joint, output, expand, reduce, magnitudes, joint_bias, expand_bias = final[:9]
    narrow = final[9:]
    grads = Params(
        norm_gain=narrow[NORM_GAIN], norm_bias=narrow[NORM_BIAS], joint_weight=joint[None],
        joint_bias=joint_bias, output_weight=output[None], output_bias=narrow[OUTPUT_BIAS],
        sandwich_gain=narrow[SANDWICH_GAIN], sandwich_bias=narrow[SANDWICH_BIAS], second_gain=narrow[SECOND_GAIN],
        second_bias=narrow[SECOND_BIAS], expand_weight=expand[None],
        expand_bias=expand_bias, reduce_weight=reduce[None],
        reduce_bias=narrow[REDUCE_BIAS], closing_gain=narrow[CLOSING_GAIN], closing_bias=narrow[CLOSING_BIAS])
    shape = (1, micro, rows, width)
    return (section_out.reshape(shape), section_grad.reshape(shape), magnitudes) + tuple(grads)


def solution(mesh):
    vector, matrix = P("section", "batch"), P("section", "batch", None)
    kinds = tuple(matrix if i in MATRICES else vector for i in range(16))
    rows = P(None, "batch", None)
    stacked = P("section", None, "batch", None)
    devices = mesh.shape["batch"]
    body = functools.partial(relay_local, devices // 4) if devices == 16 else plain_local
    return jax.shard_map(
        body,
        mesh=mesh,
        in_specs=(rows, P(None, "batch")) + kinds + (rows,),
        out_specs=(stacked, stacked, P("section", None)) + kinds,
        check_vma=False,
    )
```

```python
import functools
import math
from typing import Any, NamedTuple

import jax
import jax.numpy as jnp
from jax import lax
from jax.experimental import pallas as pl
from jax.experimental.pallas import tpu as pltpu
from jax.sharding import PartitionSpec as P

HEADS = 16
HEAD_DIM = 64
EPSILON = 1e-05
RELAX = 32.0
MASKED = -1000000000.0
QUERY_SCALE = 1.0 / (RELAX * math.sqrt(HEAD_DIM))

BF = jnp.bfloat16
F32 = jnp.float32
VMEM_LIMIT = 62 * 2**20

class Params(NamedTuple):
    norm_gain: Any
    norm_bias: Any
    joint_weight: Any
    joint_bias: Any
    output_weight: Any
    output_bias: Any
    sandwich_gain: Any
    sandwich_bias: Any
    second_gain: Any
    second_bias: Any
    expand_weight: Any
    expand_bias: Any
    reduce_weight: Any
    reduce_bias: Any
    closing_gain: Any
    closing_bias: Any


MATRICES = (2, 4, 10, 12)
VECTORS = tuple(i for i in range(16) if i not in MATRICES)


class Kept(NamedTuple):
    n1: Any
    r1: Any
    a: Any
    qh: Any
    kh: Any
    vh: Any
    probs: Any
    o: Any
    y: Any
    ny: Any
    ry: Any
    nm: Any
    rm: Any
    c: Any
    f: Any
    g: Any
    e: Any
    ne: Any
    re: Any
    out: Any


def dot(left, right, left_dim, right_dim):
    return lax.dot_general(left, right, (((left_dim,), (right_dim,)), ((), ())), preferred_element_type=F32)


def norm_parts(value):
    center = jnp.mean(value, axis=-1, keepdims=True)
    centered = value - center
    rate = lax.rsqrt(jnp.mean(centered * centered, axis=-1, keepdims=True) + EPSILON)
    return centered * rate, rate


def norm_back(grad, normal, rate, gain):
    scaled = grad * gain
    first = jnp.mean(scaled, axis=-1, keepdims=True)
    second = jnp.mean(scaled * normal, axis=-1, keepdims=True)
    gain_grad = jnp.sum(grad * normal, axis=0)
    bias_grad = jnp.sum(grad, axis=0)
    return rate * (scaled - first - normal * second), gain_grad, bias_grad


def heads_of(flat, sequences):
    return flat.reshape(sequences, flat.shape[0] // sequences, HEADS, HEAD_DIM)


def layer_fore(hidden_in, w, lengths):
    sequences = lengths.shape[0]
    model = hidden_in.shape[1]
    hidden = hidden_in.astype(F32)
    n1, r1 = norm_parts(hidden)
    a = (n1 * w.norm_gain + w.norm_bias).astype(BF)
    mixed = dot(a, w.joint_weight, 1, 0)
    q = ((mixed[:, :model] + w.joint_bias[:model]) * QUERY_SCALE).astype(BF)
    k = mixed[:, model : 2 * model].astype(BF)
    v = (mixed[:, 2 * model :] + w.joint_bias[model:]).astype(BF)
    qh, kh, vh = heads_of(q, sequences), heads_of(k, sequences), heads_of(v, sequences)
    scores = jnp.einsum("bqhd,bkhd->bhqk", qh, kh, preferred_element_type=F32)
    slots = scores.shape[-1]
    query_slot = lax.broadcasted_iota(jnp.int32, (sequences, slots, slots), 1)
    key_slot = lax.broadcasted_iota(jnp.int32, (sequences, slots, slots), 2)
    seen = (key_slot <= query_slot) & (key_slot < lengths[:, None, None])
    scores = jnp.where(seen[:, None], scores, MASKED)
    exponent = jnp.exp(RELAX * (scores - jnp.max(scores, axis=-1, keepdims=True)))
    probs = exponent / jnp.sum(exponent, axis=-1, keepdims=True)
    o = jnp.einsum("bhqk,bkhd->bqhd", probs.astype(BF), vh, preferred_element_type=F32)
    o = o.reshape(hidden.shape).astype(BF)
    y = dot(o, w.output_weight, 1, 0) + w.output_bias
    ny, ry = norm_parts(y)
    mid = hidden + ny * w.sandwich_gain + w.sandwich_bias
    nm, rm = norm_parts(mid)
    c = (nm * w.second_gain + w.second_bias).astype(BF)
    f = dot(c, w.expand_weight, 1, 0) + w.expand_bias
    g = jax.nn.gelu(f).astype(BF)
    e = dot(g, w.reduce_weight, 1, 0) + w.reduce_bias
    ne, re = norm_parts(e)
    out = mid + ne * w.closing_gain + w.closing_bias
    return out, Kept(n1, r1, a, qh, kh, vh, probs, o, y, ny, ry, nm, rm, c, f, g, e, ne, re, out)


def layer_back(dout, w, s, want_weights):
    sequences = s.qh.shape[0]
    de, closing_gain, closing_bias = norm_back(dout, s.ne, s.re, w.closing_gain)
    de = de.astype(BF)
    dg = dot(de, w.reduce_weight, 1, 1)
    df = jax.vjp(jax.nn.gelu, s.f)[1](dg)[0].astype(BF)
    dc = dot(df, w.expand_weight, 1, 1)
    dmid, second_gain, second_bias = norm_back(dc, s.nm, s.rm, w.second_gain)
    dmid = dmid + dout
    dy, sandwich_gain, sandwich_bias = norm_back(dmid, s.ny, s.ry, w.sandwich_gain)
    dy = dy.astype(BF)
    do = heads_of(dot(dy, w.output_weight, 1, 1).astype(BF), sequences)
    dprobs = jnp.einsum("bqhd,bkhd->bhqk", do, s.vh, preferred_element_type=F32)
    dv = jnp.einsum("bhqk,bqhd->bkhd", s.probs.astype(BF), do, preferred_element_type=F32)
    ds = RELAX * s.probs * (dprobs - jnp.sum(dprobs * s.probs, axis=-1, keepdims=True))
    ds = ds.astype(BF)
    dq = jnp.einsum("bhqk,bkhd->bqhd", ds, s.kh, preferred_element_type=F32)
    dk = jnp.einsum("bhqk,bqhd->bkhd", ds, s.qh, preferred_element_type=F32)
    flat = dout.shape
    dmixed = jnp.concatenate([dq.reshape(flat) * QUERY_SCALE, dk.reshape(flat), dv.reshape(flat)], axis=1).astype(BF)
    da = dot(dmixed, w.joint_weight, 1, 1)
    dh, norm_gain, norm_bias = norm_back(da, s.n1, s.r1, w.norm_gain)
    din = dmid + dh
    if not want_weights:
        return din, None
    model = flat[1]
    sums = jnp.sum(dmixed.astype(F32), axis=0)
    return din, Params(
        norm_gain=norm_gain,
        norm_bias=norm_bias,
        joint_weight=dot(s.a, dmixed, 0, 0),
        joint_bias=jnp.concatenate([sums[:model], sums[2 * model :]]),
        output_weight=dot(s.o, dy, 0, 0),
        output_bias=jnp.sum(dy.astype(F32), axis=0),
        sandwich_gain=sandwich_gain,
        sandwich_bias=sandwich_bias,
        second_gain=second_gain,
        second_bias=second_bias,
        expand_weight=dot(s.c, df, 0, 0),
        expand_bias=jnp.sum(df.astype(F32), axis=0),
        reduce_weight=dot(s.g, de, 0, 0),
        reduce_bias=jnp.sum(de.astype(F32), axis=0),
        closing_gain=closing_gain,
        closing_bias=closing_bias,
    )


def passed_along(block, axis, distance):
    devices = range(lax.axis_size(axis))
    route = [(i - distance, i) for i in devices if i - distance in devices]
    return lax.ppermute(block, axis, route)


def plain_local(tokens, lengths, *parameters):
    cotangent = parameters[-1]
    own = parameters[:-1]
    section = lax.axis_index("section")
    micro, rows, model = tokens.shape
    sequences = lengths.shape[1]
    slots = rows // sequences
    total_rows = micro * rows

    packed = jnp.concatenate([own[i] for i in VECTORS], axis=1)
    packed = lax.all_gather(packed, "batch", axis=0, tiled=True).astype(F32)
    w = list(own)
    start = 0
    for i in VECTORS:
        width = own[i].shape[1]
        w[i] = packed[:, start : start + width].reshape(-1)
        start += width
    for i, whole in zip(MATRICES, plain_gather([own[i] for i in MATRICES])):
        w[i] = whole
    w = Params(*w)

    flat_lengths = lengths.reshape(-1)
    seen = lax.broadcasted_iota(jnp.int32, (micro * sequences, slots), 1) < flat_lengths[:, None]
    valid = seen.astype(F32).reshape(total_rows, 1)
    source = tokens.reshape(total_rows, model)
    first_out, _ = layer_fore(source, w, flat_lengths)
    incoming = passed_along(first_out.astype(BF), "section", 1)
    out, s = layer_fore(jnp.where(section == 0, source, incoming), w, flat_lengths)
    section_out = out.astype(BF).reshape(1, micro, rows, model)
    squares = jnp.stack([jnp.sum(part * part * valid) for part in (s.y, s.e, s.out)])

    seed = cotangent.reshape(total_rows, model).astype(F32) * valid
    last_in, _ = layer_back(seed, w, s, False)
    incoming = passed_along(last_in.astype(BF), "section", -1)
    din, grads = layer_back(jnp.where(section == 1, seed, incoming.astype(F32)), w, s, True)
    section_grad = din.reshape(1, micro, rows, model)

    result = list(grads)
    for i, part in zip(MATRICES, plain_scatter([grads[i].astype(BF) for i in MATRICES])):
        result[i] = part
    devices = lax.axis_size("batch")
    small = jnp.concatenate([grads[i].reshape(devices, -1) for i in VECTORS], axis=1)
    small = lax.psum_scatter(small, "batch", scatter_dimension=0, tiled=True)
    start = 0
    for i in VECTORS:
        width = own[i].shape[1]
        result[i] = small[:, start : start + width]
        start += width
    count = jnp.sum(lengths).astype(F32)
    square_all, count_all = lax.psum((squares, count), "batch")
    magnitudes = jnp.sqrt(square_all / (count_all * model))[None]
    return (section_out, section_grad, magnitudes) + tuple(result)


def plain_gather(shards):
    return [lax.all_gather(w, "batch", axis=1, tiled=True)[0] for w in shards]


def plain_scatter(grads):
    return [lax.psum_scatter(g[None], "batch", scatter_dimension=1, tiled=True).astype(F32) for g in grads]


MESH = pl.DeviceIdType.MESH
BLOCKS = 12
VECTOR_ITEM = 12
PART = 64
SLOTS, EARLY_SLOTS = 5, 3
CROSS = 16
LAGS = (1, 2, 3, 4, 5)
GATHER_ORDER = (VECTOR_ITEM,) + tuple(range(BLOCKS))
GATHER_CROSSED = (3, 11)
GATHER_AHEAD = 4
SIDE_LAG, REST_LAG = 2, 3
SCATTER_ORDER = (8, 9, 10, 11, 4, 5, 6, 7, 3, 0, 1, 2)
UP, DOWN, SIDE = 0, 1, 2


def when(condition, action):
    if condition is True:
        action()
    else:
        pl.when(condition)(action)


def both(first, second):
    if first is True:
        return second
    if second is True:
        return first
    return first & second


class Place:
    def __init__(self, depth):
        index = lax.axis_index("batch")
        self.s = lax.axis_index("section")
        self.depth = depth
        self.z = index // 4
        self.x = (index // 2) % 2
        self.c = index % 2

    def device(self, z, x, c):
        return (self.s, (z * 2 + x) * 2 + c)

    def shard(self, z, x, c):
        return (z * 2 + x) * 2 + c

    def me(self):
        return self.shard(self.z, self.x, self.c)

    def across(self):
        return (1 - self.s, self.me())

    def greet(self):
        z, x, c = self.z, self.x, self.c
        sem = pltpu.get_barrier_semaphore()

        def signal(device):
            pl.semaphore_signal(sem, inc=1, device_id=device, device_id_type=MESH)

        signal(self.device(z, 1 - x, c))
        signal(self.device(z, x, 1 - c))
        signal(self.across())
        pl.when(z < self.depth - 1)(lambda: signal(self.device(z + 1, x, c)))
        pl.when(z > 0)(lambda: signal(self.device(z - 1, x, c)))
        chain = (z < self.depth - 1).astype(jnp.int32) + (z > 0).astype(jnp.int32)
        pl.semaphore_wait(sem, 3 + chain)


def spot(item, shard):
    if item < 8:
        return item, pl.multiple_of(shard * PART, 16)
    return 8 + shard // 4, pl.multiple_of((shard % 4) * 4 * PART + (item - 8) * PART, 16)


def shard_view(refs, item, width):
    joint, output, expand, reduce, vectors = refs
    if item < 3:
        return joint.at[:, pl.ds(item * width, width)]
    if item == 3:
        return output
    if item < 8:
        return expand.at[:, pl.ds((item - 4) * width, width)]
    if item < VECTOR_ITEM:
        return reduce.at[pl.ds((item - 8) * PART, PART)]
    return vectors


class Gather:
    def __init__(self, place, own, store, vectors, sems):
        self.p, self.own, self.store, self.vectors = place, own, store, vectors
        self.send, self.share, self.recv, self.local = sems
        self.sent = []

    def at(self, item, shard):
        if item == VECTOR_ITEM:
            return self.vectors.at[shard]
        block, row = spot(item, shard)
        return self.store.at[block, pl.ds(row, PART)]

    def copy(self, item, shard, way, first=False):
        p = self.p
        target = self.at(item, shard)
        source = shard_view(self.own, item, self.store.shape[2]) if first else target
        recv = self.recv.at[item, shard]
        if way is None:
            send, device = self.share.at[item, shard // 2], p.device(p.z, p.x, 1 - p.c)
        else:
            send = self.send.at[item, shard // 2, way]
            device = (p.device(p.z + 1, p.x, p.c), p.device(p.z - 1, p.x, p.c), p.device(p.z, 1 - p.x, p.c))[way]
        return pltpu.make_async_remote_copy(source, target, send, recv, device_id=device, device_id_type=MESH)

    def go(self, item, shard, way, condition, first=False):
        self.sent.append((item, shard, way, condition, first))
        when(condition, lambda: self.copy(item, shard, way, first).start())

    def arrived(self, item, shard):
        self.copy(item, shard, None).wait_recv()

    def keep_own(self):
        me = self.p.me()
        copies = [
            pltpu.make_async_copy(shard_view(self.own, item, self.store.shape[2]), self.at(item, me), self.local.at[item])
            for item in range(BLOCKS + 1)
        ]
        for copy in copies:
            copy.start()
        return copies

    def own_sends(self, item):
        p = self.p
        self.go(item, p.me(), UP, p.z < p.depth - 1, True)
        self.go(item, p.me(), DOWN, p.z > 0, True)
        self.go(item, p.me(), SIDE, True, True)
        self.go(item, p.me(), None, True, True)

    def chain_round(self, item, hop):
        p = self.p
        crossed = item in GATHER_CROSSED
        for x in (p.x, 1 - p.x) if crossed else (p.x,):
            for origin, present, way, onward in (
                (p.z - hop, p.z >= hop, UP, p.z < p.depth - 1),
                (p.z + hop, p.z + hop < p.depth, DOWN, p.z > 0),
            ):
                shard = p.shard(origin, x, p.c)
                when(present, lambda: self.arrived(item, shard))
                self.go(item, shard, way, both(present, onward))
                if not crossed:
                    self.go(item, shard, SIDE, present)
                self.go(item, shard, None, present)

    def side_own(self, item):
        p = self.p
        shard = p.shard(p.z, 1 - p.x, p.c)
        self.arrived(item, shard)
        if item in GATHER_CROSSED:
            self.go(item, shard, UP, p.z < p.depth - 1)
            self.go(item, shard, DOWN, p.z > 0)
        self.go(item, shard, None, True)

    def side_round(self, item, hop):
        p = self.p
        if item in GATHER_CROSSED:
            return
        for origin, present in ((p.z - hop, p.z >= hop), (p.z + hop, p.z + hop < p.depth)):
            shard = p.shard(origin, 1 - p.x, p.c)
            when(present, lambda: self.arrived(item, shard))
            self.go(item, shard, None, present)

    def rest(self, item):
        p = self.p
        for z in range(p.depth):
            for x in range(2):
                self.arrived(item, p.shard(z, x, 1 - p.c))

    def drain(self):
        for item, shard, way, condition, first in self.sent:
            when(condition, lambda: self.copy(item, shard, way, first).wait_send())


def run_gather(gather, ready):
    depth, count = gather.p.depth, len(GATHER_ORDER)
    pending = []
    kept = gather.keep_own()
    for item in GATHER_ORDER[:GATHER_AHEAD]:
        gather.own_sends(item)

    def sides(item):
        for hop in range(1, depth):
            gather.side_round(item, hop)

    def finish(item):
        gather.rest(item)
        kept[item].wait()
        pending.extend(ready(item))

    for place, item in enumerate(GATHER_ORDER):
        if item in GATHER_CROSSED:
            gather.side_own(item)
        for hop in range(1, depth):
            gather.chain_round(item, hop)
            if hop == 1:
                if place + GATHER_AHEAD < count:
                    gather.own_sends(GATHER_ORDER[place + GATHER_AHEAD])
                if item not in GATHER_CROSSED:
                    gather.side_own(item)
            if pending:
                pending.pop(0)()
        if place >= SIDE_LAG:
            sides(GATHER_ORDER[place - SIDE_LAG])
        if place >= REST_LAG:
            finish(GATHER_ORDER[place - REST_LAG])
    for item in GATHER_ORDER[count - SIDE_LAG :]:
        sides(item)
    for item in GATHER_ORDER[count - REST_LAG :]:
        finish(item)
        while pending:
            pending.pop(0)()


def gather_sems(depth):
    kind, items = pltpu.SemaphoreType.DMA, BLOCKS + 1
    return [kind((items, 2 * depth, 3)), kind((items, 2 * depth)), kind((items, 4 * depth)), kind((items,))]


def total(*refs):
    value = refs[0][...].astype(F32)
    for ref in refs[1:]:
        value = value + ref[...].astype(F32)
    return value


def crossing(step, rows):
    return 0 if rows <= CROSS or step % 3 == 2 else CROSS


class Scatter:
    def __init__(self, place, part, count, slots, early, buffers, outs, sems, first_part=lambda z: None):
        self.first_part = first_part
        self.p, self.part, self.count, self.slots, self.early, self.outs = place, part, count, slots, early, outs
        self.core_in, self.side_in, self.chain_in, self.cross_in, self.last_in = buffers
        (self.core_send, self.core_recv, self.side_send, self.side_recv, self.chain_send, self.chain_recv,
         self.cross_send, self.cross_recv, self.last_send, self.last_recv,
         self.core_free, self.side_free, self.chain_free) = sems
        depth = place.depth
        self.rows = self.core_in.shape[2]
        self.origins = [q for pair in zip(range(depth - 1, -1, -1), range(depth)) for q in pair][:depth]

    def main(self, step):
        return pl.ds(0, self.rows - crossing(step, self.rows))

    def tail(self, step):
        cut = crossing(step, self.rows)
        return pl.ds(self.rows - cut, cut)

    def mine(self, step, z, x, c):
        return self.part(step, self.p.shard(z, x, c))

    def core_copy(self, step, z, x):
        p, slot = self.p, step % self.early
        return pltpu.make_async_remote_copy(
            self.mine(step, z, x, 1 - p.c), self.core_in.at[slot, z * 2 + x],
            self.core_send.at[slot, z * 2 + x], self.core_recv.at[slot, z * 2 + x],
            device_id=p.device(p.z, p.x, 1 - p.c), device_id_type=MESH)

    def side_copy(self, step, z):
        p, slot, rows = self.p, step % self.early, self.main(step)
        return pltpu.make_async_remote_copy(
            self.mine(step, z, 1 - p.x, p.c).at[rows], self.side_in.at[slot, z, rows],
            self.side_send.at[slot, z], self.side_recv.at[slot, z],
            device_id=p.device(p.z, 1 - p.x, p.c), device_id_type=MESH)

    def chain_copy(self, step, z, up):
        p, slot = self.p, step % self.slots
        return pltpu.make_async_remote_copy(
            self.mine(step, z, p.x, p.c), self.chain_in.at[slot, 1 - up, z],
            self.chain_send.at[slot, 1 - up, z], self.chain_recv.at[slot, 1 - up, z],
            device_id=p.device(p.z + 2 * up - 1, p.x, p.c), device_id_type=MESH)

    def cross_copy(self, step, z, up):
        p, slot, rows = self.p, step % self.slots, self.tail(step)
        return pltpu.make_async_remote_copy(
            self.mine(step, z, 1 - p.x, p.c).at[rows], self.cross_in.at[slot, 1 - up, z, pl.ds(0, rows.size)],
            self.cross_send.at[slot, 1 - up, z], self.cross_recv.at[slot, 1 - up, z],
            device_id=p.device(p.z + 2 * up - 1, p.x, p.c), device_id_type=MESH)

    def last_copy(self, step):
        p, slot, rows = self.p, step % self.slots, self.tail(step)
        return pltpu.make_async_remote_copy(
            self.mine(step, p.z, 1 - p.x, p.c).at[rows], self.last_in.at[slot, pl.ds(0, rows.size)],
            self.last_send.at[slot], self.last_recv.at[slot],
            device_id=p.device(p.z, 1 - p.x, p.c), device_id_type=MESH)

    def core_stage(self, step):
        p = self.p
        if step >= self.early:
            self.core_drain(step - self.early)
            pl.semaphore_wait(self.core_free, 1)
        if step == 0:
            for z in self.origins:
                self.first_part(z)
                for x in range(2):
                    self.core_copy(step, z, x).start()
            return
        for x in (1 - p.x, p.x):
            for z in self.origins:
                self.core_copy(step, z, x).start()

    def core_drain(self, step):
        for z in self.origins:
            for x in range(2):
                self.core_copy(step, z, x).wait_send()

    def from_core(self, step, z, x):
        self.core_copy(step, z, x).wait_recv()
        return self.core_in.at[step % self.early, z * 2 + x]

    def side_stage(self, step):
        p = self.p
        if step >= self.early:
            self.side_drain(step - self.early)
            pl.semaphore_wait(self.side_free, 1)
        for z in self.origins:
            twin = self.from_core(step, z, 1 - p.x)
            mine = self.mine(step, z, 1 - p.x, p.c)
            mine[...] = total(mine, twin).astype(mine.dtype)
            self.side_copy(step, z).start()

    def side_drain(self, step):
        for z in self.origins:
            self.side_copy(step, z).wait_send()

    def ways(self, z):
        p, last = self.p, self.p.depth - 1
        return (p.z < z).astype(jnp.int32), ((p.z < z) & (p.z > 0)) | ((p.z > z) & (p.z < last))

    def chain_stage(self, step, near):
        p, slot, last = self.p, step % self.slots, self.p.depth - 1
        cut = crossing(step, self.rows)
        if near and step >= self.slots:
            self.chain_drain(step - self.slots)
            pl.when(p.z < last)(lambda: pl.semaphore_wait(self.chain_free.at[0], 1))
            pl.when(p.z > 0)(lambda: pl.semaphore_wait(self.chain_free.at[1], 1))
        for z in self.origins:
            up, fed = self.ways(z)
            begun = jnp.where(p.z < z, p.z, last - p.z)
            if near:
                self.sum_side(step, z)

            @pl.when((p.z != z) & ((begun <= 1) if near else (begun > 1)))
            def _():
                mine = self.mine(step, z, p.x, p.c)
                other = self.mine(step, z, 1 - p.x, p.c)

                @pl.when(fed)
                def _():
                    self.chain_copy(step, z, up).wait_recv()
                    mine[...] = total(mine, self.chain_in.at[slot, 1 - up, z]).astype(mine.dtype)

                self.chain_copy(step, z, up).start()
                if cut:
                    @pl.when(fed)
                    def _():
                        self.cross_copy(step, z, up).wait_recv()
                        here = other.at[self.tail(step)]
                        here[...] = total(here, self.cross_in.at[slot, 1 - up, z, pl.ds(0, cut)]).astype(here.dtype)

                    self.cross_copy(step, z, up).start()
        if near and step + self.early < self.count:
            self.signal(self.core_free, p.device(p.z, p.x, 1 - p.c))
            self.signal(self.side_free, p.device(p.z, 1 - p.x, p.c))

    @staticmethod
    def signal(sem, device):
        pl.semaphore_signal(sem, inc=1, device_id=device, device_id_type=MESH)

    def sum_side(self, step, z):
        p, main = self.p, self.main(step)
        mine, twin = self.mine(step, z, p.x, p.c), self.from_core(step, z, p.x)
        self.side_copy(step, z).wait_recv()
        here = mine.at[main]
        here[...] = total(here, twin.at[main], self.side_in.at[step % self.early, z, main]).astype(mine.dtype)
        if crossing(step, self.rows):
            here = mine.at[self.tail(step)]
            here[...] = total(here, twin.at[self.tail(step)]).astype(mine.dtype)

    def chain_drain(self, step):
        p = self.p
        for z in self.origins:
            up, _ = self.ways(z)

            @pl.when(p.z != z)
            def _():
                self.chain_copy(step, z, up).wait_send()
                if crossing(step, self.rows):
                    self.cross_copy(step, z, up).wait_send()
        if crossing(step, self.rows):
            self.last_copy(step).wait_send()

    def incoming(self, copy):
        p = self.p
        pl.when(p.z > 0)(lambda: copy(1).wait_recv())
        pl.when(p.z < p.depth - 1)(lambda: copy(0).wait_recv())

    def outcome(self, put, parts, below, above):
        p, last = self.p, self.p.depth - 1
        pl.when(p.z == 0)(lambda: put(*parts, above))
        pl.when(p.z == last)(lambda: put(*parts, below))
        pl.when((p.z > 0) & (p.z < last))(lambda: put(*parts, below, above))

    def last_stage(self, step):
        p, slot, cut = self.p, step % self.slots, crossing(step, self.rows)
        if not cut:
            return
        self.incoming(lambda up: self.cross_copy(step, p.z, up))
        here = self.mine(step, p.z, 1 - p.x, p.c).at[self.tail(step)]

        def put(*refs):
            here[...] = total(*refs).astype(here.dtype)

        self.outcome(put, [here], *(self.cross_in.at[slot, way, p.z, pl.ds(0, cut)] for way in range(2)))
        self.last_copy(step).start()

    def own_stage(self, step):
        p, slot, last, cut = self.p, step % self.slots, self.p.depth - 1, crossing(step, self.rows)
        self.incoming(lambda up: self.chain_copy(step, p.z, up))
        mine, out = self.mine(step, p.z, p.x, p.c), self.outs[step]
        if cut:
            self.last_copy(step).wait_recv()
        for rows, extra in ((self.main(step), []), (self.tail(step), [self.last_in.at[slot, pl.ds(0, cut)]] if cut else None)):
            if extra is None:
                continue

            def put(*refs):
                out[rows] = total(*refs)

            self.outcome(put, [mine.at[rows]] + extra, *(self.chain_in.at[slot, way, p.z, rows] for way in range(2)))
        if step + self.slots < self.count:
            pl.when(p.z > 0)(lambda: self.signal(self.chain_free.at[0], p.device(p.z - 1, p.x, p.c)))
            pl.when(p.z < last)(lambda: self.signal(self.chain_free.at[1], p.device(p.z + 1, p.x, p.c)))

    def drain(self):
        for step in range(self.count - self.early, self.count):
            self.core_drain(step)
            self.side_drain(step)
        for step in range(self.count - self.slots, self.count):
            self.chain_drain(step)


def run_scatter(scatter, vector_scatter, ready, beside, done):
    side_lag, near_lag, far_lag, last_lag, own_lag = LAGS
    for tick in range(BLOCKS + own_lag):
        if tick < BLOCKS:
            ready(tick)
        if tick >= own_lag:
            scatter.own_stage(tick - own_lag)
            done(tick - own_lag)
        if 0 <= tick - last_lag < BLOCKS:
            scatter.last_stage(tick - last_lag)
        if tick < BLOCKS:
            scatter.core_stage(tick)
        if 0 <= tick - side_lag < BLOCKS:
            scatter.side_stage(tick - side_lag)
        if 0 <= tick - far_lag < BLOCKS:
            scatter.chain_stage(tick - far_lag, False)
        beside(tick)
        if 0 <= tick - near_lag < BLOCKS:
            scatter.chain_stage(tick - near_lag, True)
        if tick == BLOCKS - 1:
            vector_scatter.core_stage(0)
        if tick == BLOCKS:
            vector_scatter.side_stage(0)
        if tick == BLOCKS + 1:
            vector_scatter.chain_stage(0, True)
            vector_scatter.chain_stage(0, False)
    vector_scatter.own_stage(0)
    scatter.drain()
    vector_scatter.drain()


def scatter_scratch(depth, slots, early, rows, width, dtype):
    dma, plain = pltpu.SemaphoreType.DMA, pltpu.SemaphoreType.REGULAR
    cross = min(CROSS, rows)
    return [
        pltpu.VMEM((early, 2 * depth, rows, width), dtype),
        pltpu.VMEM((early, depth, rows, width), dtype),
        pltpu.VMEM((slots, 2, depth, rows, width), dtype),
        pltpu.VMEM((slots, 2, depth, cross, width), dtype), pltpu.VMEM((slots, cross, width), dtype),
        dma((early, 2 * depth)), dma((early, 2 * depth)), dma((early, depth)), dma((early, depth)),
        dma((slots, 2, depth)), dma((slots, 2, depth)), dma((slots, 2, depth)), dma((slots, 2, depth)),
        dma((slots,)), dma((slots,)), plain, plain, plain((2,)),
    ]


(NORM_GAIN, NORM_BIAS, OUTPUT_BIAS, SANDWICH_GAIN, SANDWICH_BIAS, SECOND_GAIN, SECOND_BIAS, REDUCE_BIAS,
 CLOSING_GAIN, CLOSING_BIAS, QUERY_BIAS, VALUE_BIAS, EXPAND_BIAS) = range(13)
NARROW = 10
VECTOR_ROWS = 16
FIGURES = 13
LANES = 128
TILE = 256
STAGED = 3
CHUNK = 64
CURVE = math.sqrt(2.0 / math.pi)
BEND = 0.044715


class Work(NamedTuple):
    vec: Any
    dvec: Any
    h: Any
    a: Any
    q: Any
    k: Any
    v: Any
    p: Any
    o: Any
    n_h: Any
    r_h: Any
    n_y: Any
    r_y: Any
    n_m: Any
    r_m: Any
    n_e: Any
    r_e: Any
    mid: Any
    c: Any
    g: Any
    slope: Any
    de: Any
    dy: Any
    do: Any
    din: Any
    sums: Any


def mxu(left, right, left_dim, right_dim):
    return lax.dot_general(left, right, (((left_dim,), (right_dim,)), ((), ())), preferred_element_type=F32)


def mean_of(value):
    return jnp.mean(value, axis=-1, keepdims=True)


def norm_of(value):
    centered = value - mean_of(value)
    rate = lax.rsqrt(mean_of(centered * centered) + EPSILON)
    return centered * rate, rate


def norm_pull(grad, normal, rate, gain):
    scaled = grad * gain
    return rate * (scaled - mean_of(scaled) - normal * mean_of(scaled * normal))


def column_sum(value):
    return jnp.sum(value, axis=0, keepdims=True)


class Layer:
    def __init__(self, work, store, lengths, swift=True):
        self.w, self.store, self.lengths, self.swift = work, store, lengths, swift
        self.tokens, self.width = work.h.shape
        self.sequences = lengths.shape[0]
        self.slots = self.tokens // self.sequences

    def row(self, index):
        return self.w.vec[index : index + 1, :]

    def add(self, index, value):
        self.w.dvec[index : index + 1, :] += value

    def chunks(self, body, first=0, last=None):
        last = self.tokens if last is None else last

        def step(i, carry):
            body(pl.ds(pl.multiple_of(i * CHUNK, CHUNK), CHUNK), i)
            return carry

        lax.fori_loop(first // CHUNK, last // CHUNK, step, 0)

    def tiles(self, body):
        def step(i, carry):
            body(pl.ds(pl.multiple_of(i * TILE, TILE), TILE))
            return carry

        lax.fori_loop(0, self.width // TILE, step, 0, unroll=self.swift)

    def valid(self, i):
        per = self.slots // CHUNK
        slot = (i % per) * CHUNK + lax.broadcasted_iota(jnp.int32, (CHUNK, 1), 0)
        return jnp.where(slot < self.lengths[i // per], 1.0, 0.0)


    def fore_start(self, source, first=0, last=None):
        w = self.w

        def body(rows, i):
            h = source[rows, :]
            if source is not w.h:
                w.h[rows, :] = h
            normal, rate = norm_of(h.astype(F32))
            w.n_h[rows, :] = normal
            w.r_h[rows, :] = rate
            w.a[rows, :] = (normal * self.row(NORM_GAIN) + self.row(NORM_BIAS)).astype(BF)

        self.chunks(body, first, last)

    def part(self, index):
        return pl.ds(index * self.slots, self.slots)

    def fore_joint(self, block, rows):
        w = self.w
        bias = (QUERY_BIAS, None, VALUE_BIAS)[block]
        target = (w.q, w.k, w.v)[block]

        def body(tile):
            mixed = mxu(w.a[rows, :], self.store[block, :, tile], 1, 0)
            if bias is not None:
                mixed = mixed + w.vec[bias : bias + 1, tile]
            if block == 0:
                mixed = mixed * QUERY_SCALE
            target[rows, tile] = mixed.astype(BF)

        self.tiles(body)

    def pairs(self, sequence, body):
        count = self.width // LANES
        rows, length = self.part(sequence), self.lengths[sequence]

        def step(i, carry):
            body(rows, pl.ds(pl.multiple_of(i * LANES, LANES), LANES), sequence * count + i, length)
            return carry

        lax.fori_loop(0, count, step, 0, unroll=8 if self.swift else 2)

    def split(self, value):
        low = lax.broadcasted_iota(jnp.int32, value.shape, 1) < HEAD_DIM
        zero = jnp.zeros_like(value)
        return jnp.concatenate([jnp.where(low, value, zero), jnp.where(low, zero, value)], axis=0)

    def merge(self, value):
        low = lax.broadcasted_iota(jnp.int32, (self.slots, LANES), 1) < HEAD_DIM
        return jnp.where(low, value[: self.slots], value[self.slots :])

    def fore_attention(self, sequence):
        w, slots = self.w, self.slots

        def body(rows, lanes, i, length):
            scores = mxu(w.k[rows, lanes], self.split(w.q[rows, lanes]), 1, 1)
            key = lax.broadcasted_iota(jnp.int32, (slots, 2 * slots), 0)
            query = lax.broadcasted_iota(jnp.int32, (slots, 2 * slots), 1) % slots
            scores = jnp.where((key <= query) & (key < length), scores, MASKED)
            weight = jnp.exp(RELAX * (scores - jnp.max(scores, axis=0, keepdims=True)))
            probs = (weight / column_sum(weight)).astype(BF)
            w.p[i] = probs
            w.o[rows, lanes] = self.merge(mxu(probs, w.v[rows, lanes], 0, 0)).astype(BF)

        self.pairs(sequence, body)

    def fore_output(self, rows):
        w = self.w

        def body(tile):
            w.n_y[rows, tile] = mxu(w.o[rows, :], self.store[3, :, tile], 1, 0) + w.vec[OUTPUT_BIAS : OUTPUT_BIAS + 1, tile]

        self.tiles(body)

    def fore_middle(self, first=0, last=None):
        w = self.w

        def middle(rows, i):
            y = w.n_y[rows, :]
            w.sums[0:1, :] += column_sum(y * y * self.valid(i))
            normal, rate = norm_of(y)
            w.n_y[rows, :] = normal
            w.r_y[rows, :] = rate
            mid = w.h[rows, :].astype(F32) + (normal * self.row(SANDWICH_GAIN) + self.row(SANDWICH_BIAS))
            w.mid[rows, :] = mid
            normal, rate = norm_of(mid)
            w.n_m[rows, :] = normal
            w.r_m[rows, :] = rate
            w.c[rows, :] = (normal * self.row(SECOND_GAIN) + self.row(SECOND_BIAS)).astype(BF)

        self.chunks(middle, first, last)

    def fore_expand(self, block, rows):
        w = self.w

        def body(tile):
            f = mxu(w.c[rows, :], self.store[4 + block, :, tile], 1, 0)
            f = f + w.vec[EXPAND_BIAS + block : EXPAND_BIAS + block + 1, tile]
            square = f * f
            bent = jnp.tanh(CURVE * f * (1.0 + BEND * square))
            half = 0.5 * (1.0 + bent)
            w.g[block, rows, tile] = (f * half).astype(BF)
            slope = half + 0.5 * f * (1.0 - bent * bent) * (CURVE * (1.0 + 3.0 * BEND * square))
            w.slope[block, rows, tile] = slope.astype(BF)

        self.tiles(body)

    def fore_reduce(self, rows):
        w = self.w

        def body(tile):
            e = mxu(w.g[0, rows, :], self.store[8, :, tile], 1, 0)
            for block in range(1, 4):
                e = e + mxu(w.g[block, rows, :], self.store[8 + block, :, tile], 1, 0)
            w.n_e[rows, tile] = e + w.vec[REDUCE_BIAS : REDUCE_BIAS + 1, tile]

        self.tiles(body)

    def fore_end(self, target, first=0, last=None):
        w = self.w

        def body(rows, i):
            e = w.n_e[rows, :]
            valid = self.valid(i)
            w.sums[1:2, :] += column_sum(e * e * valid)
            normal, rate = norm_of(e)
            w.n_e[rows, :] = normal
            w.r_e[rows, :] = rate
            out = w.mid[rows, :] + (normal * self.row(CLOSING_GAIN) + self.row(CLOSING_BIAS))
            w.sums[2:3, :] += column_sum(out * out * valid)
            target[rows, :] = out.astype(BF)

        self.chunks(body, first, last)


    def back_start(self, seed, masked, first=0, last=None):
        w = self.w

        def body(rows, i):
            dout = seed[rows, :].astype(F32)
            if masked:
                dout = dout * self.valid(i)
            w.din[rows, :] = dout
            normal = w.n_e[rows, :]
            self.add(CLOSING_GAIN, column_sum(dout * normal))
            self.add(CLOSING_BIAS, column_sum(dout))
            de = norm_pull(dout, normal, w.r_e[rows, :], self.row(CLOSING_GAIN)).astype(BF)
            w.de[rows, :] = de
            self.add(REDUCE_BIAS, column_sum(de.astype(F32)))

        self.chunks(body, first, last)

    def back_reduce(self, block, rows):
        w = self.w

        def body(tile):
            dg = mxu(w.de[rows, :], self.store[8 + block, tile, :], 1, 1)
            df = (dg * w.slope[block, rows, tile].astype(F32)).astype(BF)
            w.slope[block, rows, tile] = df
            w.dvec[EXPAND_BIAS + block : EXPAND_BIAS + block + 1, tile] += column_sum(df.astype(F32))

        self.tiles(body)

    def back_expand(self):
        w = self.w

        def body(tile):
            dc = mxu(w.slope[0], self.store[4, tile, :], 1, 1)
            for block in range(1, 4):
                dc = dc + mxu(w.slope[block], self.store[4 + block, tile, :], 1, 1)
            w.mid[:, tile] = dc

        self.tiles(body)

    def back_middle(self):
        w = self.w

        def middle(rows, i):
            dc = w.mid[rows, :]
            normal = w.n_m[rows, :]
            self.add(SECOND_GAIN, column_sum(dc * normal))
            self.add(SECOND_BIAS, column_sum(dc))
            dmid = w.din[rows, :] + norm_pull(dc, normal, w.r_m[rows, :], self.row(SECOND_GAIN))
            w.din[rows, :] = dmid
            normal = w.n_y[rows, :]
            self.add(SANDWICH_GAIN, column_sum(dmid * normal))
            self.add(SANDWICH_BIAS, column_sum(dmid))
            dy = norm_pull(dmid, normal, w.r_y[rows, :], self.row(SANDWICH_GAIN)).astype(BF)
            w.dy[rows, :] = dy
            self.add(OUTPUT_BIAS, column_sum(dy.astype(F32)))

        self.chunks(middle)

    def back_output(self):
        w = self.w

        def body(tile):
            w.do[:, tile] = mxu(w.dy[...], self.store[3, tile, :], 1, 1).astype(BF)

        self.tiles(body)

    def back_attention(self, sequence):
        w, slots = self.w, self.slots

        def body(rows, lanes, i, length):
            grad, key = self.split(w.do[rows, lanes]), w.k[rows, lanes]
            probs = w.p[i]
            value = probs.astype(F32)
            dprobs = mxu(w.v[rows, lanes], grad, 1, 1)
            ds = (RELAX * value * (dprobs - column_sum(dprobs * value))).astype(BF)
            dv = mxu(probs, grad, 1, 0)
            dk = mxu(ds, self.split(w.q[rows, lanes]), 1, 0)
            dq = self.merge(mxu(ds, key, 0, 0)) * QUERY_SCALE
            w.q[rows, lanes] = dq.astype(BF)
            w.k[rows, lanes] = dk.astype(BF)
            w.v[rows, lanes] = dv.astype(BF)

        self.pairs(sequence, body)

    def back_joint(self, rows):
        w = self.w

        def body(tile):
            da = mxu(w.q[rows, :], self.store[0, tile, :], 1, 1)
            da = da + mxu(w.k[rows, :], self.store[1, tile, :], 1, 1)
            w.mid[rows, tile] = da + mxu(w.v[rows, :], self.store[2, tile, :], 1, 1)

        self.tiles(body)

    def back_end(self, target, first=0, last=None):
        w = self.w

        def body(rows, i):
            da = w.mid[rows, :]
            normal = w.n_h[rows, :]
            self.add(NORM_GAIN, column_sum(da * normal))
            self.add(NORM_BIAS, column_sum(da))
            self.add(QUERY_BIAS, column_sum(w.q[rows, :].astype(F32)))
            self.add(VALUE_BIAS, column_sum(w.v[rows, :].astype(F32)))
            din = w.din[rows, :] + norm_pull(da, normal, w.r_h[rows, :], self.row(NORM_GAIN))
            w.din[rows, :] = din
            target[rows, :] = din.astype(BF)

        self.chunks(body, first, last)


    def weight_grad(self, block):
        w = self.w
        if block < 3:
            left, right = w.a, (w.q, w.k, w.v)[block]
        elif block == 3:
            left, right = w.o, w.dy
        elif block < 8:
            left, right = w.c, w.slope.at[block - 4]
        else:
            left, right = w.g.at[block - 8], w.de

        def body(tile):
            self.store[block, tile, :] = mxu(left[:, tile], right[...], 0, 0).astype(BF)

        self.tiles(body)


def unfold_vectors(tiles, vec, count):
    for pair in range(count // 2):
        vec[:NARROW, pair * LANES : (pair + 1) * LANES] = tiles[2 * pair, :NARROW, :] + tiles[2 * pair + 1, :NARROW, :]
    half, quarter = count // 2, count // 4
    for shard in range(count):
        row, lane = QUERY_BIAS + shard // half, (shard % half) * LANES
        vec[row : row + 1, lane : lane + LANES] = tiles[shard, NARROW : NARROW + 1, :]
        for part in range(2):
            row, lane = EXPAND_BIAS + shard // quarter, ((shard % quarter) * 2 + part) * LANES
            source = NARROW + 1 + part
            vec[row : row + 1, lane : lane + LANES] = tiles[shard, source : source + 1, :]


def fold_vectors(tiles, dvec, figures, count):
    half, quarter = count // 2, count // 4
    for shard in range(count):
        pair = shard // 2
        tiles[shard, :NARROW, :] = dvec[:NARROW, pair * LANES : (pair + 1) * LANES]
        row, lane = QUERY_BIAS + shard // half, (shard % half) * LANES
        tiles[shard, NARROW : NARROW + 1, :] = dvec[row : row + 1, lane : lane + LANES]
        for part in range(2):
            row, lane = EXPAND_BIAS + shard // quarter, ((shard % quarter) * 2 + part) * LANES
            target = NARROW + 1 + part
            tiles[shard, target : target + 1, :] = dvec[row : row + 1, lane : lane + LANES]
        tiles[shard, FIGURES : FIGURES + 1, :] = figures
        tiles[shard, FIGURES + 1 :, :] = jnp.zeros((VECTOR_ROWS - FIGURES - 1, LANES), F32)


def figures_of(sums, lengths):
    lane = lax.broadcasted_iota(jnp.int32, (1, LANES), 1)
    row = jnp.zeros((1, LANES), F32)
    for i in range(3):
        row = jnp.where(lane == i, jnp.sum(sums[i : i + 1, :], axis=1, keepdims=True), row)
    seen = lengths[0]
    for i in range(1, lengths.shape[0]):
        seen = seen + lengths[i]
    return jnp.where(lane == 3, seen.astype(F32), row)


def relay_kernel(depth, lengths, tokens, cotangent, joint, output, expand, reduce, *refs):
    relay_body(depth, lengths, tokens, cotangent, joint, output, expand, reduce, refs[: NARROW + 2], *refs[NARROW + 2 :])


def own_vectors(place, refs, tile):
    tile[...] = jnp.zeros_like(tile)
    for i in range(NARROW):
        value = refs[i][...].astype(F32)
        zero = jnp.zeros_like(value)
        tile[i : i + 1, :] = jnp.where(
            place.c == 0, jnp.concatenate([value, zero], axis=1), jnp.concatenate([zero, value], axis=1))
    tile[NARROW : NARROW + 1, :] = refs[NARROW][...].astype(F32)
    for part in range(2):
        tile[NARROW + 1 + part : NARROW + 2 + part, :] = refs[NARROW + 1][:, part * LANES : (part + 1) * LANES].astype(F32)


def relay_body(depth, lengths, tokens, cotangent, joint, output, expand, reduce, vector_refs,
                 section_out, section_grad, joint_out, output_out, expand_out, reduce_out, vector_out,
                 store, vectors, tiles, vec, dvec, sums, h, a, q, k, v, p, o, n_h, r_h, n_y, r_y, n_m, r_m, n_e, r_e,
                 mid, c, g, slope, de, dy, do, din, result, staged, incoming, pass_sems, out_sems, *rest):
    place = Place(depth)
    width = store.shape[2]
    count = 4 * depth
    gather_parts, rest = rest[:4], rest[4:]
    scatter_parts, vector_parts = rest[:18], rest[18:]
    work = Work(vec, dvec, h, a, q, k, v, p, o, n_h, r_h, n_y, r_y, n_m, r_m, n_e, r_e, mid, c, g, slope,
                de, dy, do, din, sums)
    layer, hidden = Layer(work, store, lengths), Layer(work, store, lengths, swift=False)
    slots, parts = layer.slots, range(layer.sequences)
    whole = pl.ds(0, layer.tokens)
    first, second = place.s == 0, place.s == 1

    def passing(source, part, way):
        rows = pl.ds(part * slots, slots)
        return pltpu.make_async_remote_copy(
            source.at[rows], incoming.at[rows], pass_sems.at[way, 0, part], pass_sems.at[way, 1, part],
            device_id=place.across(), device_id_type=MESH)

    def forward(part):
        return passing(result, part, 0)

    def backward(part):
        return passing(do, part, 1)

    out_copy = pltpu.make_async_copy(result, section_out, out_sems.at[BLOCKS])
    grad_copy = pltpu.make_async_copy(din, section_grad, out_sems.at[BLOCKS + 1])

    token_copy = pltpu.make_async_copy(tokens, h, out_sems.at[BLOCKS + 2])
    seed_copy = pltpu.make_async_copy(cotangent, dy, out_sems.at[BLOCKS + 3])
    pl.when(first)(lambda: token_copy.start())
    pl.when(second)(lambda: seed_copy.start())
    own_vectors(place, vector_refs, vectors)
    place.greet()
    dvec[...] = jnp.zeros_like(dvec)
    sums[...] = jnp.zeros_like(sums)

    def fore_last(part):
        layer.fore_reduce(layer.part(part))
        layer.fore_end(result, part * slots, (part + 1) * slots)

    def back_rest(part, layer):
        layer.back_joint(layer.part(part))
        layer.back_end(do, part * slots, (part + 1) * slots)

    def ready(item):
        if item == VECTOR_ITEM:
            unfold_vectors(tiles, vec, count)

        def enter():
            token_copy.wait()
            hidden.fore_start(h)

        def leave(part):
            fore_last(part)
            forward(part).start()

        pieces = []
        if item == VECTOR_ITEM:
            pieces = [enter]
        elif item < 3:
            pieces = [functools.partial(hidden.fore_joint, item, whole)]
            if item == 2:
                pieces += [functools.partial(hidden.fore_attention, part) for part in parts]
        elif item == 3:
            pieces = [functools.partial(hidden.fore_output, whole), hidden.fore_middle]
        elif item < 8:
            pieces = [functools.partial(hidden.fore_expand, item - 4, whole)]
        elif item == BLOCKS - 1:
            pieces = [functools.partial(leave, part) for part in parts]
        return [lambda piece=piece: pl.when(first)(piece) for piece in pieces]

    gather = Gather(place, (joint, output, expand, reduce, vectors), store, tiles, gather_parts)
    run_gather(gather, ready)
    gather.drain()

    @pl.when(second)
    def _():
        for part in parts:
            forward(part).wait_recv()
            rows, span = layer.part(part), (part * slots, (part + 1) * slots)
            layer.fore_start(incoming, *span)
            for block in range(3):
                layer.fore_joint(block, rows)
            layer.fore_attention(part)
            layer.fore_output(rows)
            layer.fore_middle(*span)
            for block in range(4):
                layer.fore_expand(block, rows)
            fore_last(part)
        seed_copy.wait()
        layer.back_start(dy, True)
        for block in range(4):
            layer.back_reduce(block, whole)
        layer.back_expand()
        layer.back_middle()
        layer.back_output()
        for part in parts:
            layer.back_attention(part)
            back_rest(part, layer)
            backward(part).start()

    out_copy.start()

    @pl.when(first)
    def _():
        for part in parts:
            backward(part).wait_recv()
            layer.back_start(incoming, False, part * slots, (part + 1) * slots)
            if part < parts[-1]:
                for block in range(4):
                    layer.back_reduce(block, layer.part(part))

    def fill(step):
        if step >= 4:
            layer.weight_grad(SCATTER_ORDER[step])
        if step == 8:
            grad_copy.start()
        if step == BLOCKS - 1:
            fold_vectors(tiles, dvec, figures_of(sums, lengths), count)

    def first_part(z):
        pl.when(first)(lambda: layer.back_reduce(z, layer.part(parts[-1])))
        layer.weight_grad(8 + z)

    def beside(step):
        pieces = {1: [hidden.back_expand], 2: [hidden.back_middle], 3: [hidden.back_output]}
        for part in parts:
            attention, rest = functools.partial(hidden.back_attention, part), functools.partial(back_rest, part, hidden)
            pieces.setdefault(4 + part % 2, []).append(attention)
            pieces.setdefault(6 + part % 2, []).append(rest)

        @pl.when(first)
        def _():
            for piece in pieces.get(step, []):
                piece()

    def part_of(step, shard):
        block, row = spot(SCATTER_ORDER[step], shard)
        return store.at[block, pl.ds(row, PART)]

    targets = [shard_view((joint_out, output_out, expand_out, reduce_out, None), item, width) for item in SCATTER_ORDER]
    outs = [staged.at[step % STAGED] for step in range(BLOCKS)]
    copies = [pltpu.make_async_copy(outs[step], targets[step], out_sems.at[step]) for step in range(BLOCKS)]
    scatter = Scatter(place, part_of, BLOCKS, SLOTS, EARLY_SLOTS, scatter_parts[:5], outs, scatter_parts[5:], first_part)
    vector_scatter = Scatter(place, lambda step, shard: tiles.at[shard], 1, 1, 1, vector_parts[:5], [vector_out], vector_parts[5:])

    def done(step):
        copies[step].start()
        if step + 1 >= STAGED and step + 1 < BLOCKS:
            copies[step + 1 - STAGED].wait()

    run_scatter(scatter, vector_scatter, fill, beside, done)

    @pl.when(first)
    def _():
        for part in parts:
            forward(part).wait_send()

    @pl.when(second)
    def _():
        for part in parts:
            backward(part).wait_send()

    for copy in copies[BLOCKS - STAGED :] + [out_copy, grad_copy]:
        copy.wait()


def finish_kernel(core, tile, *refs):
    sources, targets, rest = refs[:6], refs[6:12], refs[12:]
    magnitudes, joint_bias, expand_bias, narrow = rest[0], rest[1], rest[2], rest[3:-7]
    held, sems = rest[-7:-1], rest[-1]
    loads = [pltpu.make_async_copy(source, buffer, sems.at[0, i]) for i, (source, buffer) in enumerate(zip(sources, held))]
    copies = [pltpu.make_async_copy(buffer, target, sems.at[1, i]) for i, (buffer, target) in enumerate(zip(held, targets))]
    for load in loads:
        load.start()
    halves = jnp.where(core[0] == 0, tile[:NARROW, :HEAD_DIM], tile[:NARROW, HEAD_DIM:])
    for i, ref in enumerate(narrow):
        ref[...] = halves[i : i + 1]
    figures = tile[FIGURES : FIGURES + 1, :]
    magnitudes[...] = jnp.sqrt(figures[:, :3] / (figures[:, 3:4] * sources[0].shape[1]))
    joint_bias[...] = tile[NARROW : NARROW + 1, :]
    for part in range(2):
        expand_bias[:, part * LANES : (part + 1) * LANES] = tile[NARROW + 1 + part : NARROW + 2 + part, :]
    for load, copy in zip(loads, copies):
        load.wait()
        copy.start()
    for copy in copies:
        copy.wait()


def relay_local(depth, tokens, lengths, *parameters):
    cotangent, own = parameters[-1], Params(*parameters[:-1])
    micro, rows, width = tokens.shape
    sequences = lengths.shape[1] * micro
    count = micro * rows
    core = lax.axis_index("batch") % 2

    vectors = [
        own.norm_gain, own.norm_bias, own.output_bias, own.sandwich_gain, own.sandwich_bias, own.second_gain,
        own.second_bias, own.reduce_bias, own.closing_gain, own.closing_bias, own.joint_bias, own.expand_bias]

    low, high, rate = (pltpu.VMEM((count, width), BF), pltpu.VMEM((count, width), F32), pltpu.VMEM((count, 1), F32))
    wide = pltpu.VMEM((4, count, width), BF)
    shards = 4 * depth
    dma = pltpu.SemaphoreType.DMA
    vmem, anywhere = pl.BlockSpec(memory_space=pltpu.VMEM), pl.BlockSpec(memory_space=pl.ANY)
    shapes = [
        jax.ShapeDtypeStruct((count, width), BF), jax.ShapeDtypeStruct((count, width), F32),
        jax.ShapeDtypeStruct((PART, 3 * width), F32), jax.ShapeDtypeStruct((PART, width), F32),
        jax.ShapeDtypeStruct((PART, 4 * width), F32), jax.ShapeDtypeStruct((4 * PART, width), F32)]
    slots = rows // lengths.shape[1]
    results = pl.pallas_call(
        functools.partial(relay_kernel, depth),
        out_shape=shapes + [jax.ShapeDtypeStruct((VECTOR_ROWS, LANES), F32)],
        in_specs=[pl.BlockSpec(memory_space=pltpu.SMEM)] + [anywhere] * 6 + [vmem] * len(vectors),
        out_specs=[anywhere] * 6 + [vmem],
        scratch_shapes=[
            pltpu.VMEM((BLOCKS, width, width), BF), pltpu.VMEM((VECTOR_ROWS, LANES), F32), pltpu.VMEM((shards, VECTOR_ROWS, LANES), F32),
            pltpu.VMEM((VECTOR_ROWS, width), F32), pltpu.VMEM((VECTOR_ROWS, width), F32), pltpu.VMEM((8, width), F32),
            low, low, low, low, low, pltpu.VMEM((sequences * width // LANES, slots, 2 * slots), BF), low,
            high, rate, high, rate, high, rate, high, rate,
            high, low, wide, wide, low, low, low, high, low, pltpu.VMEM((STAGED, PART, width), F32), low,
            dma((2, 2, sequences)), dma((BLOCKS + 4,)),
        ] + gather_sems(depth) + scatter_scratch(depth, SLOTS, EARLY_SLOTS, PART, width, BF) + scatter_scratch(depth, 1, 1, VECTOR_ROWS, LANES, F32),
        compiler_params=pltpu.CompilerParams(collective_id=1, has_side_effects=True, vmem_limit_bytes=VMEM_LIMIT),
        cost_estimate=pl.CostEstimate(flops=6 * count * BLOCKS * width * width, bytes_accessed=2 * BLOCKS * width * width, transcendentals=0),
        name="relay",
    )(lengths.reshape(-1), tokens.reshape(count, width), cotangent.reshape(count, width),
      own.joint_weight[0], own.output_weight[0], own.expand_weight[0], own.reduce_weight[0], *vectors)

    vector = jax.ShapeDtypeStruct((1, HEAD_DIM), F32)
    small = [jax.ShapeDtypeStruct((1, 3), F32), jax.ShapeDtypeStruct((1, LANES), F32),
             jax.ShapeDtypeStruct((1, 2 * LANES), F32)] + [vector] * NARROW
    final = pl.pallas_call(
        finish_kernel,
        out_shape=shapes + small,
        in_specs=[pl.BlockSpec(memory_space=pltpu.SMEM), vmem] + [anywhere] * 6,
        out_specs=[anywhere] * 6 + [vmem] * len(small),
        scratch_shapes=[pltpu.VMEM(s.shape, s.dtype) for s in shapes] + [dma((2, 6))],
        compiler_params=pltpu.CompilerParams(vmem_limit_bytes=VMEM_LIMIT),
        name="finish",
    )(core.reshape(1), results[6], *results[:6])
    section_out, section_grad, joint, output, expand, reduce, magnitudes, joint_bias, expand_bias = final[:9]
    narrow = final[9:]
    grads = Params(
        norm_gain=narrow[NORM_GAIN], norm_bias=narrow[NORM_BIAS], joint_weight=joint[None],
        joint_bias=joint_bias, output_weight=output[None], output_bias=narrow[OUTPUT_BIAS],
        sandwich_gain=narrow[SANDWICH_GAIN], sandwich_bias=narrow[SANDWICH_BIAS], second_gain=narrow[SECOND_GAIN],
        second_bias=narrow[SECOND_BIAS], expand_weight=expand[None],
        expand_bias=expand_bias, reduce_weight=reduce[None],
        reduce_bias=narrow[REDUCE_BIAS], closing_gain=narrow[CLOSING_GAIN], closing_bias=narrow[CLOSING_BIAS])
    shape = (1, micro, rows, width)
    return (section_out.reshape(shape), section_grad.reshape(shape), magnitudes) + tuple(grads)


def solution(mesh):
    vector, matrix = P("section", "batch"), P("section", "batch", None)
    kinds = tuple(matrix if i in MATRICES else vector for i in range(16))
    rows = P(None, "batch", None)
    stacked = P("section", None, "batch", None)
    devices = mesh.shape["batch"]
    body = functools.partial(relay_local, devices // 4) if devices == 16 else plain_local
    return jax.shard_map(
        body,
        mesh=mesh,
        in_specs=(rows, P(None, "batch")) + kinds + (rows,),
        out_specs=(stacked, stacked, P("section", None)) + kinds,
        check_vma=False,
    )
```

```python
import functools
import math
from typing import Any, NamedTuple

import jax
import jax.numpy as jnp
from jax import lax
from jax.experimental import pallas as pl
from jax.experimental.pallas import tpu as pltpu
from jax.sharding import PartitionSpec as P

HEADS = 16
HEAD_DIM = 64
EPSILON = 1e-05
RELAX = 32.0
MASKED = -1000000000.0
QUERY_SCALE = 1.0 / (RELAX * math.sqrt(HEAD_DIM))

BF = jnp.bfloat16
F32 = jnp.float32
VMEM_LIMIT = 62 * 2**20

class Params(NamedTuple):
    norm_gain: Any
    norm_bias: Any
    joint_weight: Any
    joint_bias: Any
    output_weight: Any
    output_bias: Any
    sandwich_gain: Any
    sandwich_bias: Any
    second_gain: Any
    second_bias: Any
    expand_weight: Any
    expand_bias: Any
    reduce_weight: Any
    reduce_bias: Any
    closing_gain: Any
    closing_bias: Any


MATRICES = (2, 4, 10, 12)
VECTORS = tuple(i for i in range(16) if i not in MATRICES)


class Kept(NamedTuple):
    n1: Any
    r1: Any
    a: Any
    qh: Any
    kh: Any
    vh: Any
    probs: Any
    o: Any
    y: Any
    ny: Any
    ry: Any
    nm: Any
    rm: Any
    c: Any
    f: Any
    g: Any
    e: Any
    ne: Any
    re: Any
    out: Any


def dot(left, right, left_dim, right_dim):
    return lax.dot_general(left, right, (((left_dim,), (right_dim,)), ((), ())), preferred_element_type=F32)


def norm_parts(value):
    center = jnp.mean(value, axis=-1, keepdims=True)
    centered = value - center
    rate = lax.rsqrt(jnp.mean(centered * centered, axis=-1, keepdims=True) + EPSILON)
    return centered * rate, rate


def norm_back(grad, normal, rate, gain):
    scaled = grad * gain
    first = jnp.mean(scaled, axis=-1, keepdims=True)
    second = jnp.mean(scaled * normal, axis=-1, keepdims=True)
    gain_grad = jnp.sum(grad * normal, axis=0)
    bias_grad = jnp.sum(grad, axis=0)
    return rate * (scaled - first - normal * second), gain_grad, bias_grad


def heads_of(flat, sequences):
    return flat.reshape(sequences, flat.shape[0] // sequences, HEADS, HEAD_DIM)


def layer_fore(hidden_in, w, lengths):
    sequences = lengths.shape[0]
    model = hidden_in.shape[1]
    hidden = hidden_in.astype(F32)
    n1, r1 = norm_parts(hidden)
    a = (n1 * w.norm_gain + w.norm_bias).astype(BF)
    mixed = dot(a, w.joint_weight, 1, 0)
    q = ((mixed[:, :model] + w.joint_bias[:model]) * QUERY_SCALE).astype(BF)
    k = mixed[:, model : 2 * model].astype(BF)
    v = (mixed[:, 2 * model :] + w.joint_bias[model:]).astype(BF)
    qh, kh, vh = heads_of(q, sequences), heads_of(k, sequences), heads_of(v, sequences)
    scores = jnp.einsum("bqhd,bkhd->bhqk", qh, kh, preferred_element_type=F32)
    slots = scores.shape[-1]
    query_slot = lax.broadcasted_iota(jnp.int32, (sequences, slots, slots), 1)
    key_slot = lax.broadcasted_iota(jnp.int32, (sequences, slots, slots), 2)
    seen = (key_slot <= query_slot) & (key_slot < lengths[:, None, None])
    scores = jnp.where(seen[:, None], scores, MASKED)
    exponent = jnp.exp(RELAX * (scores - jnp.max(scores, axis=-1, keepdims=True)))
    probs = exponent / jnp.sum(exponent, axis=-1, keepdims=True)
    o = jnp.einsum("bhqk,bkhd->bqhd", probs.astype(BF), vh, preferred_element_type=F32)
    o = o.reshape(hidden.shape).astype(BF)
    y = dot(o, w.output_weight, 1, 0) + w.output_bias
    ny, ry = norm_parts(y)
    mid = hidden + ny * w.sandwich_gain + w.sandwich_bias
    nm, rm = norm_parts(mid)
    c = (nm * w.second_gain + w.second_bias).astype(BF)
    f = dot(c, w.expand_weight, 1, 0) + w.expand_bias
    g = jax.nn.gelu(f).astype(BF)
    e = dot(g, w.reduce_weight, 1, 0) + w.reduce_bias
    ne, re = norm_parts(e)
    out = mid + ne * w.closing_gain + w.closing_bias
    return out, Kept(n1, r1, a, qh, kh, vh, probs, o, y, ny, ry, nm, rm, c, f, g, e, ne, re, out)


def layer_back(dout, w, s, want_weights):
    sequences = s.qh.shape[0]
    de, closing_gain, closing_bias = norm_back(dout, s.ne, s.re, w.closing_gain)
    de = de.astype(BF)
    dg = dot(de, w.reduce_weight, 1, 1)
    df = jax.vjp(jax.nn.gelu, s.f)[1](dg)[0].astype(BF)
    dc = dot(df, w.expand_weight, 1, 1)
    dmid, second_gain, second_bias = norm_back(dc, s.nm, s.rm, w.second_gain)
    dmid = dmid + dout
    dy, sandwich_gain, sandwich_bias = norm_back(dmid, s.ny, s.ry, w.sandwich_gain)
    dy = dy.astype(BF)
    do = heads_of(dot(dy, w.output_weight, 1, 1).astype(BF), sequences)
    dprobs = jnp.einsum("bqhd,bkhd->bhqk", do, s.vh, preferred_element_type=F32)
    dv = jnp.einsum("bhqk,bqhd->bkhd", s.probs.astype(BF), do, preferred_element_type=F32)
    ds = RELAX * s.probs * (dprobs - jnp.sum(dprobs * s.probs, axis=-1, keepdims=True))
    ds = ds.astype(BF)
    dq = jnp.einsum("bhqk,bkhd->bqhd", ds, s.kh, preferred_element_type=F32)
    dk = jnp.einsum("bhqk,bqhd->bkhd", ds, s.qh, preferred_element_type=F32)
    flat = dout.shape
    dmixed = jnp.concatenate([dq.reshape(flat) * QUERY_SCALE, dk.reshape(flat), dv.reshape(flat)], axis=1).astype(BF)
    da = dot(dmixed, w.joint_weight, 1, 1)
    dh, norm_gain, norm_bias = norm_back(da, s.n1, s.r1, w.norm_gain)
    din = dmid + dh
    if not want_weights:
        return din, None
    model = flat[1]
    sums = jnp.sum(dmixed.astype(F32), axis=0)
    return din, Params(
        norm_gain=norm_gain,
        norm_bias=norm_bias,
        joint_weight=dot(s.a, dmixed, 0, 0),
        joint_bias=jnp.concatenate([sums[:model], sums[2 * model :]]),
        output_weight=dot(s.o, dy, 0, 0),
        output_bias=jnp.sum(dy.astype(F32), axis=0),
        sandwich_gain=sandwich_gain,
        sandwich_bias=sandwich_bias,
        second_gain=second_gain,
        second_bias=second_bias,
        expand_weight=dot(s.c, df, 0, 0),
        expand_bias=jnp.sum(df.astype(F32), axis=0),
        reduce_weight=dot(s.g, de, 0, 0),
        reduce_bias=jnp.sum(de.astype(F32), axis=0),
        closing_gain=closing_gain,
        closing_bias=closing_bias,
    )


def passed_along(block, axis, distance):
    devices = range(lax.axis_size(axis))
    route = [(i - distance, i) for i in devices if i - distance in devices]
    return lax.ppermute(block, axis, route)


def plain_local(tokens, lengths, *parameters):
    cotangent = parameters[-1]
    own = parameters[:-1]
    section = lax.axis_index("section")
    micro, rows, model = tokens.shape
    sequences = lengths.shape[1]
    slots = rows // sequences
    total_rows = micro * rows

    packed = jnp.concatenate([own[i] for i in VECTORS], axis=1)
    packed = lax.all_gather(packed, "batch", axis=0, tiled=True).astype(F32)
    w = list(own)
    start = 0
    for i in VECTORS:
        width = own[i].shape[1]
        w[i] = packed[:, start : start + width].reshape(-1)
        start += width
    for i, whole in zip(MATRICES, plain_gather([own[i] for i in MATRICES])):
        w[i] = whole
    w = Params(*w)

    flat_lengths = lengths.reshape(-1)
    seen = lax.broadcasted_iota(jnp.int32, (micro * sequences, slots), 1) < flat_lengths[:, None]
    valid = seen.astype(F32).reshape(total_rows, 1)
    source = tokens.reshape(total_rows, model)
    first_out, _ = layer_fore(source, w, flat_lengths)
    incoming = passed_along(first_out.astype(BF), "section", 1)
    out, s = layer_fore(jnp.where(section == 0, source, incoming), w, flat_lengths)
    section_out = out.astype(BF).reshape(1, micro, rows, model)
    squares = jnp.stack([jnp.sum(part * part * valid) for part in (s.y, s.e, s.out)])

    seed = cotangent.reshape(total_rows, model).astype(F32) * valid
    last_in, _ = layer_back(seed, w, s, False)
    incoming = passed_along(last_in.astype(BF), "section", -1)
    din, grads = layer_back(jnp.where(section == 1, seed, incoming.astype(F32)), w, s, True)
    section_grad = din.reshape(1, micro, rows, model)

    result = list(grads)
    for i, part in zip(MATRICES, plain_scatter([grads[i].astype(BF) for i in MATRICES])):
        result[i] = part
    devices = lax.axis_size("batch")
    small = jnp.concatenate([grads[i].reshape(devices, -1) for i in VECTORS], axis=1)
    small = lax.psum_scatter(small, "batch", scatter_dimension=0, tiled=True)
    start = 0
    for i in VECTORS:
        width = own[i].shape[1]
        result[i] = small[:, start : start + width]
        start += width
    count = jnp.sum(lengths).astype(F32)
    square_all, count_all = lax.psum((squares, count), "batch")
    magnitudes = jnp.sqrt(square_all / (count_all * model))[None]
    return (section_out, section_grad, magnitudes) + tuple(result)


def plain_gather(shards):
    return [lax.all_gather(w, "batch", axis=1, tiled=True)[0] for w in shards]


def plain_scatter(grads):
    return [lax.psum_scatter(g[None], "batch", scatter_dimension=1, tiled=True).astype(F32) for g in grads]


MESH = pl.DeviceIdType.MESH
BLOCKS = 12
VECTOR_ITEM = 12
PART = 64
SLOTS, EARLY_SLOTS = 5, 3
CROSS = 16
LAGS = (1, 2, 3, 4, 5)
GATHER_ORDER = (VECTOR_ITEM,) + tuple(range(BLOCKS))
GATHER_CROSSED = (6, 11)
GATHER_AHEAD = 4
SIDE_LAG, REST_LAG = 2, 3
SCATTER_ORDER = (8, 9, 10, 11, 4, 5, 6, 7, 3, 0, 1, 2)
UP, DOWN, SIDE = 0, 1, 2


def when(condition, action):
    if condition is True:
        action()
    else:
        pl.when(condition)(action)


def both(first, second):
    if first is True:
        return second
    if second is True:
        return first
    return first & second


class Place:
    def __init__(self, depth):
        index = lax.axis_index("batch")
        self.s = lax.axis_index("section")
        self.depth = depth
        self.z = index // 4
        self.x = (index // 2) % 2
        self.c = index % 2

    def device(self, z, x, c):
        return (self.s, (z * 2 + x) * 2 + c)

    def shard(self, z, x, c):
        return (z * 2 + x) * 2 + c

    def me(self):
        return self.shard(self.z, self.x, self.c)

    def across(self):
        return (1 - self.s, self.me())

    def greet(self):
        z, x, c = self.z, self.x, self.c
        sem = pltpu.get_barrier_semaphore()

        def signal(device):
            pl.semaphore_signal(sem, inc=1, device_id=device, device_id_type=MESH)

        signal(self.device(z, 1 - x, c))
        signal(self.device(z, x, 1 - c))
        signal(self.across())
        pl.when(z < self.depth - 1)(lambda: signal(self.device(z + 1, x, c)))
        pl.when(z > 0)(lambda: signal(self.device(z - 1, x, c)))
        chain = (z < self.depth - 1).astype(jnp.int32) + (z > 0).astype(jnp.int32)
        pl.semaphore_wait(sem, 3 + chain)


def spot(item, shard):
    if item < 8:
        return item, pl.multiple_of(shard * PART, 16)
    return 8 + shard // 4, pl.multiple_of((shard % 4) * 4 * PART + (item - 8) * PART, 16)


def shard_view(refs, item, width):
    joint, output, expand, reduce, vectors = refs
    if item < 3:
        return joint.at[:, pl.ds(item * width, width)]
    if item == 3:
        return output
    if item < 8:
        return expand.at[:, pl.ds((item - 4) * width, width)]
    if item < VECTOR_ITEM:
        return reduce.at[pl.ds((item - 8) * PART, PART)]
    return vectors


class Gather:
    def __init__(self, place, own, store, vectors, sems):
        self.p, self.own, self.store, self.vectors = place, own, store, vectors
        self.send, self.share, self.recv, self.local = sems
        self.sent = []

    def at(self, item, shard):
        if item == VECTOR_ITEM:
            return self.vectors.at[shard]
        block, row = spot(item, shard)
        return self.store.at[block, pl.ds(row, PART)]

    def copy(self, item, shard, way, first=False):
        p = self.p
        target = self.at(item, shard)
        source = shard_view(self.own, item, self.store.shape[2]) if first else target
        recv = self.recv.at[item, shard]
        if way is None:
            send, device = self.share.at[item, shard // 2], p.device(p.z, p.x, 1 - p.c)
        else:
            send = self.send.at[item, shard // 2, way]
            device = (p.device(p.z + 1, p.x, p.c), p.device(p.z - 1, p.x, p.c), p.device(p.z, 1 - p.x, p.c))[way]
        return pltpu.make_async_remote_copy(source, target, send, recv, device_id=device, device_id_type=MESH)

    def go(self, item, shard, way, condition, first=False):
        self.sent.append((item, shard, way, condition, first))
        when(condition, lambda: self.copy(item, shard, way, first).start())

    def arrived(self, item, shard):
        self.copy(item, shard, None).wait_recv()

    def keep_own(self):
        me = self.p.me()
        copies = [
            pltpu.make_async_copy(shard_view(self.own, item, self.store.shape[2]), self.at(item, me), self.local.at[item])
            for item in range(BLOCKS + 1)
        ]
        for copy in copies:
            copy.start()
        return copies

    def own_sends(self, item):
        p = self.p
        self.go(item, p.me(), UP, p.z < p.depth - 1, True)
        self.go(item, p.me(), DOWN, p.z > 0, True)
        self.go(item, p.me(), SIDE, True, True)
        self.go(item, p.me(), None, True, True)

    def chain_round(self, item, hop):
        p = self.p
        crossed = item in GATHER_CROSSED
        for x in (p.x, 1 - p.x) if crossed else (p.x,):
            for origin, present, way, onward in (
                (p.z - hop, p.z >= hop, UP, p.z < p.depth - 1),
                (p.z + hop, p.z + hop < p.depth, DOWN, p.z > 0),
            ):
                shard = p.shard(origin, x, p.c)
                when(present, lambda: self.arrived(item, shard))
                self.go(item, shard, way, both(present, onward))
                if not crossed:
                    self.go(item, shard, SIDE, present)
                self.go(item, shard, None, present)

    def side_own(self, item):
        p = self.p
        shard = p.shard(p.z, 1 - p.x, p.c)
        self.arrived(item, shard)
        if item in GATHER_CROSSED:
            self.go(item, shard, UP, p.z < p.depth - 1)
            self.go(item, shard, DOWN, p.z > 0)
        self.go(item, shard, None, True)

    def side_round(self, item, hop):
        p = self.p
        if item in GATHER_CROSSED:
            return
        for origin, present in ((p.z - hop, p.z >= hop), (p.z + hop, p.z + hop < p.depth)):
            shard = p.shard(origin, 1 - p.x, p.c)
            when(present, lambda: self.arrived(item, shard))
            self.go(item, shard, None, present)

    def rest(self, item):
        p = self.p
        for z in range(p.depth):
            for x in range(2):
                self.arrived(item, p.shard(z, x, 1 - p.c))

    def drain(self):
        for item, shard, way, condition, first in self.sent:
            when(condition, lambda: self.copy(item, shard, way, first).wait_send())


def run_gather(gather, ready):
    depth, count = gather.p.depth, len(GATHER_ORDER)
    pending = []
    kept = gather.keep_own()
    for item in GATHER_ORDER[:GATHER_AHEAD]:
        gather.own_sends(item)

    def sides(item):
        for hop in range(1, depth):
            gather.side_round(item, hop)

    def finish(item):
        gather.rest(item)
        kept[item].wait()
        pending.extend(ready(item))

    for place, item in enumerate(GATHER_ORDER):
        if item in GATHER_CROSSED:
            gather.side_own(item)
        for hop in range(1, depth):
            gather.chain_round(item, hop)
            if hop == 1:
                if place + GATHER_AHEAD < count:
                    gather.own_sends(GATHER_ORDER[place + GATHER_AHEAD])
                if item not in GATHER_CROSSED:
                    gather.side_own(item)
            if pending:
                pending.pop(0)()
        if place >= SIDE_LAG:
            sides(GATHER_ORDER[place - SIDE_LAG])
        if place >= REST_LAG:
            finish(GATHER_ORDER[place - REST_LAG])
    for item in GATHER_ORDER[count - SIDE_LAG :]:
        sides(item)
    for item in GATHER_ORDER[count - REST_LAG :]:
        finish(item)
        while pending:
            pending.pop(0)()


def gather_sems(depth):
    kind, items = pltpu.SemaphoreType.DMA, BLOCKS + 1
    return [kind((items, 2 * depth, 3)), kind((items, 2 * depth)), kind((items, 4 * depth)), kind((items,))]


def total(*refs):
    value = refs[0][...].astype(F32)
    for ref in refs[1:]:
        value = value + ref[...].astype(F32)
    return value


def crossing(step, rows):
    return 0 if rows <= CROSS or step % 3 == 2 else CROSS


class Scatter:
    def __init__(self, place, part, count, slots, early, buffers, outs, sems, first_part=lambda z: None):
        self.first_part = first_part
        self.p, self.part, self.count, self.slots, self.early, self.outs = place, part, count, slots, early, outs
        self.core_in, self.side_in, self.chain_in, self.cross_in, self.last_in = buffers
        (self.core_send, self.core_recv, self.side_send, self.side_recv, self.chain_send, self.chain_recv,
         self.cross_send, self.cross_recv, self.last_send, self.last_recv,
         self.core_free, self.side_free, self.chain_free) = sems
        depth = place.depth
        self.rows = self.core_in.shape[2]
        self.origins = [q for pair in zip(range(depth - 1, -1, -1), range(depth)) for q in pair][:depth]

    def main(self, step):
        return pl.ds(0, self.rows - crossing(step, self.rows))

    def tail(self, step):
        cut = crossing(step, self.rows)
        return pl.ds(self.rows - cut, cut)

    def mine(self, step, z, x, c):
        return self.part(step, self.p.shard(z, x, c))

    def core_copy(self, step, z, x):
        p, slot = self.p, step % self.early
        return pltpu.make_async_remote_copy(
            self.mine(step, z, x, 1 - p.c), self.core_in.at[slot, z * 2 + x],
            self.core_send.at[slot, z * 2 + x], self.core_recv.at[slot, z * 2 + x],
            device_id=p.device(p.z, p.x, 1 - p.c), device_id_type=MESH)

    def side_copy(self, step, z):
        p, slot, rows = self.p, step % self.early, self.main(step)
        return pltpu.make_async_remote_copy(
            self.mine(step, z, 1 - p.x, p.c).at[rows], self.side_in.at[slot, z, rows],
            self.side_send.at[slot, z], self.side_recv.at[slot, z],
            device_id=p.device(p.z, 1 - p.x, p.c), device_id_type=MESH)

    def chain_copy(self, step, z, up):
        p, slot = self.p, step % self.slots
        return pltpu.make_async_remote_copy(
            self.mine(step, z, p.x, p.c), self.chain_in.at[slot, 1 - up, z],
            self.chain_send.at[slot, 1 - up, z], self.chain_recv.at[slot, 1 - up, z],
            device_id=p.device(p.z + 2 * up - 1, p.x, p.c), device_id_type=MESH)

    def cross_copy(self, step, z, up):
        p, slot, rows = self.p, step % self.slots, self.tail(step)
        return pltpu.make_async_remote_copy(
            self.mine(step, z, 1 - p.x, p.c).at[rows], self.cross_in.at[slot, 1 - up, z, pl.ds(0, rows.size)],
            self.cross_send.at[slot, 1 - up, z], self.cross_recv.at[slot, 1 - up, z],
            device_id=p.device(p.z + 2 * up - 1, p.x, p.c), device_id_type=MESH)

    def last_copy(self, step):
        p, slot, rows = self.p, step % self.slots, self.tail(step)
        return pltpu.make_async_remote_copy(
            self.mine(step, p.z, 1 - p.x, p.c).at[rows], self.last_in.at[slot, pl.ds(0, rows.size)],
            self.last_send.at[slot], self.last_recv.at[slot],
            device_id=p.device(p.z, 1 - p.x, p.c), device_id_type=MESH)

    def core_stage(self, step):
        p = self.p
        if step >= self.early:
            self.core_drain(step - self.early)
            pl.semaphore_wait(self.core_free, 1)
        if step == 0:
            for z in self.origins:
                self.first_part(z)
                for x in range(2):
                    self.core_copy(step, z, x).start()
            return
        for x in (1 - p.x, p.x):
            for z in self.origins:
                self.core_copy(step, z, x).start()

    def core_drain(self, step):
        for z in self.origins:
            for x in range(2):
                self.core_copy(step, z, x).wait_send()

    def from_core(self, step, z, x):
        self.core_copy(step, z, x).wait_recv()
        return self.core_in.at[step % self.early, z * 2 + x]

    def side_stage(self, step):
        p = self.p
        if step >= self.early:
            self.side_drain(step - self.early)
            pl.semaphore_wait(self.side_free, 1)
        for z in self.origins:
            twin = self.from_core(step, z, 1 - p.x)
            mine = self.mine(step, z, 1 - p.x, p.c)
            mine[...] = total(mine, twin).astype(mine.dtype)
            self.side_copy(step, z).start()

    def side_drain(self, step):
        for z in self.origins:
            self.side_copy(step, z).wait_send()

    def ways(self, z):
        p, last = self.p, self.p.depth - 1
        return (p.z < z).astype(jnp.int32), ((p.z < z) & (p.z > 0)) | ((p.z > z) & (p.z < last))

    def chain_stage(self, step, near):
        p, slot, last = self.p, step % self.slots, self.p.depth - 1
        cut = crossing(step, self.rows)
        if near and step >= self.slots:
            self.chain_drain(step - self.slots)
            pl.when(p.z < last)(lambda: pl.semaphore_wait(self.chain_free.at[0], 1))
            pl.when(p.z > 0)(lambda: pl.semaphore_wait(self.chain_free.at[1], 1))
        for z in self.origins:
            up, fed = self.ways(z)
            begun = jnp.where(p.z < z, p.z, last - p.z)
            if near:
                self.sum_side(step, z)

            @pl.when((p.z != z) & ((begun <= 1) if near else (begun > 1)))
            def _():
                mine = self.mine(step, z, p.x, p.c)
                other = self.mine(step, z, 1 - p.x, p.c)

                @pl.when(fed)
                def _():
                    self.chain_copy(step, z, up).wait_recv()
                    mine[...] = total(mine, self.chain_in.at[slot, 1 - up, z]).astype(mine.dtype)

                self.chain_copy(step, z, up).start()
                if cut:
                    @pl.when(fed)
                    def _():
                        self.cross_copy(step, z, up).wait_recv()
                        here = other.at[self.tail(step)]
                        here[...] = total(here, self.cross_in.at[slot, 1 - up, z, pl.ds(0, cut)]).astype(here.dtype)

                    self.cross_copy(step, z, up).start()
        if near and step + self.early < self.count:
            self.signal(self.core_free, p.device(p.z, p.x, 1 - p.c))
            self.signal(self.side_free, p.device(p.z, 1 - p.x, p.c))

    @staticmethod
    def signal(sem, device):
        pl.semaphore_signal(sem, inc=1, device_id=device, device_id_type=MESH)

    def sum_side(self, step, z):
        p, main = self.p, self.main(step)
        mine, twin = self.mine(step, z, p.x, p.c), self.from_core(step, z, p.x)
        self.side_copy(step, z).wait_recv()
        here = mine.at[main]
        here[...] = total(here, twin.at[main], self.side_in.at[step % self.early, z, main]).astype(mine.dtype)
        if crossing(step, self.rows):
            here = mine.at[self.tail(step)]
            here[...] = total(here, twin.at[self.tail(step)]).astype(mine.dtype)

    def chain_drain(self, step):
        p = self.p
        for z in self.origins:
            up, _ = self.ways(z)

            @pl.when(p.z != z)
            def _():
                self.chain_copy(step, z, up).wait_send()
                if crossing(step, self.rows):
                    self.cross_copy(step, z, up).wait_send()
        if crossing(step, self.rows):
            self.last_copy(step).wait_send()

    def incoming(self, copy):
        p = self.p
        pl.when(p.z > 0)(lambda: copy(1).wait_recv())
        pl.when(p.z < p.depth - 1)(lambda: copy(0).wait_recv())

    def outcome(self, put, parts, below, above):
        p, last = self.p, self.p.depth - 1
        pl.when(p.z == 0)(lambda: put(*parts, above))
        pl.when(p.z == last)(lambda: put(*parts, below))
        pl.when((p.z > 0) & (p.z < last))(lambda: put(*parts, below, above))

    def last_stage(self, step):
        p, slot, cut = self.p, step % self.slots, crossing(step, self.rows)
        if not cut:
            return
        self.incoming(lambda up: self.cross_copy(step, p.z, up))
        here = self.mine(step, p.z, 1 - p.x, p.c).at[self.tail(step)]

        def put(*refs):
            here[...] = total(*refs).astype(here.dtype)

        self.outcome(put, [here], *(self.cross_in.at[slot, way, p.z, pl.ds(0, cut)] for way in range(2)))
        self.last_copy(step).start()

    def own_stage(self, step):
        p, slot, last, cut = self.p, step % self.slots, self.p.depth - 1, crossing(step, self.rows)
        self.incoming(lambda up: self.chain_copy(step, p.z, up))
        mine, out = self.mine(step, p.z, p.x, p.c), self.outs[step]
        if cut:
            self.last_copy(step).wait_recv()
        for rows, extra in ((self.main(step), []), (self.tail(step), [self.last_in.at[slot, pl.ds(0, cut)]] if cut else None)):
            if extra is None:
                continue

            def put(*refs):
                out[rows] = total(*refs)

            self.outcome(put, [mine.at[rows]] + extra, *(self.chain_in.at[slot, way, p.z, rows] for way in range(2)))
        if step + self.slots < self.count:
            pl.when(p.z > 0)(lambda: self.signal(self.chain_free.at[0], p.device(p.z - 1, p.x, p.c)))
            pl.when(p.z < last)(lambda: self.signal(self.chain_free.at[1], p.device(p.z + 1, p.x, p.c)))

    def drain(self):
        for step in range(self.count - self.early, self.count):
            self.core_drain(step)
            self.side_drain(step)
        for step in range(self.count - self.slots, self.count):
            self.chain_drain(step)


def run_scatter(scatter, vector_scatter, ready, beside, done):
    side_lag, near_lag, far_lag, last_lag, own_lag = LAGS
    for tick in range(BLOCKS + own_lag):
        if tick < BLOCKS:
            ready(tick)
        if tick >= own_lag:
            scatter.own_stage(tick - own_lag)
            done(tick - own_lag)
        if 0 <= tick - last_lag < BLOCKS:
            scatter.last_stage(tick - last_lag)
        if tick < BLOCKS:
            scatter.core_stage(tick)
        if 0 <= tick - side_lag < BLOCKS:
            scatter.side_stage(tick - side_lag)
        if 0 <= tick - far_lag < BLOCKS:
            scatter.chain_stage(tick - far_lag, False)
        beside(tick)
        if 0 <= tick - near_lag < BLOCKS:
            scatter.chain_stage(tick - near_lag, True)
        if tick == BLOCKS - 1:
            vector_scatter.core_stage(0)
        if tick == BLOCKS:
            vector_scatter.side_stage(0)
        if tick == BLOCKS + 1:
            vector_scatter.chain_stage(0, True)
            vector_scatter.chain_stage(0, False)
    vector_scatter.own_stage(0)
    scatter.drain()
    vector_scatter.drain()


def scatter_scratch(depth, slots, early, rows, width, dtype):
    dma, plain = pltpu.SemaphoreType.DMA, pltpu.SemaphoreType.REGULAR
    cross = min(CROSS, rows)
    return [
        pltpu.VMEM((early, 2 * depth, rows, width), dtype),
        pltpu.VMEM((early, depth, rows, width), dtype),
        pltpu.VMEM((slots, 2, depth, rows, width), dtype),
        pltpu.VMEM((slots, 2, depth, cross, width), dtype), pltpu.VMEM((slots, cross, width), dtype),
        dma((early, 2 * depth)), dma((early, 2 * depth)), dma((early, depth)), dma((early, depth)),
        dma((slots, 2, depth)), dma((slots, 2, depth)), dma((slots, 2, depth)), dma((slots, 2, depth)),
        dma((slots,)), dma((slots,)), plain, plain, plain((2,)),
    ]


(NORM_GAIN, NORM_BIAS, OUTPUT_BIAS, SANDWICH_GAIN, SANDWICH_BIAS, SECOND_GAIN, SECOND_BIAS, REDUCE_BIAS,
 CLOSING_GAIN, CLOSING_BIAS, QUERY_BIAS, VALUE_BIAS, EXPAND_BIAS) = range(13)
NARROW = 10
VECTOR_ROWS = 16
FIGURES = 13
LANES = 128
TILE = 256
STAGED = 3
CHUNK = 64
CURVE = math.sqrt(2.0 / math.pi)
BEND = 0.044715


class Work(NamedTuple):
    vec: Any
    dvec: Any
    h: Any
    a: Any
    q: Any
    k: Any
    v: Any
    p: Any
    o: Any
    n_h: Any
    r_h: Any
    n_y: Any
    r_y: Any
    n_m: Any
    r_m: Any
    n_e: Any
    r_e: Any
    mid: Any
    c: Any
    g: Any
    slope: Any
    de: Any
    dy: Any
    do: Any
    din: Any
    sums: Any


def mxu(left, right, left_dim, right_dim):
    return lax.dot_general(left, right, (((left_dim,), (right_dim,)), ((), ())), preferred_element_type=F32)


def mean_of(value):
    return jnp.mean(value, axis=-1, keepdims=True)


def norm_of(value):
    centered = value - mean_of(value)
    rate = lax.rsqrt(mean_of(centered * centered) + EPSILON)
    return centered * rate, rate


def norm_pull(grad, normal, rate, gain):
    scaled = grad * gain
    return rate * (scaled - mean_of(scaled) - normal * mean_of(scaled * normal))


def column_sum(value):
    return jnp.sum(value, axis=0, keepdims=True)


class Layer:
    def __init__(self, work, store, lengths, swift=True):
        self.w, self.store, self.lengths, self.swift = work, store, lengths, swift
        self.tokens, self.width = work.h.shape
        self.sequences = lengths.shape[0]
        self.slots = self.tokens // self.sequences

    def row(self, index):
        return self.w.vec[index : index + 1, :]

    def add(self, index, value):
        self.w.dvec[index : index + 1, :] += value

    def chunks(self, body, first=0, last=None):
        last = self.tokens if last is None else last

        def step(i, carry):
            body(pl.ds(pl.multiple_of(i * CHUNK, CHUNK), CHUNK), i)
            return carry

        lax.fori_loop(first // CHUNK, last // CHUNK, step, 0)

    def tiles(self, body):
        def step(i, carry):
            body(pl.ds(pl.multiple_of(i * TILE, TILE), TILE))
            return carry

        lax.fori_loop(0, self.width // TILE, step, 0, unroll=self.swift)

    def valid(self, i):
        per = self.slots // CHUNK
        slot = (i % per) * CHUNK + lax.broadcasted_iota(jnp.int32, (CHUNK, 1), 0)
        return jnp.where(slot < self.lengths[i // per], 1.0, 0.0)


    def fore_start(self, source, first=0, last=None):
        w = self.w

        def body(rows, i):
            h = source[rows, :]
            if source is not w.h:
                w.h[rows, :] = h
            normal, rate = norm_of(h.astype(F32))
            w.n_h[rows, :] = normal
            w.r_h[rows, :] = rate
            w.a[rows, :] = (normal * self.row(NORM_GAIN) + self.row(NORM_BIAS)).astype(BF)

        self.chunks(body, first, last)

    def part(self, index):
        return pl.ds(index * self.slots, self.slots)

    def fore_joint(self, block, rows):
        w = self.w
        bias = (QUERY_BIAS, None, VALUE_BIAS)[block]
        target = (w.q, w.k, w.v)[block]

        def body(tile):
            mixed = mxu(w.a[rows, :], self.store[block, :, tile], 1, 0)
            if bias is not None:
                mixed = mixed + w.vec[bias : bias + 1, tile]
            if block == 0:
                mixed = mixed * QUERY_SCALE
            target[rows, tile] = mixed.astype(BF)

        self.tiles(body)

    def pairs(self, sequence, body):
        count = self.width // LANES
        rows, length = self.part(sequence), self.lengths[sequence]

        def step(i, carry):
            body(rows, pl.ds(pl.multiple_of(i * LANES, LANES), LANES), sequence * count + i, length)
            return carry

        lax.fori_loop(0, count, step, 0, unroll=8 if self.swift else 2)

    def split(self, value):
        low = lax.broadcasted_iota(jnp.int32, value.shape, 1) < HEAD_DIM
        zero = jnp.zeros_like(value)
        return jnp.concatenate([jnp.where(low, value, zero), jnp.where(low, zero, value)], axis=0)

    def merge(self, value):
        low = lax.broadcasted_iota(jnp.int32, (self.slots, LANES), 1) < HEAD_DIM
        return jnp.where(low, value[: self.slots], value[self.slots :])

    def fore_attention(self, sequence):
        w, slots = self.w, self.slots

        def body(rows, lanes, i, length):
            scores = mxu(w.k[rows, lanes], self.split(w.q[rows, lanes]), 1, 1)
            key = lax.broadcasted_iota(jnp.int32, (slots, 2 * slots), 0)
            query = lax.broadcasted_iota(jnp.int32, (slots, 2 * slots), 1) % slots
            scores = jnp.where((key <= query) & (key < length), scores, MASKED)
            weight = jnp.exp(RELAX * (scores - jnp.max(scores, axis=0, keepdims=True)))
            probs = (weight / column_sum(weight)).astype(BF)
            w.p[i] = probs
            w.o[rows, lanes] = self.merge(mxu(probs, w.v[rows, lanes], 0, 0)).astype(BF)

        self.pairs(sequence, body)

    def fore_output(self, rows):
        w = self.w

        def body(tile):
            w.n_y[rows, tile] = mxu(w.o[rows, :], self.store[3, :, tile], 1, 0) + w.vec[OUTPUT_BIAS : OUTPUT_BIAS + 1, tile]

        self.tiles(body)

    def fore_middle(self, first=0, last=None):
        w = self.w

        def middle(rows, i):
            y = w.n_y[rows, :]
            w.sums[0:1, :] += column_sum(y * y * self.valid(i))
            normal, rate = norm_of(y)
            w.n_y[rows, :] = normal
            w.r_y[rows, :] = rate
            mid = w.h[rows, :].astype(F32) + (normal * self.row(SANDWICH_GAIN) + self.row(SANDWICH_BIAS))
            w.mid[rows, :] = mid
            normal, rate = norm_of(mid)
            w.n_m[rows, :] = normal
            w.r_m[rows, :] = rate
            w.c[rows, :] = (normal * self.row(SECOND_GAIN) + self.row(SECOND_BIAS)).astype(BF)

        self.chunks(middle, first, last)

    def fore_expand(self, block, rows):
        w = self.w

        def body(tile):
            f = mxu(w.c[rows, :], self.store[4 + block, :, tile], 1, 0)
            f = f + w.vec[EXPAND_BIAS + block : EXPAND_BIAS + block + 1, tile]
            square = f * f
            bent = jnp.tanh(CURVE * f * (1.0 + BEND * square))
            half = 0.5 * (1.0 + bent)
            w.g[block, rows, tile] = (f * half).astype(BF)
            slope = half + 0.5 * f * (1.0 - bent * bent) * (CURVE * (1.0 + 3.0 * BEND * square))
            w.slope[block, rows, tile] = slope.astype(BF)

        self.tiles(body)

    def fore_reduce(self, rows):
        w = self.w

        def body(tile):
            e = mxu(w.g[0, rows, :], self.store[8, :, tile], 1, 0)
            for block in range(1, 4):
                e = e + mxu(w.g[block, rows, :], self.store[8 + block, :, tile], 1, 0)
            w.n_e[rows, tile] = e + w.vec[REDUCE_BIAS : REDUCE_BIAS + 1, tile]

        self.tiles(body)

    def fore_end(self, target, first=0, last=None):
        w = self.w

        def body(rows, i):
            e = w.n_e[rows, :]
            valid = self.valid(i)
            w.sums[1:2, :] += column_sum(e * e * valid)
            normal, rate = norm_of(e)
            w.n_e[rows, :] = normal
            w.r_e[rows, :] = rate
            out = w.mid[rows, :] + (normal * self.row(CLOSING_GAIN) + self.row(CLOSING_BIAS))
            w.sums[2:3, :] += column_sum(out * out * valid)
            target[rows, :] = out.astype(BF)

        self.chunks(body, first, last)


    def back_start(self, seed, masked, first=0, last=None):
        w = self.w

        def body(rows, i):
            dout = seed[rows, :].astype(F32)
            if masked:
                dout = dout * self.valid(i)
            w.din[rows, :] = dout
            normal = w.n_e[rows, :]
            self.add(CLOSING_GAIN, column_sum(dout * normal))
            self.add(CLOSING_BIAS, column_sum(dout))
            de = norm_pull(dout, normal, w.r_e[rows, :], self.row(CLOSING_GAIN)).astype(BF)
            w.de[rows, :] = de
            self.add(REDUCE_BIAS, column_sum(de.astype(F32)))

        self.chunks(body, first, last)

    def back_reduce(self, block, rows):
        w = self.w

        def body(tile):
            dg = mxu(w.de[rows, :], self.store[8 + block, tile, :], 1, 1)
            df = (dg * w.slope[block, rows, tile].astype(F32)).astype(BF)
            w.slope[block, rows, tile] = df
            w.dvec[EXPAND_BIAS + block : EXPAND_BIAS + block + 1, tile] += column_sum(df.astype(F32))

        self.tiles(body)

    def back_expand(self):
        w = self.w

        def body(tile):
            dc = mxu(w.slope[0], self.store[4, tile, :], 1, 1)
            for block in range(1, 4):
                dc = dc + mxu(w.slope[block], self.store[4 + block, tile, :], 1, 1)
            w.mid[:, tile] = dc

        self.tiles(body)

    def back_middle(self):
        w = self.w

        def middle(rows, i):
            dc = w.mid[rows, :]
            normal = w.n_m[rows, :]
            self.add(SECOND_GAIN, column_sum(dc * normal))
            self.add(SECOND_BIAS, column_sum(dc))
            dmid = w.din[rows, :] + norm_pull(dc, normal, w.r_m[rows, :], self.row(SECOND_GAIN))
            w.din[rows, :] = dmid
            normal = w.n_y[rows, :]
            self.add(SANDWICH_GAIN, column_sum(dmid * normal))
            self.add(SANDWICH_BIAS, column_sum(dmid))
            dy = norm_pull(dmid, normal, w.r_y[rows, :], self.row(SANDWICH_GAIN)).astype(BF)
            w.dy[rows, :] = dy
            self.add(OUTPUT_BIAS, column_sum(dy.astype(F32)))

        self.chunks(middle)

    def back_output(self):
        w = self.w

        def body(tile):
            w.do[:, tile] = mxu(w.dy[...], self.store[3, tile, :], 1, 1).astype(BF)

        self.tiles(body)

    def back_attention(self, sequence):
        w, slots = self.w, self.slots

        def body(rows, lanes, i, length):
            grad, key = self.split(w.do[rows, lanes]), w.k[rows, lanes]
            probs = w.p[i]
            value = probs.astype(F32)
            dprobs = mxu(w.v[rows, lanes], grad, 1, 1)
            ds = (RELAX * value * (dprobs - column_sum(dprobs * value))).astype(BF)
            dv = mxu(probs, grad, 1, 0)
            dk = mxu(ds, self.split(w.q[rows, lanes]), 1, 0)
            dq = self.merge(mxu(ds, key, 0, 0)) * QUERY_SCALE
            w.q[rows, lanes] = dq.astype(BF)
            w.k[rows, lanes] = dk.astype(BF)
            w.v[rows, lanes] = dv.astype(BF)

        self.pairs(sequence, body)

    def back_joint(self, rows):
        w = self.w

        def body(tile):
            da = mxu(w.q[rows, :], self.store[0, tile, :], 1, 1)
            da = da + mxu(w.k[rows, :], self.store[1, tile, :], 1, 1)
            w.mid[rows, tile] = da + mxu(w.v[rows, :], self.store[2, tile, :], 1, 1)

        self.tiles(body)

    def back_end(self, target, first=0, last=None):
        w = self.w

        def body(rows, i):
            da = w.mid[rows, :]
            normal = w.n_h[rows, :]
            self.add(NORM_GAIN, column_sum(da * normal))
            self.add(NORM_BIAS, column_sum(da))
            self.add(QUERY_BIAS, column_sum(w.q[rows, :].astype(F32)))
            self.add(VALUE_BIAS, column_sum(w.v[rows, :].astype(F32)))
            din = w.din[rows, :] + norm_pull(da, normal, w.r_h[rows, :], self.row(NORM_GAIN))
            w.din[rows, :] = din
            target[rows, :] = din.astype(BF)

        self.chunks(body, first, last)


    def weight_grad(self, block):
        w = self.w
        if block < 3:
            left, right = w.a, (w.q, w.k, w.v)[block]
        elif block == 3:
            left, right = w.o, w.dy
        elif block < 8:
            left, right = w.c, w.slope.at[block - 4]
        else:
            left, right = w.g.at[block - 8], w.de

        def body(tile):
            self.store[block, tile, :] = mxu(left[:, tile], right[...], 0, 0).astype(BF)

        self.tiles(body)


def unfold_vectors(tiles, vec, count):
    for pair in range(count // 2):
        vec[:NARROW, pair * LANES : (pair + 1) * LANES] = tiles[2 * pair, :NARROW, :] + tiles[2 * pair + 1, :NARROW, :]
    half, quarter = count // 2, count // 4
    for shard in range(count):
        row, lane = QUERY_BIAS + shard // half, (shard % half) * LANES
        vec[row : row + 1, lane : lane + LANES] = tiles[shard, NARROW : NARROW + 1, :]
        for part in range(2):
            row, lane = EXPAND_BIAS + shard // quarter, ((shard % quarter) * 2 + part) * LANES
            source = NARROW + 1 + part
            vec[row : row + 1, lane : lane + LANES] = tiles[shard, source : source + 1, :]


def fold_vectors(tiles, dvec, figures, count):
    half, quarter = count // 2, count // 4
    for shard in range(count):
        pair = shard // 2
        tiles[shard, :NARROW, :] = dvec[:NARROW, pair * LANES : (pair + 1) * LANES]
        row, lane = QUERY_BIAS + shard // half, (shard % half) * LANES
        tiles[shard, NARROW : NARROW + 1, :] = dvec[row : row + 1, lane : lane + LANES]
        for part in range(2):
            row, lane = EXPAND_BIAS + shard // quarter, ((shard % quarter) * 2 + part) * LANES
            target = NARROW + 1 + part
            tiles[shard, target : target + 1, :] = dvec[row : row + 1, lane : lane + LANES]
        tiles[shard, FIGURES : FIGURES + 1, :] = figures
        tiles[shard, FIGURES + 1 :, :] = jnp.zeros((VECTOR_ROWS - FIGURES - 1, LANES), F32)


def figures_of(sums, lengths):
    lane = lax.broadcasted_iota(jnp.int32, (1, LANES), 1)
    row = jnp.zeros((1, LANES), F32)
    for i in range(3):
        row = jnp.where(lane == i, jnp.sum(sums[i : i + 1, :], axis=1, keepdims=True), row)
    seen = lengths[0]
    for i in range(1, lengths.shape[0]):
        seen = seen + lengths[i]
    return jnp.where(lane == 3, seen.astype(F32), row)


def relay_kernel(depth, lengths, tokens, cotangent, joint, output, expand, reduce, *refs):
    relay_body(depth, lengths, tokens, cotangent, joint, output, expand, reduce, refs[: NARROW + 2], *refs[NARROW + 2 :])


def own_vectors(place, refs, tile):
    tile[...] = jnp.zeros_like(tile)
    for i in range(NARROW):
        value = refs[i][...].astype(F32)
        zero = jnp.zeros_like(value)
        tile[i : i + 1, :] = jnp.where(
            place.c == 0, jnp.concatenate([value, zero], axis=1), jnp.concatenate([zero, value], axis=1))
    tile[NARROW : NARROW + 1, :] = refs[NARROW][...].astype(F32)
    for part in range(2):
        tile[NARROW + 1 + part : NARROW + 2 + part, :] = refs[NARROW + 1][:, part * LANES : (part + 1) * LANES].astype(F32)


def relay_body(depth, lengths, tokens, cotangent, joint, output, expand, reduce, vector_refs,
                 section_out, section_grad, joint_out, output_out, expand_out, reduce_out, vector_out,
                 store, vectors, tiles, vec, dvec, sums, h, a, q, k, v, p, o, n_h, r_h, n_y, r_y, n_m, r_m, n_e, r_e,
                 mid, c, g, slope, de, dy, do, din, result, staged, incoming, pass_sems, out_sems, *rest):
    place = Place(depth)
    width = store.shape[2]
    count = 4 * depth
    gather_parts, rest = rest[:4], rest[4:]
    scatter_parts, vector_parts = rest[:18], rest[18:]
    work = Work(vec, dvec, h, a, q, k, v, p, o, n_h, r_h, n_y, r_y, n_m, r_m, n_e, r_e, mid, c, g, slope,
                de, dy, do, din, sums)
    layer, hidden = Layer(work, store, lengths), Layer(work, store, lengths, swift=False)
    slots, parts = layer.slots, range(layer.sequences)
    whole = pl.ds(0, layer.tokens)
    first, second = place.s == 0, place.s == 1

    def passing(source, part, way):
        rows = pl.ds(part * slots, slots)
        return pltpu.make_async_remote_copy(
            source.at[rows], incoming.at[rows], pass_sems.at[way, 0, part], pass_sems.at[way, 1, part],
            device_id=place.across(), device_id_type=MESH)

    def forward(part):
        return passing(result, part, 0)

    def backward(part):
        return passing(do, part, 1)

    out_copy = pltpu.make_async_copy(result, section_out, out_sems.at[BLOCKS])
    grad_copy = pltpu.make_async_copy(din, section_grad, out_sems.at[BLOCKS + 1])

    token_copy = pltpu.make_async_copy(tokens, h, out_sems.at[BLOCKS + 2])
    seed_copy = pltpu.make_async_copy(cotangent, dy, out_sems.at[BLOCKS + 3])
    pl.when(first)(lambda: token_copy.start())
    pl.when(second)(lambda: seed_copy.start())
    own_vectors(place, vector_refs, vectors)
    place.greet()
    dvec[...] = jnp.zeros_like(dvec)
    sums[...] = jnp.zeros_like(sums)

    def fore_last(part):
        layer.fore_reduce(layer.part(part))
        layer.fore_end(result, part * slots, (part + 1) * slots)

    def back_rest(part, layer):
        layer.back_joint(layer.part(part))
        layer.back_end(do, part * slots, (part + 1) * slots)

    def ready(item):
        if item == VECTOR_ITEM:
            unfold_vectors(tiles, vec, count)

        def enter():
            token_copy.wait()
            hidden.fore_start(h)

        def leave(part):
            fore_last(part)
            forward(part).start()

        pieces = []
        if item == VECTOR_ITEM:
            pieces = [enter]
        elif item < 3:
            pieces = [functools.partial(hidden.fore_joint, item, whole)]
            if item == 2:
                pieces += [functools.partial(hidden.fore_attention, part) for part in parts]
        elif item == 3:
            pieces = [functools.partial(hidden.fore_output, whole), hidden.fore_middle]
        elif item < 8:
            pieces = [functools.partial(hidden.fore_expand, item - 4, whole)]
        elif item == BLOCKS - 1:
            pieces = [functools.partial(leave, part) for part in parts]
        return [lambda piece=piece: pl.when(first)(piece) for piece in pieces]

    gather = Gather(place, (joint, output, expand, reduce, vectors), store, tiles, gather_parts)
    run_gather(gather, ready)
    gather.drain()

    @pl.when(second)
    def _():
        for part in parts:
            forward(part).wait_recv()
            rows, span = layer.part(part), (part * slots, (part + 1) * slots)
            layer.fore_start(incoming, *span)
            for block in range(3):
                layer.fore_joint(block, rows)
            layer.fore_attention(part)
            layer.fore_output(rows)
            layer.fore_middle(*span)
            for block in range(4):
                layer.fore_expand(block, rows)
            fore_last(part)
        seed_copy.wait()
        layer.back_start(dy, True)
        for block in range(4):
            layer.back_reduce(block, whole)
        layer.back_expand()
        layer.back_middle()
        layer.back_output()
        for part in parts:
            layer.back_attention(part)
            back_rest(part, layer)
            backward(part).start()

    out_copy.start()

    @pl.when(first)
    def _():
        for part in parts:
            backward(part).wait_recv()
            layer.back_start(incoming, False, part * slots, (part + 1) * slots)
            if part < parts[-1]:
                for block in range(4):
                    layer.back_reduce(block, layer.part(part))

    def fill(step):
        if step >= 4:
            layer.weight_grad(SCATTER_ORDER[step])
        if step == 8:
            grad_copy.start()
        if step == BLOCKS - 1:
            fold_vectors(tiles, dvec, figures_of(sums, lengths), count)

    def first_part(z):
        pl.when(first)(lambda: layer.back_reduce(z, layer.part(parts[-1])))
        layer.weight_grad(8 + z)

    def beside(step):
        pieces = {1: [hidden.back_expand], 2: [hidden.back_middle], 3: [hidden.back_output]}
        for part in parts:
            attention, rest = functools.partial(hidden.back_attention, part), functools.partial(back_rest, part, hidden)
            pieces.setdefault(4 + part % 2, []).append(attention)
            pieces.setdefault(6 + part % 2, []).append(rest)

        @pl.when(first)
        def _():
            for piece in pieces.get(step, []):
                piece()

    def part_of(step, shard):
        block, row = spot(SCATTER_ORDER[step], shard)
        return store.at[block, pl.ds(row, PART)]

    targets = [shard_view((joint_out, output_out, expand_out, reduce_out, None), item, width) for item in SCATTER_ORDER]
    outs = [staged.at[step % STAGED] for step in range(BLOCKS)]
    copies = [pltpu.make_async_copy(outs[step], targets[step], out_sems.at[step]) for step in range(BLOCKS)]
    scatter = Scatter(place, part_of, BLOCKS, SLOTS, EARLY_SLOTS, scatter_parts[:5], outs, scatter_parts[5:], first_part)
    vector_scatter = Scatter(place, lambda step, shard: tiles.at[shard], 1, 1, 1, vector_parts[:5], [vector_out], vector_parts[5:])

    def done(step):
        copies[step].start()
        if step + 1 >= STAGED and step + 1 < BLOCKS:
            copies[step + 1 - STAGED].wait()

    run_scatter(scatter, vector_scatter, fill, beside, done)

    @pl.when(first)
    def _():
        for part in parts:
            forward(part).wait_send()

    @pl.when(second)
    def _():
        for part in parts:
            backward(part).wait_send()

    for copy in copies[BLOCKS - STAGED :] + [out_copy, grad_copy]:
        copy.wait()


def finish_kernel(core, *refs):
    large, small = 6, NARROW + 3
    sources, targets = refs[: large + 1], refs[large + 1 : 2 * large + 1 + small]
    held, sems = refs[2 * large + 1 + small : -1], refs[-1]
    tile, made = held[large], held[large + 1 :]
    loads = [pltpu.make_async_copy(source, buffer, sems.at[0, i]) for i, (source, buffer) in enumerate(zip(sources, held))]
    stores = [pltpu.make_async_copy(buffer, target, sems.at[1, i]) for i, (buffer, target) in enumerate(zip(held[:large] + made, targets))]
    for load in loads[::-1]:
        load.start()
    loads[large].wait()
    magnitudes, joint_bias, expand_bias, narrow = made[0], made[1], made[2], made[3:]
    halves = jnp.where(core[0] == 0, tile[:NARROW, :HEAD_DIM], tile[:NARROW, HEAD_DIM:])
    for i, ref in enumerate(narrow):
        ref[...] = halves[i : i + 1]
    figures = tile[FIGURES : FIGURES + 1, :]
    magnitudes[...] = jnp.sqrt(figures[:, :3] / (figures[:, 3:4] * sources[0].shape[1]))
    joint_bias[...] = tile[NARROW : NARROW + 1, :]
    for part in range(2):
        expand_bias[:, part * LANES : (part + 1) * LANES] = tile[NARROW + 1 + part : NARROW + 2 + part, :]
    for store in stores[large:]:
        store.start()
    for load, store in list(zip(loads, stores))[large - 1 :: -1]:
        load.wait()
        store.start()
    for store in stores:
        store.wait()


def relay_local(depth, tokens, lengths, *parameters):
    cotangent, own = parameters[-1], Params(*parameters[:-1])
    micro, rows, width = tokens.shape
    sequences = lengths.shape[1] * micro
    count = micro * rows
    core = lax.axis_index("batch") % 2

    vectors = [
        own.norm_gain, own.norm_bias, own.output_bias, own.sandwich_gain, own.sandwich_bias, own.second_gain,
        own.second_bias, own.reduce_bias, own.closing_gain, own.closing_bias, own.joint_bias, own.expand_bias]

    low, high, rate = (pltpu.VMEM((count, width), BF), pltpu.VMEM((count, width), F32), pltpu.VMEM((count, 1), F32))
    wide = pltpu.VMEM((4, count, width), BF)
    shards = 4 * depth
    dma = pltpu.SemaphoreType.DMA
    vmem, anywhere = pl.BlockSpec(memory_space=pltpu.VMEM), pl.BlockSpec(memory_space=pl.ANY)
    shapes = [
        jax.ShapeDtypeStruct((count, width), BF), jax.ShapeDtypeStruct((count, width), F32),
        jax.ShapeDtypeStruct((PART, 3 * width), F32), jax.ShapeDtypeStruct((PART, width), F32),
        jax.ShapeDtypeStruct((PART, 4 * width), F32), jax.ShapeDtypeStruct((4 * PART, width), F32)]
    tile = jax.ShapeDtypeStruct((VECTOR_ROWS, LANES), F32)
    slots = rows // lengths.shape[1]
    results = pl.pallas_call(
        functools.partial(relay_kernel, depth),
        out_shape=shapes + [tile],
        in_specs=[pl.BlockSpec(memory_space=pltpu.SMEM)] + [anywhere] * 6 + [vmem] * len(vectors),
        out_specs=[anywhere] * 6 + [vmem],
        scratch_shapes=[
            pltpu.VMEM((BLOCKS, width, width), BF), pltpu.VMEM((VECTOR_ROWS, LANES), F32), pltpu.VMEM((shards, VECTOR_ROWS, LANES), F32),
            pltpu.VMEM((VECTOR_ROWS, width), F32), pltpu.VMEM((VECTOR_ROWS, width), F32), pltpu.VMEM((8, width), F32),
            low, low, low, low, low, pltpu.VMEM((sequences * width // LANES, slots, 2 * slots), BF), low,
            high, rate, high, rate, high, rate, high, rate,
            high, low, wide, wide, low, low, low, high, low, pltpu.VMEM((STAGED, PART, width), F32), low,
            dma((2, 2, sequences)), dma((BLOCKS + 4,)),
        ] + gather_sems(depth) + scatter_scratch(depth, SLOTS, EARLY_SLOTS, PART, width, BF) + scatter_scratch(depth, 1, 1, VECTOR_ROWS, LANES, F32),
        compiler_params=pltpu.CompilerParams(collective_id=1, has_side_effects=True, vmem_limit_bytes=VMEM_LIMIT),
        cost_estimate=pl.CostEstimate(flops=6 * count * BLOCKS * width * width, bytes_accessed=2 * BLOCKS * width * width, transcendentals=0),
        name="relay",
    )(lengths.reshape(-1), tokens.reshape(count, width), cotangent.reshape(count, width),
      own.joint_weight[0], own.output_weight[0], own.expand_weight[0], own.reduce_weight[0], *vectors)

    vector = jax.ShapeDtypeStruct((1, HEAD_DIM), F32)
    small = [jax.ShapeDtypeStruct((1, 3), F32), jax.ShapeDtypeStruct((1, LANES), F32),
             jax.ShapeDtypeStruct((1, 2 * LANES), F32)] + [vector] * NARROW
    final = pl.pallas_call(
        finish_kernel,
        out_shape=shapes + small,
        in_specs=[pl.BlockSpec(memory_space=pltpu.SMEM)] + [anywhere] * 7,
        out_specs=[anywhere] * (6 + len(small)),
        scratch_shapes=[pltpu.VMEM(s.shape, s.dtype) for s in shapes + [tile] + small] + [dma((2, 6 + len(small)))],
        compiler_params=pltpu.CompilerParams(vmem_limit_bytes=VMEM_LIMIT),
        name="finish",
    )(core.reshape(1), *results)
    section_out, section_grad, joint, output, expand, reduce, magnitudes, joint_bias, expand_bias = final[:9]
    narrow = final[9:]
    grads = Params(
        norm_gain=narrow[NORM_GAIN], norm_bias=narrow[NORM_BIAS], joint_weight=joint[None],
        joint_bias=joint_bias, output_weight=output[None], output_bias=narrow[OUTPUT_BIAS],
        sandwich_gain=narrow[SANDWICH_GAIN], sandwich_bias=narrow[SANDWICH_BIAS], second_gain=narrow[SECOND_GAIN],
        second_bias=narrow[SECOND_BIAS], expand_weight=expand[None],
        expand_bias=expand_bias, reduce_weight=reduce[None],
        reduce_bias=narrow[REDUCE_BIAS], closing_gain=narrow[CLOSING_GAIN], closing_bias=narrow[CLOSING_BIAS])
    shape = (1, micro, rows, width)
    return (section_out.reshape(shape), section_grad.reshape(shape), magnitudes) + tuple(grads)


def solution(mesh):
    vector, matrix = P("section", "batch"), P("section", "batch", None)
    kinds = tuple(matrix if i in MATRICES else vector for i in range(16))
    rows = P(None, "batch", None)
    stacked = P("section", None, "batch", None)
    devices = mesh.shape["batch"]
    body = functools.partial(relay_local, devices // 4) if devices == 16 else plain_local
    return jax.shard_map(
        body,
        mesh=mesh,
        in_specs=(rows, P(None, "batch")) + kinds + (rows,),
        out_specs=(stacked, stacked, P("section", None)) + kinds,
        check_vma=False,
    )
```
